32 devices in a mesh: fsdp: 32 (over z, y, x, core).
Axes of the slice: x: 2, y: 2, z: 4, core: 2. Of those that a mesh axis runs over, the one named last changes fastest.
Arguments:
- loop_state: bfloat16 [65536, 256], P('fsdp'), may hold values from -6 to 6
- embedding: bfloat16 [65536, 256], P('fsdp'), may hold values from -6 to 6
- output_grad: bfloat16 [65536, 256], P('fsdp'), may hold values from -6 to 6
- entry_weight: bfloat16 [256, 768], P('fsdp'), may hold values from -0.375 to 0.375
- exit_weight: bfloat16 [256, 256], P('fsdp'), may hold values from -1.5 to 1.5
- lead_gain: bfloat16 [256], P('fsdp'), may hold values from 0.25 to 1.75
- lead_shift: bfloat16 [256], P('fsdp'), may hold values from -3 to 3
- expand_weight: bfloat16 [256, 1024], P('fsdp'), may hold values from -0.375 to 0.375
- reduce_weight: bfloat16 [1024, 256], P('fsdp'), may hold values from -0.25 to 0.25
- middle_gain: bfloat16 [256], P('fsdp'), may hold values from 0.25 to 1.75
- middle_shift: bfloat16 [256], P('fsdp'), may hold values from -3 to 3
- expand_bias: bfloat16 [1024], P('fsdp'), may hold values from -3 to 3
- reduce_bias: bfloat16 [256], P('fsdp'), may hold values from -3 to 3
Outputs:
- final_state: bfloat16 [65536, 256], P('fsdp')
- state_grad: float32 [65536, 256], P('fsdp')
- embed_grad: float32 [65536, 256], P('fsdp')
- entry_grad: float32 [256, 768], P('fsdp')
- exit_grad: float32 [256, 256], P('fsdp')
- lead_gain_grad: float32 [256], P('fsdp')
- lead_shift_grad: float32 [256], P('fsdp')
- expand_grad: float32 [256, 1024], P('fsdp')
- reduce_grad: float32 [1024, 256], P('fsdp')
- middle_gain_grad: float32 [256], P('fsdp')
- middle_shift_grad: float32 [256], P('fsdp')
- expand_bias_grad: float32 [1024], P('fsdp')
- reduce_bias_grad: float32 [256], P('fsdp')
The draws below stay inside these ranges and needn't reach their ends.
All inputs are finite; a program needn't handle non-finite values.
Results may differ from the reference program's by a relative error of at most 0.013.
Values may be sent and summed in bfloat16 or wider, within the bound.
A program may use at most 192 MiB of HBM per device.

```python
import jax
import jax.numpy as jnp
from jax import lax

D = 256
HEADS = 4
HD = 64
FF = 1024
LEN = 1024
LOOPS = 2
SEQ_DEV = 2
SEQS = 64
TOKENS = 65536


def level_of(key, dims, shards, smallest, top_value):
    level, own = 1.0, jax.random.fold_in(key, 6)
    for axis_at, parts in shards:
        steps = jnp.exp(jax.random.uniform(jax.random.fold_in(own, axis_at), (parts,), jnp.float32, smallest / len(shards), top_value / len(shards)))
        level = level * jnp.repeat(steps, dims[axis_at] // parts).reshape([-1 if axis == axis_at else 1 for axis in range(len(dims))])
    return level


def scatter_about(rng, shape, deviation, most, cuts=(), dtype=jnp.bfloat16):
    drawn = deviation * jax.random.normal(rng, shape, jnp.float32)
    if cuts:
        drawn = drawn * level_of(rng, shape, cuts, -0.22, 0.18)
    return jnp.clip(drawn, -most, most).astype(dtype)


def setup_inputs(seed: int = 0) -> dict:
    key_of = jax.random.split(jax.random.key(seed), 14)
    loop_state = scatter_about(key_of[0], (TOKENS, D), 1.0, 6.0, ((0, 32),))
    embedding = scatter_about(key_of[1], (TOKENS, D), 1.0, 6.0, ((0, 32),))
    output_grad = scatter_about(key_of[2], (TOKENS, D), 1.0, 6.0, ((0, 32),))
    entry_weight = scatter_about(key_of[3], (D, 3 * D), D ** -0.5, 0.375, ((0, 32),))
    exit_weight = scatter_about(key_of[4], (D, D), (D // 16) ** -0.5, 1.5, ((0, 32),))
    lead_gain = jnp.clip(1.0 + 0.15 * jax.random.normal(key_of[5], (D,), jnp.float32), 0.25, 1.75).astype(jnp.bfloat16)
    lead_shift = scatter_about(key_of[6], (D,), 0.3, 3.0, ((0, 32),))
    expand_weight = scatter_about(key_of[7], (D, FF), D ** -0.5, 0.375, ((0, 32),))
    reduce_weight = scatter_about(key_of[8], (FF, D), (FF // 2) ** -0.5, 0.25, ((0, 32),))
    middle_gain = jnp.clip(1.0 + 0.15 * jax.random.normal(key_of[9], (D,), jnp.float32), 0.25, 1.75).astype(jnp.bfloat16)
    middle_shift = scatter_about(key_of[10], (D,), 0.3, 3.0, ((0, 32),))
    expand_bias = scatter_about(key_of[11], (FF,), 0.3, 3.0, ((0, 32),))
    reduce_bias = scatter_about(key_of[12], (D,), 0.3, 3.0, ((0, 32),))
    return {"loop_state": loop_state, "embedding": embedding, "output_grad": output_grad, "entry_weight": entry_weight, "exit_weight": exit_weight, "lead_gain": lead_gain, "lead_shift": lead_shift, "expand_weight": expand_weight, "reduce_weight": reduce_weight, "middle_gain": middle_gain, "middle_shift": middle_shift, "expand_bias": expand_bias, "reduce_bias": reduce_bias}


@jax.custom_vjp
def low(v):
    return lax.optimization_barrier(v.astype(jnp.bfloat16)).astype(jnp.float32)

@jax.custom_vjp
def low_back(v):
    return v

def low_keep(v):
    return (low(v), None)

def low_pass(kept, grad):
    return (grad,)

def back_keep(v):
    return (v, None)

def back_low(kept, grad):
    return (low(grad),)
low.defvjp(low_keep, low_pass)
low_back.defvjp(back_keep, back_low)
EPS = 1e-05
HIGH = lax.Precision.HIGHEST

def norm_layer(values, gain, shift):
    center = values - lax.optimization_barrier(jnp.mean(values, axis=-1, keepdims=True))
    spread = lax.optimization_barrier(jnp.mean(center * center, axis=-1, keepdims=True))
    return center * lax.rsqrt(spread + EPS) * gain + shift

def attention(qkv):
    seqs = qkv.shape[0]
    length = qkv.shape[1]
    block = min(512, length)
    query = qkv[:, :, :D].reshape(seqs, length, HEADS, HD)
    keys = qkv[:, :, D:2 * D].reshape(seqs, length, HEADS, HD)
    values = qkv[:, :, 2 * D:].reshape(seqs, length, HEADS, HD)
    key_place = jnp.arange(length).astype(jnp.int32)

    def one_block(index):
        start = (index * block).astype(jnp.int32)
        q_block = lax.dynamic_slice_in_dim(query, start, block, 1)
        scores = jnp.einsum('sqhd,skhd->shqk', q_block, keys, precision=HIGH) * 0.125
        scores = low_back(scores)
        query_place = start + jnp.arange(block).astype(jnp.int32)
        allowed = key_place[None, :] <= query_place[:, None]
        scores = jnp.where(allowed, scores, -1e+30)
        top = lax.optimization_barrier(jnp.max(scores, axis=-1, keepdims=True))
        weights = jnp.exp(scores - top)
        probs = low(weights / lax.optimization_barrier(jnp.sum(weights, axis=-1, keepdims=True)))
        return jnp.einsum('shqk,skhd->sqhd', probs, values, precision=HIGH)
    blocks = lax.map(jax.checkpoint(one_block), jnp.arange(length // block).astype(jnp.int32))
    return jnp.transpose(blocks, (1, 0, 2, 3, 4)).reshape(seqs, length, D)

def loop_block(state, embed, params):
    entry_w, exit_w, lead_g, lead_s, expand_w, reduce_w, mid_g, mid_s, expand_b, reduce_b = params
    seqs, length, width = state.shape
    mixed = state + embed
    normed = low(norm_layer(mixed, lead_g, lead_s)).reshape(-1, width)
    qkv = jnp.dot(normed, entry_w, precision=HIGH)
    qkv = low(low_back(qkv)).reshape(seqs, length, 3 * width)
    attended = low(low_back(attention(qkv))).reshape(-1, width)
    branch = low_back(jnp.dot(attended, exit_w, precision=HIGH)).reshape(seqs, length, width)
    middle = mixed + branch
    normed2 = low(norm_layer(middle, mid_g, mid_s)).reshape(-1, width)
    hidden = low_back(jnp.dot(normed2, expand_w, precision=HIGH) + expand_b)
    active = low(jax.nn.gelu(hidden, approximate=False))
    result = low_back(jnp.dot(active, reduce_w, precision=HIGH) + reduce_b)
    return middle + result.reshape(seqs, length, width)

def reference(loop_state, embedding, output_grad, entry_weight, exit_weight, lead_gain, lead_shift, expand_weight, reduce_weight, middle_gain, middle_shift, expand_bias, reduce_bias):
    params = tuple((p.astype(jnp.float32) for p in (entry_weight, exit_weight, lead_gain, lead_shift, expand_weight, reduce_weight, middle_gain, middle_shift, expand_bias, reduce_bias)))
    group = SEQ_DEV
    count = SEQS // group

    def shaped(values):
        return values.astype(jnp.float32).reshape(count, group, LEN, D)

    def run(weights, state, embed):
        for turn in range(LOOPS):
            state = loop_block(state, embed, weights)
        return state

    def step(totals, item):
        state, embed, cotangent = item
        final, pull = jax.vjp(run, params, state, embed)
        d_params, d_state, d_embed = pull(cotangent)
        totals = tuple((a + b for a, b in zip(totals, d_params)))
        return (totals, (final.astype(jnp.bfloat16), d_state, d_embed))
    zeros = tuple((jnp.zeros(p.shape, jnp.float32) for p in params))
    totals, outputs = lax.scan(step, zeros, (shaped(loop_state), shaped(embedding), shaped(output_grad)))
    finals, d_states, d_embeds = outputs
    return (finals.reshape(TOKENS, D), d_states.reshape(TOKENS, D), d_embeds.reshape(TOKENS, D), totals[0], totals[1], totals[2], totals[3], totals[4], totals[5], totals[6], totals[7], totals[8], totals[9])
```

```python
import functools
import math
import jax
import jax.numpy as jnp
from jax import lax
from jax.experimental import pallas as pl
from jax.experimental.pallas import tpu as pltpu
from jax.sharding import PartitionSpec as P

F32, BF16 = jnp.float32, jnp.bfloat16
LEN = 1024
LOOPS = 2
EPS = 1e-05
D = 256
FF = 1024
HD = 64
LOG2E = 1.4426950408889634
LN2 = 0.6931471805599453
BLK = 256
NEG = -1e30


def dot_nn(a, b):
    return lax.dot_general(a, b, (((1,), (0,)), ((), ())), preferred_element_type=F32)


def dot_nt(a, b):
    return lax.dot_general(a, b, (((1,), (1,)), ((), ())), preferred_element_type=F32)


def dot_tn(a, b):
    return lax.dot_general(a, b, (((0,), (0,)), ((), ())), preferred_element_type=F32)


def norm_parts(x):
    mean = jnp.mean(x, axis=-1, keepdims=True)
    center = x - mean
    var = jnp.mean(center * center, axis=-1, keepdims=True)
    rstd = lax.rsqrt(var + EPS)
    return center * rstd, rstd


def norm_pull(xhat, rstd, gain, dy):
    dn = dy * gain
    m1 = jnp.mean(dn, axis=-1, keepdims=True)
    m2 = jnp.mean(dn * xhat, axis=-1, keepdims=True)
    return rstd * (dn - m1 - xhat * m2)


def gelu_parts(x):
    z = jnp.abs(x)
    t = 1.0 / (1.0 + (0.3275911 / math.sqrt(2.0)) * z)
    e = jnp.exp2((-0.5 * LOG2E) * (x * x))
    poly = t * (0.5 * 0.254829592 + t * (0.5 * -0.284496736 + t * (0.5 * 1.421413741 + t * (0.5 * -1.453152027 + t * (0.5 * 1.061405429)))))
    tail = poly * e
    cdf = jnp.where(x >= 0.0, 1.0 - tail, tail)
    return cdf, e


INV_SQRT_2PI = 1.0 / math.sqrt(2.0 * math.pi)


def lane_iota(rows):
    return lax.broadcasted_iota(jnp.int32, (rows, 128), 1)


def three_parts(x):
    hi = x.astype(BF16).astype(F32)
    r = x - hi
    mid = r.astype(BF16).astype(F32)
    return hi, mid, r - mid


def spread_parts(x, lane, spare):
    hi, mid, lo = three_parts(x)
    return jnp.where(lane == spare, hi, jnp.where(lane == spare + 1, mid, jnp.where(lane == spare + 2, lo, 0.0)))


def attn_forward(qkv, p, att, lx, vx, seqs):
    nblk = LEN // BLK

    def body(it, carry):
        s = it // 2
        pair = it % 2
        r0 = pl.multiple_of(s * LEN, LEN)
        cq = pl.multiple_of(pair * 128, 128)
        ck = pl.multiple_of(D + pair * 128, 128)
        cv = pl.multiple_of(2 * D + pair * 128, 128)
        lane = lane_iota(LEN)
        v = qkv[p, pl.ds(r0, LEN), pl.ds(cv, 128)]
        one = jnp.ones((LEN, 128), BF16)
        vx[0] = jnp.where(lane < HD, v, one)
        vx[1] = jnp.where(lane < HD, one, v)
        laneb = lane_iota(BLK)
        keep = lax.broadcasted_iota(jnp.int32, (BLK, BLK), 1) <= lax.broadcasted_iota(jnp.int32, (BLK, BLK), 0)
        for j in range(nblk):
            rows = pl.ds(pl.multiple_of(r0 + j * BLK, BLK), BLK)
            q = qkv[p, rows, pl.ds(cq, 128)]
            zero = jnp.zeros_like(q)
            outs, pieces = [], []
            for h in range(2):
                mine = (laneb < HD) if h == 0 else (laneb >= HD)
                qm = jnp.where(mine, q, zero)
                m_rows = (j + 1) * BLK
                k = qkv[p, pl.ds(r0, m_rows), pl.ds(ck, 128)]
                sc = dot_nt(qm, k)
                diag = jnp.where(keep, sc[:, j * BLK:], NEG)
                sc = jnp.concatenate([sc[:, : j * BLK], diag], axis=1) if j else diag
                top = jnp.max(sc, axis=-1, keepdims=True)
                pr = jnp.exp2(sc - top).astype(BF16)
                ox = dot_nn(pr, vx[h, :m_rows])
                den = pltpu.roll(ox, HD, 1)
                outs.append(ox / den)
                lse = top + jnp.log(ox) * LOG2E
                lse = jnp.where(mine, 0.0, lse)
                pieces.append(spread_parts(-lse, laneb, HD if h == 0 else 0))
            att[p, rows, pl.ds(cq, 128)] = jnp.where(laneb < HD, outs[0], outs[1]).astype(BF16)
            lx[p, rows, pl.ds(cq, 128)] = jnp.where(laneb < HD, pieces[1], pieces[0]).astype(BF16)
        return carry

    lax.fori_loop(0, seqs * 2, body, 0)


def attn_backward(qkv, p, att, lx, dmid_att, vx, kx, qx, dox, dk, dv, dq, seqs):
    nblk = LEN // BLK

    def body(it, carry):
        s = it // 2
        pair = it % 2
        r0 = pl.multiple_of(s * LEN, LEN)
        cq = pl.multiple_of(pair * 128, 128)
        ck = pl.multiple_of(D + pair * 128, 128)
        cv = pl.multiple_of(2 * D + pair * 128, 128)
        lane = lane_iota(LEN)
        seq = pl.ds(r0, LEN)
        low = lane < HD
        one = jnp.ones((LEN, 128), BF16)
        v = qkv[p, seq, pl.ds(cv, 128)]
        vx[0] = jnp.where(low, v, one)
        vx[1] = jnp.where(low, one, v)
        k = qkv[p, seq, pl.ds(ck, 128)]
        kx[0] = jnp.where(low, k, one)
        kx[1] = jnp.where(low, one, k)
        q = qkv[p, seq, pl.ds(cq, 128)]
        ls = lx[p, seq, pl.ds(cq, 128)]
        qx[0] = jnp.where(low, q, ls)
        qx[1] = jnp.where(low, ls, q)
        do = dmid_att[seq, pl.ds(cq, 128)]
        dof = do.astype(F32)
        prod = dof * att[p, seq, pl.ds(cq, 128)].astype(F32)
        in0 = jnp.sum(jnp.where(low, prod, 0.0), axis=-1, keepdims=True)
        in1 = jnp.sum(jnp.where(low, 0.0, prod), axis=-1, keepdims=True)
        dox[0] = jnp.where(low, dof, spread_parts(jnp.broadcast_to(-in0, (LEN, 128)), lane, HD)).astype(BF16)
        dox[1] = jnp.where(low, spread_parts(jnp.broadcast_to(-in1, (LEN, 128)), lane, 0), dof).astype(BF16)
        keep = lax.broadcasted_iota(jnp.int32, (BLK, BLK), 0) <= lax.broadcasted_iota(jnp.int32, (BLK, BLK), 1)
        for h in range(2):
            for j in reversed(range(nblk)):
                m = (j + 1) * BLK
                qj = qx[h, j * BLK:m]
                dj = dox[h, j * BLK:m]
                kk = kx[h, :m]
                st = dot_nt(kk, qj)
                pt = jnp.exp2(st)
                diag = jnp.where(keep, pt[j * BLK:], 0.0)
                pt = jnp.concatenate([pt[: j * BLK], diag], axis=0) if j else diag
                dpt = dot_nt(vx[h, :m], dj)
                dst = (pt * dpt).astype(BF16)
                ptb = pt.astype(BF16)
                if j == nblk - 1:
                    dv[h, :m] = dot_nn(ptb, dj)
                    dk[h, :m] = dot_nn(dst, qj)
                else:
                    dv[h, :m] += dot_nn(ptb, dj)
                    dk[h, :m] += dot_nn(dst, qj)
                dq[h, j * BLK:m] = dot_tn(dst, kk)
        qkv[p, seq, pl.ds(cq, 128)] = (jnp.where(low, dq[0], dq[1]) * 0.125).astype(BF16)
        qkv[p, seq, pl.ds(ck, 128)] = (jnp.where(low, dk[0], dk[1]) * LN2).astype(BF16)
        qkv[p, seq, pl.ds(cv, 128)] = jnp.where(low, dv[0], dv[1]).astype(BF16)
        return carry

    lax.fori_loop(0, seqs * 2, body, 0)


def compute_kernel(
    state_in, embed_in, grad_in, entry_w, exit_w, expand_w, reduce_w, lead_g, lead_s, mid_g, mid_s, exp_b, red_b,
    final_out, grad, embed_total, g_entry, g_exit, g_expand, g_reduce, g_small,
    mixed, qkv, att, lx, middle, active, gelup, datt, entry_t, exit_t, expand_t, reduce_t,
    vx, kx, qx, dox, dk, dv, dq, g_reduce_t, g_exp_b, *, tokens,
):
    seqs = tokens // LEN
    RA, RF, RC = 512, 512, 512

    def tiles(rows, fn):
        def body(i, c):
            fn(pl.ds(pl.multiple_of(i * rows, rows), rows))
            return c
        lax.fori_loop(0, tokens // rows, body, 0)

    lg, ls_, mg, ms = (r[...].astype(F32) for r in (lead_g, lead_s, mid_g, mid_s))
    eb, rb = exp_b[...].astype(F32), red_b[...].astype(F32)
    entry_t[...] = entry_w[...].T
    exit_t[...] = exit_w[...].T
    expand_t[...] = expand_w[...].T
    reduce_t[...] = reduce_w[...].T
    g_entry[...] = jnp.zeros_like(g_entry)
    g_exit[...] = jnp.zeros_like(g_exit)
    g_expand[...] = jnp.zeros_like(g_expand)
    g_reduce_t[...] = jnp.zeros_like(g_reduce_t)
    g_small[...] = jnp.zeros_like(g_small)
    g_exp_b[...] = jnp.zeros_like(g_exp_b)

    def enter(p):
        def fn(rows):
            e = embed_in[rows, :].astype(F32)
            x = (state_in[rows, :].astype(F32) if p == 0 else grad[rows, :]) + e
            mixed[p, rows, :] = x
            xhat, _ = norm_parts(x)
            n = (xhat * lg + ls_).astype(BF16)
            y = dot_nn(n, entry_w[...])
            qkv[p, rows, :D] = (y[:, :D] * (LOG2E * 0.125)).astype(BF16)
            qkv[p, rows, D:] = y[:, D:].astype(BF16)
        tiles(RA, fn)

    def feed_forward(p, rows):
        mid = mixed[p, rows, :] + dot_nn(att[p, rows, :], exit_w[...])
        middle[p, rows, :] = mid
        xhat, rstd = norm_parts(mid)
        n2 = (xhat * mg + ms).astype(BF16)
        hid = dot_nn(n2, expand_w[...]) + eb
        cdf, e = gelu_parts(hid)
        act = (hid * cdf).astype(BF16)
        gp = cdf + hid * (e * INV_SQRT_2PI)
        res = mid + dot_nn(act, reduce_w[...]) + rb
        return mid, xhat, rstd, n2, act, gp, res

    def feed_backward(p, rows, g, xhat, rstd, n2, act, gp):
        d_out = g.astype(BF16)
        g_small[5:6, :] += jnp.sum(g, axis=0, keepdims=True)
        g_reduce_t[...] += dot_tn(d_out, act)
        dh = dot_nn(d_out, reduce_t[...]) * gp
        g_exp_b[...] += jnp.sum(dh, axis=0, keepdims=True)
        dh = dh.astype(BF16)
        g_expand[...] += dot_tn(n2, dh)
        dn = dot_nn(dh, expand_t[...])
        g_small[2:3, :] += jnp.sum(dn * xhat, axis=0, keepdims=True)
        g_small[3:4, :] += jnp.sum(dn, axis=0, keepdims=True)
        dm = g + norm_pull(xhat, rstd, mg, dn)
        grad[rows, :] = dm
        db = dm.astype(BF16)
        g_exit[...] += dot_tn(att[p, rows, :], db)
        datt[rows, :] = dot_nn(db, exit_t[...]).astype(BF16)

    def ff_first(rows):
        mid, xhat, rstd, n2, act, gp, res = feed_forward(0, rows)
        active[rows, :] = act
        gelup[rows, :] = gp.astype(BF16)
        grad[rows, :] = res

    def ff_last(rows):
        mid, xhat, rstd, n2, act, gp, res = feed_forward(1, rows)
        final_out[rows, :] = res.astype(BF16)
        feed_backward(1, rows, grad_in[rows, :].astype(F32), xhat, rstd, n2, act, gp)

    def ff_back(rows):
        xhat, rstd = norm_parts(middle[0, rows, :])
        n2 = (xhat * mg + ms).astype(BF16)
        feed_backward(0, rows, grad[rows, :], xhat, rstd, n2, active[rows, :], gelup[rows, :].astype(F32))

    def leave(p):
        def fn(rows):
            xhat, rstd = norm_parts(mixed[p, rows, :])
            n = (xhat * lg + ls_).astype(BF16)
            dqkv = qkv[p, rows, :]
            g_entry[...] += dot_tn(n, dqkv)
            dn = dot_nn(dqkv, entry_t[...])
            g_small[0:1, :] += jnp.sum(dn * xhat, axis=0, keepdims=True)
            g_small[1:2, :] += jnp.sum(dn, axis=0, keepdims=True)
            g = grad[rows, :] + norm_pull(xhat, rstd, lg, dn)
            grad[rows, :] = g
            embed_total[rows, :] = g if p == 1 else embed_total[rows, :] + g
        tiles(RC, fn)

    enter(0)
    attn_forward(qkv, 0, att, lx, vx, seqs)
    tiles(RF, ff_first)
    enter(1)
    attn_forward(qkv, 1, att, lx, vx, seqs)
    tiles(RF, ff_last)
    attn_backward(qkv, 1, att, lx, datt, vx, kx, qx, dox, dk, dv, dq, seqs)
    leave(1)
    tiles(RF, ff_back)
    attn_backward(qkv, 0, att, lx, datt, vx, kx, qx, dox, dk, dv, dq, seqs)
    leave(0)
    g_reduce[...] = g_reduce_t[...].T
    for i in range(4):
        g_small[8 + i:9 + i, :] = g_exp_b[:, i * D:(i + 1) * D]


def compute(tokens):
    T = tokens
    sds = jax.ShapeDtypeStruct
    vm = pl.BlockSpec(memory_space=pltpu.VMEM)
    return pl.pallas_call(
        functools.partial(compute_kernel, tokens=tokens),
        in_specs=[vm] * 13,
        out_specs=[vm] * 8,
        out_shape=[
            sds((T, D), BF16), sds((T, D), F32), sds((T, D), F32),
            sds((D, 3 * D), F32), sds((D, D), F32), sds((D, FF), F32), sds((FF, D), F32), sds((16, D), F32),
        ],
        scratch_shapes=[
            pltpu.VMEM((2, T, D), F32), pltpu.VMEM((2, T, 3 * D), BF16), pltpu.VMEM((2, T, D), BF16), pltpu.VMEM((2, T, D), BF16),
            pltpu.VMEM((2, T, D), F32), pltpu.VMEM((T, FF), BF16), pltpu.VMEM((T, FF), BF16), pltpu.VMEM((T, D), BF16),
            pltpu.VMEM((3 * D, D), BF16), pltpu.VMEM((D, D), BF16), pltpu.VMEM((FF, D), BF16), pltpu.VMEM((D, FF), BF16),
            pltpu.VMEM((2, LEN, 128), BF16), pltpu.VMEM((2, LEN, 128), BF16), pltpu.VMEM((2, LEN, 128), BF16), pltpu.VMEM((2, LEN, 128), BF16),
            pltpu.VMEM((2, LEN, 128), F32), pltpu.VMEM((2, LEN, 128), F32), pltpu.VMEM((2, LEN, 128), F32),
            pltpu.VMEM((D, FF), F32), pltpu.VMEM((1, FF), F32),
        ],
        compiler_params=pltpu.CompilerParams(vmem_limit_bytes=62 * 1024 * 1024),
        name="compute",
    )


def on_device(loop_state, embedding, output_grad, entry_weight, exit_weight, lead_gain, lead_shift, expand_weight, reduce_weight, middle_gain, middle_shift, expand_bias, reduce_bias):
    n = lax.axis_size("fsdp")
    tokens = loop_state.shape[0]
    shards = (entry_weight, exit_weight, expand_weight, reduce_weight, lead_gain, lead_shift, middle_gain, middle_shift, expand_bias, reduce_bias)
    packed = jnp.concatenate([a.reshape(-1) for a in shards])
    whole = lax.all_gather(packed, "fsdp", axis=0)
    full, at = [], 0
    for a in shards:
        full.append(whole[:, at : at + a.size].reshape((n * a.shape[0],) + a.shape[1:]))
        at += a.size
    entry_w, exit_w, expand_w, reduce_w, lg, ls, mg, ms, eb, rb = full
    row = lambda a: a.reshape(1, -1)
    final, grad, total, g_entry, g_exit, g_expand, g_reduce, small = compute(tokens)(
        loop_state, embedding, output_grad, entry_w, exit_w, expand_w, reduce_w, row(lg), row(ls), row(mg), row(ms), row(eb), row(rb)
    )
    terms = (g_entry, g_exit, g_expand, g_reduce, small[0], small[1], small[2], small[3], small[8:12].reshape(-1), small[5])
    sums = lax.psum_scatter(jnp.concatenate([a.reshape(n, -1) for a in terms], axis=1), "fsdp", scatter_dimension=0, tiled=True)[0]
    outs, at = [], 0
    for a in terms:
        shape = (a.shape[0] // n,) + a.shape[1:]
        size = a.size // n
        outs.append(sums[at : at + size].reshape(shape))
        at += size
    entry_g, exit_g, expand_g, reduce_g, lgg, lsg, mgg, msg, ebg, rbg = outs
    return (final, grad, total, entry_g, exit_g, lgg, lsg, expand_g, reduce_g, mgg, msg, ebg, rbg)


def solution(mesh):
    two, one = P("fsdp", None), P("fsdp")
    in_specs = (two, two, two, two, two, one, one, two, two, one, one, one, one)
    out_specs = (two, two, two, two, two, one, one, two, two, one, one, one, one)
    return jax.shard_map(on_device, mesh=mesh, in_specs=in_specs, out_specs=out_specs, check_vma=False)
```

```python
import functools
import math
import jax
import jax.numpy as jnp
from jax import lax
from jax.experimental import pallas as pl
from jax.experimental.pallas import tpu as pltpu
from jax.sharding import PartitionSpec as P
from types import SimpleNamespace

F32, BF16 = jnp.float32, jnp.bfloat16
LEN = 1024
LOOPS = 2
EPS = 1e-05
D = 256
FF = 1024
HD = 64
LOG2E = 1.4426950408889634
LN2 = 0.6931471805599453
BLK = 256
NEG = -1e30


def dot_nn(a, b):
    return lax.dot_general(a, b, (((1,), (0,)), ((), ())), preferred_element_type=F32)


def dot_nt(a, b):
    return lax.dot_general(a, b, (((1,), (1,)), ((), ())), preferred_element_type=F32)


def dot_tn(a, b):
    return lax.dot_general(a, b, (((0,), (0,)), ((), ())), preferred_element_type=F32)


def norm_parts(x):
    mean = jnp.mean(x, axis=-1, keepdims=True)
    center = x - mean
    var = jnp.mean(center * center, axis=-1, keepdims=True)
    rstd = lax.rsqrt(var + EPS)
    return center * rstd, rstd


def norm_pull(xhat, rstd, gain, dy):
    dn = dy * gain
    m1 = jnp.mean(dn, axis=-1, keepdims=True)
    m2 = jnp.mean(dn * xhat, axis=-1, keepdims=True)
    return rstd * (dn - m1 - xhat * m2)


def gelu_parts(x):
    z = jnp.abs(x)
    t = 1.0 / (1.0 + (0.3275911 / math.sqrt(2.0)) * z)
    e = jnp.exp2((-0.5 * LOG2E) * (x * x))
    poly = t * (0.5 * 0.254829592 + t * (0.5 * -0.284496736 + t * (0.5 * 1.421413741 + t * (0.5 * -1.453152027 + t * (0.5 * 1.061405429)))))
    tail = poly * e
    cdf = jnp.where(x >= 0.0, 1.0 - tail, tail)
    return cdf, e


INV_SQRT_2PI = 1.0 / math.sqrt(2.0 * math.pi)


def lane_iota(rows):
    return lax.broadcasted_iota(jnp.int32, (rows, 128), 1)


def three_parts(x):
    hi = x.astype(BF16).astype(F32)
    r = x - hi
    mid = r.astype(BF16).astype(F32)
    return hi, mid, r - mid


def spread_parts(x, lane, spare):
    hi, mid, lo = three_parts(x)
    return jnp.where(lane == spare, hi, jnp.where(lane == spare + 1, mid, jnp.where(lane == spare + 2, lo, 0.0)))


def attn_forward(qkv, p, att, lx, vx, seqs, hook=None):
    nblk = LEN // BLK

    def body(it, carry):
        if hook is not None:
            hook(it)
        s = it // 2
        pair = it % 2
        r0 = pl.multiple_of(s * LEN, LEN)
        cq = pl.multiple_of(pair * 128, 128)
        ck = pl.multiple_of(D + pair * 128, 128)
        cv = pl.multiple_of(2 * D + pair * 128, 128)
        lane = lane_iota(LEN)
        v = qkv[p, pl.ds(r0, LEN), pl.ds(cv, 128)]
        one = jnp.ones((LEN, 128), BF16)
        vx[0] = jnp.where(lane < HD, v, one)
        vx[1] = jnp.where(lane < HD, one, v)
        laneb = lane_iota(BLK)
        keep = lax.broadcasted_iota(jnp.int32, (BLK, BLK), 1) <= lax.broadcasted_iota(jnp.int32, (BLK, BLK), 0)
        for j in range(nblk):
            rows = pl.ds(pl.multiple_of(r0 + j * BLK, BLK), BLK)
            q = qkv[p, rows, pl.ds(cq, 128)]
            zero = jnp.zeros_like(q)
            outs, pieces = [], []
            for h in range(2):
                mine = (laneb < HD) if h == 0 else (laneb >= HD)
                qm = jnp.where(mine, q, zero)
                m_rows = (j + 1) * BLK
                k = qkv[p, pl.ds(r0, m_rows), pl.ds(ck, 128)]
                sc = dot_nt(qm, k)
                diag = jnp.where(keep, sc[:, j * BLK:], NEG)
                sc = jnp.concatenate([sc[:, : j * BLK], diag], axis=1) if j else diag
                top = jnp.max(sc, axis=-1, keepdims=True)
                pr = jnp.exp2(sc - top).astype(BF16)
                ox = dot_nn(pr, vx[h, :m_rows])
                den = pltpu.roll(ox, HD, 1)
                outs.append(ox / den)
                lse = top + jnp.log(ox) * LOG2E
                lse = jnp.where(mine, 0.0, lse)
                pieces.append(spread_parts(-lse, laneb, HD if h == 0 else 0))
            att[p, rows, pl.ds(cq, 128)] = jnp.where(laneb < HD, outs[0], outs[1]).astype(BF16)
            lx[p, rows, pl.ds(cq, 128)] = jnp.where(laneb < HD, pieces[1], pieces[0]).astype(BF16)
        return carry

    lax.fori_loop(0, seqs * 2, body, 0)


def attn_backward(qkv, p, att, lx, dmid_att, vx, kx, qx, dox, dk, dv, dq, seqs, hook=None):
    nblk = LEN // BLK

    def body(it, carry):
        if hook is not None:
            hook(it)
        s = it // 2
        pair = it % 2
        r0 = pl.multiple_of(s * LEN, LEN)
        cq = pl.multiple_of(pair * 128, 128)
        ck = pl.multiple_of(D + pair * 128, 128)
        cv = pl.multiple_of(2 * D + pair * 128, 128)
        lane = lane_iota(LEN)
        seq = pl.ds(r0, LEN)
        low = lane < HD
        one = jnp.ones((LEN, 128), BF16)
        v = qkv[p, seq, pl.ds(cv, 128)]
        vx[0] = jnp.where(low, v, one)
        vx[1] = jnp.where(low, one, v)
        k = qkv[p, seq, pl.ds(ck, 128)]
        kx[0] = jnp.where(low, k, one)
        kx[1] = jnp.where(low, one, k)
        q = qkv[p, seq, pl.ds(cq, 128)]
        ls = lx[p, seq, pl.ds(cq, 128)]
        qx[0] = jnp.where(low, q, ls)
        qx[1] = jnp.where(low, ls, q)
        do = dmid_att[seq, pl.ds(cq, 128)]
        dof = do.astype(F32)
        prod = dof * att[p, seq, pl.ds(cq, 128)].astype(F32)
        in0 = jnp.sum(jnp.where(low, prod, 0.0), axis=-1, keepdims=True)
        in1 = jnp.sum(jnp.where(low, 0.0, prod), axis=-1, keepdims=True)
        dox[0] = jnp.where(low, dof, spread_parts(jnp.broadcast_to(-in0, (LEN, 128)), lane, HD)).astype(BF16)
        dox[1] = jnp.where(low, spread_parts(jnp.broadcast_to(-in1, (LEN, 128)), lane, 0), dof).astype(BF16)
        keep = lax.broadcasted_iota(jnp.int32, (BLK, BLK), 0) <= lax.broadcasted_iota(jnp.int32, (BLK, BLK), 1)
        for h in range(2):
            for j in reversed(range(nblk)):
                m = (j + 1) * BLK
                qj = qx[h, j * BLK:m]
                dj = dox[h, j * BLK:m]
                kk = kx[h, :m]
                st = dot_nt(kk, qj)
                pt = jnp.exp2(st)
                diag = jnp.where(keep, pt[j * BLK:], 0.0)
                pt = jnp.concatenate([pt[: j * BLK], diag], axis=0) if j else diag
                dpt = dot_nt(vx[h, :m], dj)
                dst = (pt * dpt).astype(BF16)
                ptb = pt.astype(BF16)
                if j == nblk - 1:
                    dv[h, :m] = dot_nn(ptb, dj)
                    dk[h, :m] = dot_nn(dst, qj)
                else:
                    dv[h, :m] += dot_nn(ptb, dj)
                    dk[h, :m] += dot_nn(dst, qj)
                dq[h, j * BLK:m] = dot_tn(dst, kk)
        qkv[p, seq, pl.ds(cq, 128)] = (jnp.where(low, dq[0], dq[1]) * 0.125).astype(BF16)
        qkv[p, seq, pl.ds(ck, 128)] = (jnp.where(low, dk[0], dk[1]) * LN2).astype(BF16)
        qkv[p, seq, pl.ds(cv, 128)] = jnp.where(low, dv[0], dv[1]).astype(BF16)
        return carry

    lax.fori_loop(0, seqs * 2, body, 0)


def digit_groups(n):
    groups = [(1, 2)]
    stride = 2
    while stride < n:
        size = min(4, n // stride)
        groups.append((stride, size))
        stride *= size
    return groups[::-1]


class Links:
    def __init__(self, n):
        self.groups = digit_groups(n)
        self.me = lax.axis_index("fsdp")
        self.digits = [(self.me // stride) % size for stride, size in self.groups]
        self.sizes = tuple(size for _, size in self.groups)

    def digit(self, g, t):
        return (self.digits[g] + t) % self.sizes[g]

    def peer(self, g, t):
        return self.me + (self.digit(g, t) - self.digits[g]) * self.groups[g][0]

    def barrier(self):
        sem = pltpu.get_barrier_semaphore()
        count = 0
        for g, size in enumerate(self.sizes):
            for t in range(1, size):
                pl.semaphore_signal(sem, inc=1, device_id=(self.peer(g, t),), device_id_type=pl.DeviceIdType.MESH)
                count += 1
        return lambda: pl.semaphore_wait(sem, count)

    def copy(self, src, dst, sems, g, t):
        return pltpu.make_async_remote_copy(
            src_ref=src,
            dst_ref=dst,
            send_sem=sems.at[0, g, t - 1],
            recv_sem=sems.at[1, g, t - 1],
            device_id=(self.peer(g, t),),
            device_id_type=pl.DeviceIdType.MESH,
        )

    def held(self, buf, g, t=0):
        tail = [self.digit(g, t)] + self.digits[g + 1:]
        return buf.at[(slice(None),) * g + tuple(tail)]

    def gather_start(self, buf, sems, g):
        for t in range(1, self.sizes[g]):
            self.copy(self.held(buf, g), self.held(buf, g), sems, g, t).start()

    def gather_wait(self, buf, sems, g):
        for t in range(1, self.sizes[g]):
            self.copy(self.held(buf, g), self.held(buf, g, -t), sems, g, t).wait_recv()
        for t in range(1, self.sizes[g]):
            self.copy(self.held(buf, g), self.held(buf, g), sems, g, t).wait_send()

    def reduce_start(self, part, got, sems, g):
        for t in range(1, self.sizes[g]):
            src = part.at[(slice(None),) * g + (self.digit(g, t),)]
            self.copy(src, got.at[t - 1], sems, g, t).start()

    def reduce_wait(self, part, got, sems, g):
        for t in range(1, self.sizes[g]):
            src = part.at[(slice(None),) * g + (self.digit(g, t),)]
            self.copy(src, got.at[t - 1], sems, g, t).wait()
        total = part[(slice(None),) * g + (self.digits[g],)].astype(F32)
        for t in range(1, self.sizes[g]):
            total = total + got[t - 1].astype(F32)
        return total


def pair_rows(x, t):
    return jnp.concatenate([x[:, 256 * t : 256 * t + 128], x[:, 256 * t + 128 : 256 * t + 256]], axis=0)


ENTRY_ROWS = 64
FEED_ROWS = 160


def mega_kernel(*refs, names, n, tokens, comm):
    o = SimpleNamespace(**dict(zip(names, refs)))
    seqs = tokens // LEN
    RA = RF = RC = 512

    def tiles(rows, fn):
        def body(i, c):
            fn(pl.ds(pl.multiple_of(i * rows, rows), rows))
            return c
        lax.fori_loop(0, tokens // rows, body, 0)

    def zero(*rs):
        for r in rs:
            r[...] = jnp.zeros_like(r)

    def pack_parameters():
        d = tuple(links.digits)
        x = o.entry_s[...].astype(F32)
        for t in range(3):
            o.buf1[d + (pl.ds(16 * t, 16),)] = pair_rows(x, t).astype(BF16)
        o.vec[...] = jnp.zeros_like(o.vec)
        for i, r in enumerate((o.lead_g, o.lead_s, o.mid_g, o.mid_s, o.red_b)):
            o.vec[i:i + 1, 0:8] = r[...].astype(F32).reshape(1, 8)
        o.vec[8:9, 0:32] = o.exp_b[...].astype(F32).reshape(1, 32)
        low = pltpu.roll(o.vec[0:8, :], (links.me * 8) % 128, 1)
        high = pltpu.roll(jnp.broadcast_to(o.vec[8:9, :], (8, 128)), (links.me * 32) % 128, 1)
        row = lax.broadcasted_iota(jnp.int32, (8, 128), 0)
        high = jnp.where(row == links.me // 4, high, 0.0)
        o.buf1[d + (pl.ds(48, 16),)] = jnp.concatenate([low, high], axis=0).astype(BF16)
        o.buf2[d + (pl.ds(0, 16),)] = pair_rows(o.exit_s[...].astype(F32), 0).astype(BF16)
        x = o.expand_s[...].astype(F32)
        for t in range(4):
            o.buf2[d + (pl.ds(16 + 16 * t, 16),)] = pair_rows(x, t).astype(BF16)
        for c in range(2):
            o.buf2[d + (pl.ds(80 + 32 * c, 32),)] = o.reduce_s[:, 128 * c:128 * c + 128]

    def unpack(buf, at, chunks, dst):
        for t in range(chunks // 2):
            x = buf[:, :, :, at + 16 * t:at + 16 * t + 16, :].astype(F32).reshape(n, 16, 128)
            dst[:, 256 * t:256 * t + 128] = x[:, :8].reshape(8 * n, 128).astype(BF16)
            dst[:, 256 * t + 128:256 * t + 256] = x[:, 8:].reshape(8 * n, 128).astype(BF16)

    def unpack_first():
        unpack(o.buf1, 0, 6, o.entry_w)
        v = o.buf1[:, :, :, 48:64, :].astype(F32).reshape(n, 16, 128)
        first = jnp.sum(v[: n // 2], axis=0)
        second = jnp.sum(v[n // 2:], axis=0)
        o.vecs[0:5, 0:128] = first[0:5]
        o.vecs[0:5, 128:256] = second[0:5]
        both = (first + second)[8:16]
        for c in range(8):
            o.eb[0:1, 128 * c:128 * c + 128] = both[c:c + 1]
        o.entry_t[...] = o.entry_w[...].T

    def unpack_second():
        unpack(o.buf2, 0, 2, o.exit_w)
        unpack(o.buf2, 16, 8, o.expand_w)
        for c in range(2):
            x = o.buf2[:, :, :, 80 + 32 * c:112 + 32 * c, :]
            o.reduce_w[:, 128 * c:128 * c + 128] = x.reshape(32 * n, 128)
        turn_second()

    def turn_second():
        o.exit_t[...] = o.exit_w[...].T
        o.expand_t[...] = o.expand_w[...].T
        o.reduce_t[...] = o.reduce_w[...].T

    def pack_gradient(part, at, chunks, grad):
        for t in range(chunks // 2):
            a = grad[:, 256 * t:256 * t + 128].reshape(n, 8, 128)
            b = grad[:, 256 * t + 128:256 * t + 256].reshape(n, 8, 128)
            x = jnp.concatenate([a, b], axis=1).astype(BF16)
            part[:, :, :, at + 16 * t:at + 16 * t + 16, :] = x.reshape(links.sizes + (16, 128))

    def pack_vectors(part, at, rows):
        x = jnp.concatenate(rows + [jnp.zeros((16 - len(rows), 128), F32)], axis=0) if len(rows) < 16 else jnp.concatenate(rows, axis=0)
        part[:, :, :, at:at + 16, :] = jnp.broadcast_to(x.astype(BF16), links.sizes + (16, 128))

    def halves(row):
        return [row[:, :128], row[:, 128:]]

    def own_eight(total, at):
        both = jnp.where(links.me >= n // 2, total[at + 1:at + 2], total[at:at + 1])
        both = pltpu.roll(jnp.broadcast_to(both, (8, 128)), (128 - (links.me * 8) % 128) % 128, 1)
        return both[0:1, 0:8].reshape(8)

    def feed_reduce_pack():
        pack_gradient(o.buf2, 0, 2, o.g_exit)
        pack_gradient(o.buf2, 16, 8, o.g_expand)
        for c in range(2):
            x = o.g_reduce_t[128 * c:128 * c + 128, :].T.astype(BF16)
            o.buf2[:, :, :, 80 + 32 * c:112 + 32 * c, :] = x.reshape(links.sizes + (32, 128))
        rows = halves(o.g_small[2:3, :]) + halves(o.g_small[3:4, :]) + halves(o.g_small[5:6, :])
        rows += [o.g_exp_b[:, 128 * c:128 * c + 128] for c in range(8)]
        pack_vectors(o.buf2, 144, rows)

    def feed_reduce_end(total):
        for c in range(2):
            o.exit_o[:, 128 * c:128 * c + 128] = total[8 * c:8 * c + 8]
            o.reduce_o[:, 128 * c:128 * c + 128] = total[80 + 32 * c:112 + 32 * c]
        for c in range(8):
            o.expand_o[:, 128 * c:128 * c + 128] = total[16 + 8 * c:24 + 8 * c]
        o.mid_g_o[...] = own_eight(total, 144)
        o.mid_s_o[...] = own_eight(total, 146)
        o.red_b_o[...] = own_eight(total, 148)
        row = lax.broadcasted_iota(jnp.int32, (8, 128), 0)
        x = jnp.sum(jnp.where(row == links.me // 4, total[150:158], 0.0), axis=0, keepdims=True)
        x = pltpu.roll(jnp.broadcast_to(x, (8, 128)), (128 - (links.me * 32) % 128) % 128, 1)
        o.exp_b_o[...] = x[0:1, 0:32].reshape(32)

    def entry_reduce_pack():
        pack_gradient(o.buf1, 0, 6, o.g_entry)
        pack_vectors(o.buf1, 48, halves(o.g_small[0:1, :]) + halves(o.g_small[1:2, :]))

    def entry_reduce_end(total):
        for c in range(6):
            o.entry_o[:, 128 * c:128 * c + 128] = total[8 * c:8 * c + 8]
        o.lead_g_o[...] = own_eight(total, 48)
        o.lead_s_o[...] = own_eight(total, 50)

    def enter(p):
        lg, ls = o.vecs[0:1, :], o.vecs[1:2, :]

        def fn(rows):
            e = o.embed_in[rows, :].astype(F32)
            x = (o.state_in[rows, :].astype(F32) if p == 0 else o.grad[rows, :]) + e
            o.mixed[p, rows, :] = x
            xhat, _ = norm_parts(x)
            y = dot_nn((xhat * lg + ls).astype(BF16), o.entry_w[...])
            o.qkv[p, rows, :D] = (y[:, :D] * (LOG2E * 0.125)).astype(BF16)
            o.qkv[p, rows, D:] = y[:, D:].astype(BF16)
        tiles(RA, fn)

    def feed_forward(p, rows):
        mg, ms, rb = o.vecs[2:3, :], o.vecs[3:4, :], o.vecs[4:5, :]
        mid = o.mixed[p, rows, :] + dot_nn(o.att[p, rows, :], o.exit_w[...])
        xhat, rstd = norm_parts(mid)
        n2 = (xhat * mg + ms).astype(BF16)
        hid = dot_nn(n2, o.expand_w[...]) + o.eb[...]
        cdf, e = gelu_parts(hid)
        act = (hid * cdf).astype(BF16)
        gp = cdf + hid * (e * INV_SQRT_2PI)
        res = mid + dot_nn(act, o.reduce_w[...]) + rb
        return mid, xhat, rstd, n2, act, gp, res

    def feed_backward(p, rows, g, xhat, rstd, n2, act, gp):
        d_out = g.astype(BF16)
        o.g_small[5:6, :] += jnp.sum(g, axis=0, keepdims=True)
        o.g_reduce_t[...] += dot_tn(d_out, act)
        dh = dot_nn(d_out, o.reduce_t[...]) * gp
        o.g_exp_b[...] += jnp.sum(dh, axis=0, keepdims=True)
        dh = dh.astype(BF16)
        o.g_expand[...] += dot_tn(n2, dh)
        dn = dot_nn(dh, o.expand_t[...])
        o.g_small[2:3, :] += jnp.sum(dn * xhat, axis=0, keepdims=True)
        o.g_small[3:4, :] += jnp.sum(dn, axis=0, keepdims=True)
        dm = g + norm_pull(xhat, rstd, o.vecs[2:3, :], dn)
        o.grad[rows, :] = dm
        db = dm.astype(BF16)
        o.g_exit[...] += dot_tn(o.att[p, rows, :], db)
        o.datt[rows, :] = dot_nn(db, o.exit_t[...]).astype(BF16)

    def ff_first(rows):
        mid, xhat, rstd, n2, act, gp, res = feed_forward(0, rows)
        o.middle[rows, :] = mid
        o.active[rows, :] = act
        o.gelup[rows, :] = gp.astype(BF16)
        o.grad[rows, :] = res

    def ff_last(rows):
        mid, xhat, rstd, n2, act, gp, res = feed_forward(1, rows)
        o.final[rows, :] = res.astype(BF16)
        feed_backward(1, rows, o.grad_in[rows, :].astype(F32), xhat, rstd, n2, act, gp)

    def ff_back(rows):
        xhat, rstd = norm_parts(o.middle[rows, :])
        n2 = (xhat * o.vecs[2:3, :] + o.vecs[3:4, :]).astype(BF16)
        feed_backward(0, rows, o.grad[rows, :], xhat, rstd, n2, o.active[rows, :], o.gelup[rows, :].astype(F32))

    def leave(p):
        lg, ls = o.vecs[0:1, :], o.vecs[1:2, :]

        def fn(rows):
            xhat, rstd = norm_parts(o.mixed[p, rows, :])
            dqkv = o.qkv[p, rows, :]
            o.g_entry[...] += dot_tn((xhat * lg + ls).astype(BF16), dqkv)
            dn = dot_nn(dqkv, o.entry_t[...])
            o.g_small[0:1, :] += jnp.sum(dn * xhat, axis=0, keepdims=True)
            o.g_small[1:2, :] += jnp.sum(dn, axis=0, keepdims=True)
            g = o.grad[rows, :] + norm_pull(xhat, rstd, lg, dn)
            o.grad[rows, :] = g
            o.total[rows, :] = g if p == 1 else o.total[rows, :] + g
        tiles(RC, fn)

    def backward(p, hook=None):
        attn_backward(o.qkv, p, o.att, o.lx, o.datt, o.vx, o.kx, o.qx, o.dox, o.dk, o.dv, o.dq, seqs, hook)

    def clear():
        zero(o.g_entry, o.g_exit, o.g_expand, o.g_reduce_t, o.g_small, o.g_exp_b)

    if comm:
        links = Links(n)
        arrived = links.barrier()
        pack_parameters()
        arrived()
        links.gather_start(o.buf1, o.sem1, 0)
        clear()
        links.gather_wait(o.buf1, o.sem1, 0)
        links.gather_start(o.buf1, o.sem1, 1)
        links.gather_start(o.buf2, o.sem2, 0)
        links.gather_wait(o.buf1, o.sem1, 1)
        links.gather_start(o.buf1, o.sem1, 2)
        links.gather_wait(o.buf1, o.sem1, 2)
        unpack_first()
    else:
        clear()
        for i, r in enumerate((o.lead_g, o.lead_s, o.mid_g, o.mid_s, o.red_b)):
            o.vecs[i:i + 1, :] = r[...].astype(F32)
        o.eb[...] = o.exp_b[...].astype(F32)
        o.entry_t[...] = o.entry_w[...].T
        turn_second()

    enter(0)
    if comm:
        links.gather_wait(o.buf2, o.sem2, 0)
        links.gather_start(o.buf2, o.sem2, 1)

        def gather_more(it):
            @pl.when(it == seqs)
            def _():
                links.gather_wait(o.buf2, o.sem2, 1)
                links.gather_start(o.buf2, o.sem2, 2)

        attn_forward(o.qkv, 0, o.att, o.lx, o.vx, seqs, gather_more)
        links.gather_wait(o.buf2, o.sem2, 2)
        unpack_second()
    else:
        attn_forward(o.qkv, 0, o.att, o.lx, o.vx, seqs)
    tiles(RF, ff_first)
    enter(1)
    attn_forward(o.qkv, 1, o.att, o.lx, o.vx, seqs)
    tiles(RF, ff_last)
    backward(1)
    leave(1)
    tiles(RF, ff_back)
    if comm:
        feed_reduce_pack()
        links.reduce_start(o.buf2, o.feed_got0, o.sem3, 2)

        def reduce_more(it):
            @pl.when(it == 1)
            def _():
                o.feed_part1[...] = links.reduce_wait(o.buf2, o.feed_got0, o.sem3, 2).astype(BF16)
                links.reduce_start(o.feed_part1, o.feed_got1, o.sem3, 1)

            @pl.when(it == 2 * seqs - 2)
            def _():
                o.feed_part2[...] = links.reduce_wait(o.feed_part1, o.feed_got1, o.sem3, 1).astype(BF16)
                links.reduce_start(o.feed_part2, o.feed_got2, o.sem3, 0)

        backward(0, reduce_more)
        feed_reduce_end(links.reduce_wait(o.feed_part2, o.feed_got2, o.sem3, 0))
        leave(0)
        entry_reduce_pack()
        links.reduce_start(o.buf1, o.entry_got0, o.sem4, 2)
        o.entry_part1[...] = links.reduce_wait(o.buf1, o.entry_got0, o.sem4, 2).astype(BF16)
        links.reduce_start(o.entry_part1, o.entry_got1, o.sem4, 1)
        o.entry_part2[...] = links.reduce_wait(o.entry_part1, o.entry_got1, o.sem4, 1).astype(BF16)
        links.reduce_start(o.entry_part2, o.entry_got2, o.sem4, 0)
        entry_reduce_end(links.reduce_wait(o.entry_part2, o.entry_got2, o.sem4, 0))
    else:
        backward(0)
        leave(0)
        o.g_reduce[...] = o.g_reduce_t[...].T
        for i in range(4):
            o.g_small[8 + i:9 + i, :] = o.g_exp_b[:, i * D:(i + 1) * D]


TOKEN_INPUTS = ("state_in", "embed_in", "grad_in")
VECTOR_INPUTS = ("lead_g", "lead_s", "mid_g", "mid_s", "red_b", "exp_b")


def mega(n, tokens, comm):
    T = tokens
    sds, vmem = jax.ShapeDtypeStruct, pltpu.VMEM
    outs = [("final", sds((T, D), BF16)), ("grad", sds((T, D), F32)), ("total", sds((T, D), F32))]
    scratch = [
        ("mixed", vmem((2, T, D), F32)), ("qkv", vmem((2, T, 3 * D), BF16)), ("att", vmem((2, T, D), BF16)), ("lx", vmem((2, T, D), BF16)),
        ("middle", vmem((T, D), F32)), ("active", vmem((T, FF), BF16)), ("gelup", vmem((T, FF), BF16)), ("datt", vmem((T, D), BF16)),
        ("entry_t", vmem((3 * D, D), BF16)), ("exit_t", vmem((D, D), BF16)), ("expand_t", vmem((FF, D), BF16)), ("reduce_t", vmem((D, FF), BF16)),
        ("vecs", vmem((8, D), F32)), ("eb", vmem((1, FF), F32)),
        ("vx", vmem((2, LEN, 128), BF16)), ("kx", vmem((2, LEN, 128), BF16)), ("qx", vmem((2, LEN, 128), BF16)), ("dox", vmem((2, LEN, 128), BF16)),
        ("dk", vmem((2, LEN, 128), F32)), ("dv", vmem((2, LEN, 128), F32)), ("dq", vmem((2, LEN, 128), F32)),
        ("g_reduce_t", vmem((D, FF), F32)), ("g_exp_b", vmem((1, FF), F32)),
    ]
    grads = [("g_entry", (D, 3 * D)), ("g_exit", (D, D)), ("g_expand", (D, FF)), ("g_small", (16, D))]
    weights = [("entry_w", (D, 3 * D)), ("exit_w", (D, D)), ("expand_w", (D, FF)), ("reduce_w", (FF, D))]
    if comm:
        ins = TOKEN_INPUTS + ("entry_s", "exit_s", "expand_s", "reduce_s") + VECTOR_INPUTS
        r, rr = D // n, FF // n
        outs += [
            ("entry_o", sds((r, 3 * D), F32)), ("exit_o", sds((r, D), F32)), ("lead_g_o", sds((r,), F32)), ("lead_s_o", sds((r,), F32)),
            ("expand_o", sds((r, FF), F32)), ("reduce_o", sds((rr, D), F32)), ("mid_g_o", sds((r,), F32)), ("mid_s_o", sds((r,), F32)),
            ("exp_b_o", sds((rr,), F32)), ("red_b_o", sds((r,), F32)),
        ]
        scratch += [(name, vmem(shape, F32)) for name, shape in grads] + [(name, vmem(shape, BF16)) for name, shape in weights]
        s = tuple(size for _, size in digit_groups(n))
        scratch += [("vec", vmem((16, 128), F32))]
        scratch += [("buf1", vmem(s + (ENTRY_ROWS, 128), BF16)), ("buf2", vmem(s + (FEED_ROWS, 128), BF16))]
        for name, rows in (("entry", ENTRY_ROWS), ("feed", FEED_ROWS)):
            for step, g in enumerate((2, 1, 0)):
                scratch.append((f"{name}_got{step}", vmem((s[g] - 1,) + s[:g] + (rows, 128), BF16)))
                if g < 2:
                    scratch.append((f"{name}_part{step}", vmem(s[: g + 1] + (rows, 128), BF16)))
        scratch += [(f"sem{i}", pltpu.SemaphoreType.DMA((2, 3, 3))) for i in (1, 2, 3, 4)]
    else:
        ins = TOKEN_INPUTS + tuple(name for name, _ in weights) + VECTOR_INPUTS
        outs += [(name, sds(shape, F32)) for name, shape in grads] + [("g_reduce", sds((FF, D), F32))]
    names = ins + tuple(name for name, _ in outs) + tuple(name for name, _ in scratch)
    spec = pl.BlockSpec(memory_space=pltpu.VMEM)
    params = dict(collective_id=0, has_side_effects=True) if comm else {}
    return pl.pallas_call(
        functools.partial(mega_kernel, names=names, n=n, tokens=T, comm=comm),
        in_specs=[spec] * len(ins),
        out_specs=[spec] * len(outs),
        out_shape=[shape for _, shape in outs],
        scratch_shapes=[shape for _, shape in scratch],
        compiler_params=pltpu.CompilerParams(vmem_limit_bytes=62 * 1024 * 1024, **params),
        name="block",
    )


def on_device(loop_state, embedding, output_grad, entry_weight, exit_weight, lead_gain, lead_shift, expand_weight, reduce_weight, middle_gain, middle_shift, expand_bias, reduce_bias):
    n = lax.axis_size("fsdp")
    tokens = loop_state.shape[0]
    vectors = (lead_gain, lead_shift, middle_gain, middle_shift, reduce_bias, expand_bias)
    weights = (entry_weight, exit_weight, expand_weight, reduce_weight)
    if entry_weight.shape[0] == 8 and len(digit_groups(n)) == 3:
        final, grad, total, entry_g, exit_g, lgg, lsg, expand_g, reduce_g, mgg, msg, ebg, rbg = mega(n, tokens, True)(
            loop_state, embedding, output_grad, *weights, *vectors
        )
        return (final, grad, total, entry_g, exit_g, lgg, lsg, expand_g, reduce_g, mgg, msg, ebg, rbg)
    shards = weights + vectors
    packed = jnp.concatenate([a.reshape(-1) for a in shards])
    whole = lax.all_gather(packed, "fsdp", axis=0)
    full, at = [], 0
    for a in shards:
        whole_a = whole[:, at : at + a.size].reshape((n * a.shape[0],) + a.shape[1:])
        full.append(whole_a if a.ndim == 2 else whole_a.reshape(1, -1))
        at += a.size
    final, grad, total, g_entry, g_exit, g_expand, small, g_reduce = mega(n, tokens, False)(loop_state, embedding, output_grad, *full)
    terms = (g_entry, g_exit, small[0], small[1], g_expand, g_reduce, small[2], small[3], small[8:12].reshape(-1), small[5])
    sums = lax.psum_scatter(jnp.concatenate([a.reshape(n, -1) for a in terms], axis=1), "fsdp", scatter_dimension=0, tiled=True)[0]
    outs, at = [], 0
    for a in terms:
        size = a.size // n
        outs.append(sums[at : at + size].reshape((a.shape[0] // n,) + a.shape[1:]))
        at += size
    return (final, grad, total, *outs)


def solution(mesh):
    two, one = P("fsdp", None), P("fsdp")
    in_specs = (two, two, two, two, two, one, one, two, two, one, one, one, one)
    out_specs = (two, two, two, two, two, one, one, two, two, one, one, one, one)
    return jax.shard_map(on_device, mesh=mesh, in_specs=in_specs, out_specs=out_specs, check_vma=False)
```

```python
import functools
import math
from types import SimpleNamespace

import jax
import jax.numpy as jnp
from jax import lax
from jax.experimental import pallas as pl
from jax.experimental.pallas import tpu as pltpu
from jax.sharding import PartitionSpec as P

F32, BF16 = jnp.float32, jnp.bfloat16
LEN = 1024
EPS = 1e-05
D = 256
FF = 1024
HD = 64
BLK = 256
LOG2E = 1.4426950408889634
LN2 = 0.6931471805599453
INV_SQRT_2PI = 1.0 / math.sqrt(2.0 * math.pi)
NEG = -1e30


def dot_nn(a, b):
    return lax.dot_general(a, b, (((1,), (0,)), ((), ())), preferred_element_type=F32)


def dot_nt(a, b):
    return lax.dot_general(a, b, (((1,), (1,)), ((), ())), preferred_element_type=F32)


def dot_tn(a, b):
    return lax.dot_general(a, b, (((0,), (0,)), ((), ())), preferred_element_type=F32)


def norm_parts(x):
    mean = jnp.mean(x, axis=-1, keepdims=True)
    center = x - mean
    var = jnp.mean(center * center, axis=-1, keepdims=True)
    rstd = lax.rsqrt(var + EPS)
    return center * rstd, rstd


def norm_pull(xhat, rstd, gain, dy):
    dn = dy * gain
    m1 = jnp.mean(dn, axis=-1, keepdims=True)
    m2 = jnp.mean(dn * xhat, axis=-1, keepdims=True)
    return rstd * (dn - m1 - xhat * m2)


def gelu_parts(x):
    cdf = 0.5 + 0.5 * lax.erf(x * math.sqrt(0.5))
    return cdf, jnp.exp2((-0.5 * LOG2E) * (x * x))


def lane_iota(rows):
    return lax.broadcasted_iota(jnp.int32, (rows, 128), 1)


def three_parts(x):
    hi = x.astype(BF16).astype(F32)
    r = x - hi
    mid = r.astype(BF16).astype(F32)
    return hi, mid, r - mid


def spread_parts(x, lane, spare):
    hi, mid, lo = three_parts(x)
    return jnp.where(lane == spare, hi, jnp.where(lane == spare + 1, mid, jnp.where(lane == spare + 2, lo, 0.0)))


def head_pairs(seqs):
    return [(pair, s) for pair in range(2) for s in range(seqs)]


def pair_slices(pair, s):
    seq = slice(s * LEN, (s + 1) * LEN)
    return seq, [slice(part * D + pair * 128, part * D + pair * 128 + 128) for part in range(3)]


def attn_forward(qkv, p, att, lx, vt, seqs, hook=None):
    nblk = LEN // BLK
    for b in range(2):
        vt[b, 0, HD:] = jnp.ones((HD, LEN), BF16)
        vt[b, 1, :HD] = jnp.ones((HD, LEN), BF16)
    low = lane_iota(BLK) < HD
    keep = lax.broadcasted_iota(jnp.int32, (BLK, BLK), 0) <= lax.broadcasted_iota(jnp.int32, (BLK, BLK), 1)
    row = lax.broadcasted_iota(jnp.int32, (8, BLK), 0)
    works = head_pairs(seqs)

    def scores(w, j, h):
        seq, (cq, ck, _) = pair_slices(*works[w])
        r0 = seq.start
        q = qkv[p, r0 + j * BLK:r0 + (j + 1) * BLK, cq]
        zero = jnp.zeros_like(q)
        q = jnp.where(low, q, zero) if h == 0 else jnp.where(low, zero, q)
        return dot_nt(qkv[p, r0:r0 + (j + 1) * BLK, ck], q)

    units = [(w, j, h) for w in range(len(works)) for j in range(nblk) for h in range(2)]
    st = None
    outs, pieces = [], []
    for u, (w, j, h) in enumerate(units):
        seq, (cq, _, cv) = pair_slices(*works[w])
        if j == 0 and h == 0:
            if hook is not None:
                hook(w)
            v = qkv[p, seq, cv].T
            vt[w % 2, 0, :HD] = v[:HD]
            vt[w % 2, 1, HD:] = v[HD:]
        if st is None:
            st = scores(w, j, h)
        later = scores(*units[u + 1]) if u + 1 < len(units) else None
        diag = jnp.where(keep, st[j * BLK:], NEG)
        st = jnp.concatenate([st[: j * BLK], diag], axis=0) if j else diag
        top = jnp.max(st, axis=0, keepdims=True)
        pr = jnp.exp2(st - top).astype(BF16)
        ox = dot_nn(vt[w % 2, h, :, : (j + 1) * BLK], pr)
        mine, den = (ox[:HD], ox[HD:]) if h == 0 else (ox[HD:], ox[:HD])
        outs.append(mine * (1.0 / den))
        hi, mid, lo = three_parts(-(top + jnp.log(den[:8]) * LOG2E))
        pieces.append(jnp.where(row == 0, hi, jnp.where(row == 1, mid, jnp.where(row == 2, lo, 0.0))))
        if h == 1:
            rows = slice(seq.start + j * BLK, seq.start + (j + 1) * BLK)
            att[p, rows, cq] = jnp.concatenate(outs, axis=0).T.astype(BF16)
            blank = jnp.zeros((HD - 8, BLK), F32)
            lx[p, rows, cq] = jnp.concatenate([pieces[1], blank, pieces[0], blank], axis=0).T.astype(BF16)
            outs, pieces = [], []
        st = later


def attn_backward(qkv, p, att, lx, datt, vx, kx, qx, dox, dkt, dvt, dq, seqs, hook=None):
    nblk = LEN // BLK
    low = lane_iota(LEN) < HD
    lane = lane_iota(LEN)
    keep = lax.broadcasted_iota(jnp.int32, (BLK, BLK), 1) <= lax.broadcasted_iota(jnp.int32, (BLK, BLK), 0)
    one = jnp.ones((LEN, 128), BF16)
    for w, (pair, s) in enumerate(head_pairs(seqs)):
        if hook is not None:
            hook(w)
        seq, (cq, ck, cv) = pair_slices(pair, s)
        v = qkv[p, seq, cv]
        vx[0] = jnp.where(low, v, one)
        vx[1] = jnp.where(low, one, v)
        k = qkv[p, seq, ck]
        kx[0] = jnp.where(low, k, one)
        kx[1] = jnp.where(low, one, k)
        q = qkv[p, seq, cq]
        ls = lx[p, seq, cq]
        qx[0] = jnp.where(low, q, ls)
        qx[1] = jnp.where(low, ls, q)
        do = datt[seq, cq]
        dof = do.astype(F32)
        prod = dof * att[p, seq, cq].astype(F32)
        in0 = jnp.sum(jnp.where(low, prod, 0.0), axis=-1, keepdims=True)
        in1 = jnp.sum(jnp.where(low, 0.0, prod), axis=-1, keepdims=True)
        dox[0] = jnp.where(low, dof, spread_parts(jnp.broadcast_to(-in0, (LEN, 128)), lane, HD)).astype(BF16)
        dox[1] = jnp.where(low, spread_parts(jnp.broadcast_to(-in1, (LEN, 128)), lane, 0), dof).astype(BF16)
        qt = q.T
        dot = do.T

        def products(h, i):
            a = i * BLK
            return dot_nt(qx[h, a:], kx[h, a:a + BLK]), dot_nt(dox[h, a:], vx[h, a:a + BLK])

        units = [(h, i) for h in range(2) for i in range(nblk)]
        ready = products(*units[0])
        for u, (h, i) in enumerate(units):
            later = products(*units[u + 1]) if u + 1 < len(units) else None
            sc, dp = ready
            a = i * BLK
            pr = jnp.exp2(sc)
            diag = jnp.where(keep, pr[:BLK], 0.0)
            pr = jnp.concatenate([diag, pr[BLK:]], axis=0) if i < nblk - 1 else diag
            ds = (pr * dp).astype(BF16)
            prb = pr.astype(BF16)
            mine = slice(h * HD, h * HD + HD)
            dvt[mine, a:a + BLK] = dot_nn(dot[:, a:], prb)[mine]
            dkt[mine, a:a + BLK] = dot_nn(qt[:, a:], ds)[mine]
            part = dot_nn(ds, kx[h, a:a + BLK])
            if i == 0:
                dq[h] = part
            else:
                dq[h, a:] += part
            ready = later
        qkv[p, seq, cq] = (jnp.where(low, dq[0], dq[1]) * 0.125).astype(BF16)
        qkv[p, seq, ck] = (dkt[...].T * LN2).astype(BF16)
        qkv[p, seq, cv] = dvt[...].T.astype(BF16)


def digit_groups(n):
    groups = [(1, 2)]
    stride = 2
    while stride < n:
        size = min(4, n // stride)
        groups.append((stride, size))
        stride *= size
    return groups[::-1]


class Links:
    def __init__(self, n):
        self.groups = digit_groups(n)
        self.me = lax.axis_index("fsdp")
        self.digits = [(self.me // stride) % size for stride, size in self.groups]
        self.sizes = tuple(size for _, size in self.groups)

    def digit(self, g, t):
        return (self.digits[g] + t) % self.sizes[g]

    def peer(self, g, t):
        return self.me + (self.digit(g, t) - self.digits[g]) * self.groups[g][0]

    def barrier(self):
        sem = pltpu.get_barrier_semaphore()
        count = 0
        for g, size in enumerate(self.sizes):
            for t in range(1, size):
                pl.semaphore_signal(sem, inc=1, device_id=(self.peer(g, t),), device_id_type=pl.DeviceIdType.MESH)
                count += 1
        return lambda: pl.semaphore_wait(sem, count)

    def copy(self, src, dst, sems, g, t):
        return pltpu.make_async_remote_copy(
            src_ref=src,
            dst_ref=dst,
            send_sem=sems.at[0, g, t - 1],
            recv_sem=sems.at[1, g, t - 1],
            device_id=(self.peer(g, t),),
            device_id_type=pl.DeviceIdType.MESH,
        )

    def held(self, buf, g, t=0):
        tail = [self.digit(g, t)] + self.digits[g + 1:]
        return buf.at[(slice(None),) * g + tuple(tail)]

    def gather_start(self, buf, sems, g):
        for t in range(1, self.sizes[g]):
            self.copy(self.held(buf, g), self.held(buf, g), sems, g, t).start()

    def gather_wait(self, buf, sems, g):
        for t in range(1, self.sizes[g]):
            self.copy(self.held(buf, g), self.held(buf, g, -t), sems, g, t).wait_recv()
        for t in range(1, self.sizes[g]):
            self.copy(self.held(buf, g), self.held(buf, g), sems, g, t).wait_send()

    def reduce_start(self, part, got, sems, g):
        for t in range(1, self.sizes[g]):
            src = part.at[(slice(None),) * g + (self.digit(g, t),)]
            self.copy(src, got.at[t - 1], sems, g, t).start()

    def reduce_wait(self, part, got, sems, g):
        for t in range(1, self.sizes[g]):
            src = part.at[(slice(None),) * g + (self.digit(g, t),)]
            self.copy(src, got.at[t - 1], sems, g, t).wait()
        total = part[(slice(None),) * g + (self.digits[g],)].astype(F32)
        for t in range(1, self.sizes[g]):
            total = total + got[t - 1].astype(F32)
        return total

    def sum_start(self, part, got, sems, g):
        for t in range(1, self.sizes[g]):
            self.copy(part.at[g], got.at[g, t - 1], sems, g, t).start()

    def sum_wait(self, part, got, sems, g):
        for t in range(1, self.sizes[g]):
            self.copy(part.at[g], got.at[g, t - 1], sems, g, t).wait()
        total = part[g]
        for t in range(1, self.sizes[g]):
            total = total + got[g, t - 1]
        part[g + 1] = total


class Reduction:
    def __init__(self, links, first, rest, sems):
        self.links, self.parts, self.gots, self.sems = links, [first] + rest[1::2], rest[0::2], sems
        self.step = 0

    def start(self):
        g = len(self.links.sizes) - 1 - self.step
        self.links.reduce_start(self.parts[self.step], self.gots[self.step], self.sems, g)

    def take(self):
        g = len(self.links.sizes) - 1 - self.step
        total = self.links.reduce_wait(self.parts[self.step], self.gots[self.step], self.sems, g)
        self.step += 1
        return total

    def turn(self):
        total = self.take()
        self.parts[self.step][...] = total.astype(BF16)
        self.start()


def pair_rows(x, t):
    return jnp.concatenate([x[:, 256 * t : 256 * t + 128], x[:, 256 * t + 128 : 256 * t + 256]], axis=0)


ENTRY_ROWS = 64
FEED_ROWS = 144
PAIR_ROWS = 32
FEED_VECS = 16
LEAD_VECS = 8
CHUNK = 256


ROWS = 1024


def mega_kernel(*refs, names, n, tokens, comm):
    o = SimpleNamespace(**dict(zip(names, refs)))
    seqs = tokens // LEN
    chunks = [slice(c, c + CHUNK) for c in range(0, FF, CHUNK)]

    def pack_parameters():
        d = tuple(links.digits)
        x = o.entry_s[...].astype(F32)
        for t in range(3):
            o.buf1[d + (pl.ds(16 * t, 16),)] = pair_rows(x, t).astype(BF16)
        o.vec[...] = jnp.zeros_like(o.vec)
        for i, r in enumerate((o.lead_g, o.lead_s, o.mid_g, o.mid_s, o.red_b)):
            o.vec[i:i + 1, 0:8] = r[...].astype(F32).reshape(1, 8)
        o.vec[8:9, 0:32] = o.exp_b[...].astype(F32).reshape(1, 32)
        low = pltpu.roll(o.vec[0:8, :], (links.me * 8) % 128, 1)
        high = pltpu.roll(jnp.broadcast_to(o.vec[8:9, :], (8, 128)), (links.me * 32) % 128, 1)
        row = lax.broadcasted_iota(jnp.int32, (8, 128), 0)
        high = jnp.where(row == links.me // 4, high, 0.0)
        o.buf1[d + (pl.ds(48, 16),)] = jnp.concatenate([low, high], axis=0).astype(BF16)

    def pack_more_parameters():
        d = tuple(links.digits)
        o.buf2[d + (pl.ds(0, 16),)] = pair_rows(o.exit_s[...].astype(F32), 0).astype(BF16)
        x = o.expand_s[...].astype(F32)
        for t in range(4):
            o.buf2[d + (pl.ds(16 + 16 * t, 16),)] = pair_rows(x, t).astype(BF16)
        for c in range(2):
            o.buf2[d + (pl.ds(80 + 32 * c, 32),)] = o.reduce_s[:, 128 * c:128 * c + 128]

    def unpack(buf, at, count, dst):
        for t in range(count // 2):
            x = buf[:, :, :, at + 16 * t:at + 16 * t + 16, :].astype(F32).reshape(n, 16, 128)
            dst[:, 256 * t:256 * t + 128] = x[:, :8].reshape(8 * n, 128).astype(BF16)
            dst[:, 256 * t + 128:256 * t + 256] = x[:, 8:].reshape(8 * n, 128).astype(BF16)

    def unpack_first():
        unpack(o.buf1, 0, 6, o.entry_w)
        v = o.buf1[:, :, :, 48:64, :].astype(F32).reshape(n, 16, 128)
        first = jnp.sum(v[: n // 2], axis=0)
        second = jnp.sum(v[n // 2:], axis=0)
        o.vecs[0:5, 0:128] = first[0:5]
        o.vecs[0:5, 128:256] = second[0:5]
        both = (first + second)[8:16]
        for c in range(8):
            o.eb[0:1, 128 * c:128 * c + 128] = both[c:c + 1]

    def unpack_second():
        unpack(o.buf2, 0, 2, o.exit_w)
        unpack(o.buf2, 16, 8, o.expand_w)
        for c in range(2):
            x = o.buf2[:, :, :, 80 + 32 * c:112 + 32 * c, :]
            o.reduce_w[:, 128 * c:128 * c + 128] = x.reshape(32 * n, 128)

    def turn_weights():
        o.entry_t[...] = o.entry_w[...].T
        o.exit_t[...] = o.exit_w[...].T
        o.expand_t[...] = o.expand_w[...].T
        o.reduce_t[...] = o.reduce_w[...].T

    def chunk_rows(grad, c):
        return grad[:, 128 * c:128 * c + 128].reshape(n, 8, 128)

    def store_rows(part, at, top, bottom):
        x = jnp.concatenate([top, bottom], axis=1).astype(BF16)
        part[:, :, :, at:at + 16, :] = x.reshape(links.sizes + (16, 128))

    def halves(row):
        return [row[:, :128], row[:, 128:]]

    def vector_rows(part, rows, count):
        for i, r in enumerate(rows):
            part[0, i:i + 1, :] = r
        if len(rows) < count:
            part[0, len(rows):count, :] = jnp.zeros((count - len(rows), 128), F32)

    def own_eight(total, at):
        both = jnp.where(links.me >= n // 2, total[at + 1:at + 2], total[at:at + 1])
        both = pltpu.roll(jnp.broadcast_to(both, (8, 128)), (128 - (links.me * 8) % 128) % 128, 1)
        return both[0:1, 0:8].reshape(8)

    def feed_pack():
        store_rows(o.buf2, 0, chunk_rows(o.g_exit, 0), chunk_rows(o.g_exit, 1))
        for t in range(4):
            store_rows(o.buf2, 16 + 16 * t, chunk_rows(o.g_expand, 2 * t), chunk_rows(o.g_expand, 2 * t + 1))
        for c in range(2):
            x = o.g_reduce_t[128 * c:128 * c + 128, :].T.astype(BF16)
            o.buf2[:, :, :, 80 + 32 * c:112 + 32 * c, :] = x.reshape(links.sizes + (32, 128))
        rows = halves(o.g_small[2:3, :]) + halves(o.g_small[3:4, :]) + halves(o.g_small[5:6, :])
        rows += [o.g_exp_b[:, 128 * c:128 * c + 128] for c in range(8)]
        vector_rows(o.feed_vec, rows, FEED_VECS)

    def feed_end(total):
        for c in range(2):
            o.exit_o[:, 128 * c:128 * c + 128] = total[8 * c:8 * c + 8]
            o.reduce_o[:, 128 * c:128 * c + 128] = total[80 + 32 * c:112 + 32 * c]
        for c in range(8):
            o.expand_o[:, 128 * c:128 * c + 128] = total[16 + 8 * c:24 + 8 * c]

    def feed_vec_end():
        total = o.feed_vec[len(links.sizes)]
        o.mid_g_o[...] = own_eight(total, 0)
        o.mid_s_o[...] = own_eight(total, 2)
        o.red_b_o[...] = own_eight(total, 4)
        row = lax.broadcasted_iota(jnp.int32, (8, 128), 0)
        x = jnp.sum(jnp.where(row == links.me // 4, total[6:14], 0.0), axis=0, keepdims=True)
        x = pltpu.roll(jnp.broadcast_to(x, (8, 128)), (128 - (links.me * 32) % 128) % 128, 1)
        o.exp_b_o[...] = x[0:1, 0:32].reshape(32)

    def pair_grad(pair, n1):
        cols = [slice(part * D + pair * 128, part * D + pair * 128 + 128) for part in range(3)]
        q, k, v = ((o.g_entry[:, c] + dot_tn(n1, o.qkv[0, :, c])).reshape(n, 8, 128) for c in cols)
        store_rows(o.buf1, PAIR_ROWS * pair, q, k)
        store_rows(o.buf1, PAIR_ROWS * pair + 16, v, jnp.zeros_like(v))

    def pair_end(pair, total):
        for part in range(3):
            at = part * D + pair * 128
            o.entry_o[:, at:at + 128] = total[8 * part:8 * part + 8]

    def lead_vec_end():
        total = o.lead_vec[len(links.sizes)]
        o.lead_g_o[...] = own_eight(total, 0)
        o.lead_s_o[...] = own_eight(total, 2)

    row_parts = [slice(r, r + ROWS) for r in range(0, tokens, ROWS)]
    every = slice(0, tokens)

    def mixed(p, rows=every):
        if p == 1:
            return o.total[rows]
        return o.state_in[rows].astype(F32) + o.embed_in[rows].astype(F32)

    def lead_normed(xhat):
        return (xhat * o.vecs[0:1, :] + o.vecs[1:2, :]).astype(BF16)

    def middle_normed(xhat):
        return (xhat * o.vecs[2:3, :] + o.vecs[3:4, :]).astype(BF16)

    def enter(p):
        if p == 1:
            o.total[...] = o.grad[...] + o.embed_in[...].astype(F32)
        xhat, _ = norm_parts(mixed(p))
        n1 = lead_normed(xhat)
        for i in range(3):
            y = dot_nn(n1, o.entry_w[:, i * D:(i + 1) * D])
            o.qkv[p, :, i * D:(i + 1) * D] = (y * (LOG2E * 0.125) if i == 0 else y).astype(BF16)

    def forward_chunk(n2, c):
        hid = dot_nn(n2, o.expand_w[:, c]) + o.eb[:, c]
        cdf, e = gelu_parts(hid)
        return (hid * cdf).astype(BF16), cdf + hid * (e * INV_SQRT_2PI)

    def backward_chunk(d_out, n2, act, gp, c, first):
        reduce_g = dot_tn(d_out, act)
        dh = dot_nn(d_out, o.reduce_t[:, c]) * gp
        bias_g = jnp.sum(dh, axis=0, keepdims=True)
        dh = dh.astype(BF16)
        expand_g = dot_tn(n2, dh)
        if first:
            o.g_reduce_t[:, c], o.g_exp_b[:, c], o.g_expand[:, c] = reduce_g, bias_g, expand_g
        else:
            o.g_reduce_t[:, c] += reduce_g
            o.g_exp_b[:, c] += bias_g
            o.g_expand[:, c] += expand_g
        return dot_nn(dh, o.expand_t[c, :])

    def add_small(at, row, first):
        if first:
            o.g_small[at:at + 1, :] = row
        else:
            o.g_small[at:at + 1, :] += row

    def feed_finish(p, rows, g, dn, xhat, rstd, first):
        add_small(5, jnp.sum(g, axis=0, keepdims=True), first)
        add_small(2, jnp.sum(dn * xhat, axis=0, keepdims=True), first)
        add_small(3, jnp.sum(dn, axis=0, keepdims=True), first)
        dm = g + norm_pull(xhat, rstd, o.vecs[2:3, :], dn)
        o.grad[rows] = dm
        db = dm.astype(BF16)
        exit_g = dot_tn(o.att[p, rows], db)
        o.g_exit[...] = exit_g if first else o.g_exit[...] + exit_g
        o.grad_in[rows] = dot_nn(db, o.exit_t[...]).astype(BF16)

    def feed_first(rows):
        mid = mixed(0, rows) + dot_nn(o.att[0, rows], o.exit_w[...])
        o.middle[rows] = mid
        n2 = middle_normed(norm_parts(mid)[0])
        res = mid + o.vecs[4:5, :]
        for c in chunks:
            act, gp = forward_chunk(n2, c)
            o.active[rows, c] = act
            o.gelup[rows, c] = gp.astype(BF16)
            res = res + dot_nn(act, o.reduce_w[c, :])
        o.grad[rows] = res

    def feed_last(rows):
        first = rows.start == 0
        mid = mixed(1, rows) + dot_nn(o.att[1, rows], o.exit_w[...])
        o.grad[rows] = mid
        n2 = middle_normed(norm_parts(mid)[0])
        res = mid + o.vecs[4:5, :]
        d_out = o.grad_in[rows]
        dn = None
        for c in chunks:
            act, gp = forward_chunk(n2, c)
            res = res + dot_nn(act, o.reduce_w[c, :])
            part = backward_chunk(d_out, n2, act, gp, c, first)
            dn = part if dn is None else dn + part
        o.final[rows] = res.astype(BF16)
        xhat, rstd = norm_parts(o.grad[rows])
        feed_finish(1, rows, o.grad_in[rows].astype(F32), dn, xhat, rstd, first)

    def feed_back(rows):
        n2 = middle_normed(norm_parts(o.middle[rows])[0])
        d_out = o.grad[rows].astype(BF16)
        dn = None
        for c in chunks:
            part = backward_chunk(d_out, n2, o.active[rows, c], o.gelup[rows, c].astype(F32), c, False)
            dn = part if dn is None else dn + part
        xhat, rstd = norm_parts(o.middle[rows])
        feed_finish(0, rows, o.grad[rows], dn, xhat, rstd, False)

    def by_rows(phase):
        for rows in row_parts:
            phase(rows)

    def leave(p, with_entry):
        if with_entry:
            entry_g = dot_tn(lead_normed(norm_parts(mixed(p))[0]), o.qkv[p])
            o.g_entry[...] = entry_g if p == 1 else o.g_entry[...] + entry_g
        dn = dot_nn(o.qkv[p], o.entry_t[...])
        xhat, rstd = norm_parts(mixed(p))
        add_small(0, jnp.sum(dn * xhat, axis=0, keepdims=True), p == 1)
        add_small(1, jnp.sum(dn, axis=0, keepdims=True), p == 1)
        g = o.grad[...] + norm_pull(xhat, rstd, o.vecs[0:1, :], dn)
        o.grad[...] = g
        o.total[...] = g if p == 1 else o.total[...] + g

    def forward(p, hook=None):
        pl.run_scoped(lambda vt: attn_forward(o.qkv, p, o.att, o.lx, vt, seqs, hook), pltpu.VMEM((2, 2, 128, LEN), BF16))

    def backward(p, hook=None):
        head = [pltpu.VMEM((2, LEN, 128), BF16)] * 4 + [pltpu.VMEM((128, LEN), F32)] * 2 + [pltpu.VMEM((2, LEN, 128), F32)]
        pl.run_scoped(lambda *bufs: attn_backward(o.qkv, p, o.att, o.lx, o.grad_in, *bufs, seqs, hook), *head)

    if not comm:
        for i, r in enumerate((o.lead_g, o.lead_s, o.mid_g, o.mid_s, o.red_b)):
            o.vecs[i:i + 1, :] = r[...].astype(F32)
        o.eb[...] = o.exp_b[...].astype(F32)
        o.grad_in[...] = o.grad_h[...]
        turn_weights()
        enter(0)
        forward(0)
        by_rows(feed_first)
        enter(1)
        forward(1)
        by_rows(feed_last)
        backward(1)
        leave(1, True)
        by_rows(feed_back)
        backward(0)
        leave(0, True)
        o.g_reduce[...] = o.g_reduce_t[...].T
        for i in range(4):
            o.g_small[8 + i:9 + i, :] = o.g_exp_b[:, i * D:(i + 1) * D]
        return

    links = Links(n)
    last = len(links.sizes) - 1
    arrived = links.barrier()
    loads = [
        pltpu.make_async_copy(src, dst, o.load_sem.at[i])
        for i, (src, dst) in enumerate(((o.state_h, o.state_in), (o.embed_h, o.embed_in), (o.grad_h, o.grad_in)))
    ]
    for load in loads:
        load.start()
    pack_parameters()
    arrived()
    links.gather_start(o.buf1, o.sem1, 0)
    pack_more_parameters()
    links.gather_wait(o.buf1, o.sem1, 0)
    links.gather_start(o.buf1, o.sem1, 1)
    links.gather_start(o.buf2, o.sem2, 0)
    for load in loads:
        load.wait()
    links.gather_wait(o.buf1, o.sem1, 1)
    links.gather_start(o.buf1, o.sem1, 2)
    links.gather_wait(o.buf2, o.sem2, 0)
    links.gather_start(o.buf2, o.sem2, 1)
    links.gather_wait(o.buf1, o.sem1, 2)
    unpack_first()
    enter(0)

    def gather_more(w):
        if w == seqs:
            links.gather_wait(o.buf2, o.sem2, 1)
            links.gather_start(o.buf2, o.sem2, 2)

    forward(0, gather_more)
    links.gather_wait(o.buf2, o.sem2, 2)
    unpack_second()
    turn_weights()
    by_rows(feed_first)
    enter(1)
    forward(1)
    by_rows(feed_last)
    backward(1)
    leave(1, True)
    by_rows(feed_back)

    feed = Reduction(links, o.buf2, [o.feed_got0, o.feed_part1, o.feed_got1, o.feed_part2, o.feed_got2], o.sem3)
    first = Reduction(links, o.buf1.at[:, :, :, pl.ds(0, PAIR_ROWS), :], [o.pair0_got0, o.pair0_part1, o.pair0_got1, o.pair0_part2, o.pair0_got2], o.sem4)
    second = Reduction(links, o.buf1.at[:, :, :, pl.ds(PAIR_ROWS, PAIR_ROWS), :], [o.pair1_got0, o.pair1_part1, o.pair1_got1, o.pair1_part2, o.pair1_got2], o.sem5)
    feed_vec = (o.feed_vec, o.feed_vec_got, o.sem6)
    lead_vec = (o.lead_vec, o.lead_vec_got, o.sem7)
    feed_pack()
    feed.start()
    links.sum_start(*feed_vec, 0)

    def reduce_more(w):
        if w == 1:
            feed.turn()
            links.sum_wait(*feed_vec, 0)
            links.sum_start(*feed_vec, 1)
        if w == seqs:
            o.att[1] = lead_normed(norm_parts(mixed(0))[0])
            pair_grad(0, o.att[1])
            first.start()
        if w == 2 * seqs - 1:
            feed.turn()
            first.turn()
            links.sum_wait(*feed_vec, 1)
            links.sum_start(*feed_vec, 2)

    backward(0, reduce_more)
    pair_grad(1, o.att[1])
    second.start()
    first.turn()
    leave(0, False)
    vector_rows(o.lead_vec, halves(o.g_small[0:1, :]) + halves(o.g_small[1:2, :]), LEAD_VECS)
    links.sum_start(*lead_vec, 0)
    second.turn()
    feed_end(feed.take())
    links.sum_wait(*feed_vec, 2)
    feed_vec_end()
    links.sum_wait(*lead_vec, 0)
    links.sum_start(*lead_vec, 1)
    second.turn()
    pair_end(0, first.take())
    links.sum_wait(*lead_vec, 1)
    links.sum_start(*lead_vec, 2)
    pair_end(1, second.take())
    links.sum_wait(*lead_vec, 2)
    lead_vec_end()


VECTOR_INPUTS = ("lead_g", "lead_s", "mid_g", "mid_s", "red_b", "exp_b")


def mega(n, tokens, comm):
    T = tokens
    vmem = pltpu.VMEM
    outs = [("final", (T, D), BF16), ("grad", (T, D), F32), ("total", (T, D), F32)]
    scratch = [
        ("qkv", vmem((2, T, 3 * D), BF16)), ("att", vmem((2, T, D), BF16)), ("lx", vmem((2, T, D), BF16)),
        ("middle", vmem((T, D), F32)), ("active", vmem((T, FF), BF16)), ("gelup", vmem((T, FF), BF16)),
        ("entry_t", vmem((3 * D, D), BF16)), ("exit_t", vmem((D, D), BF16)), ("expand_t", vmem((FF, D), BF16)), ("reduce_t", vmem((D, FF), BF16)),
        ("vecs", vmem((8, D), F32)), ("eb", vmem((1, FF), F32)),
        ("g_reduce_t", vmem((D, FF), F32)), ("g_exp_b", vmem((1, FF), F32)),
    ]
    grads = [("g_entry", (D, 3 * D)), ("g_exit", (D, D)), ("g_expand", (D, FF)), ("g_small", (16, D))]
    weights = [("entry_w", (D, 3 * D)), ("exit_w", (D, D)), ("expand_w", (D, FF)), ("reduce_w", (FF, D))]
    in_vmem, in_hbm = pl.BlockSpec(memory_space=pltpu.VMEM), pl.BlockSpec(memory_space=pl.ANY)
    if comm:
        ins = ("state_h", "embed_h", "grad_h", "entry_s", "exit_s", "expand_s", "reduce_s") + VECTOR_INPUTS
        in_specs = [in_hbm] * 3 + [in_vmem] * 10
        r, rr = D // n, FF // n
        outs += [
            ("entry_o", (r, 3 * D), F32), ("exit_o", (r, D), F32), ("lead_g_o", (r,), F32), ("lead_s_o", (r,), F32),
            ("expand_o", (r, FF), F32), ("reduce_o", (rr, D), F32), ("mid_g_o", (r,), F32), ("mid_s_o", (r,), F32),
            ("exp_b_o", (rr,), F32), ("red_b_o", (r,), F32),
        ]
        scratch += [(name, vmem((T, D), BF16)) for name in ("state_in", "embed_in", "grad_in")]
        scratch += [(name, vmem(shape, F32)) for name, shape in grads] + [(name, vmem(shape, BF16)) for name, shape in weights]
        s = tuple(size for _, size in digit_groups(n))
        scratch += [("vec", vmem((16, 128), F32))]
        scratch += [("buf1", vmem(s + (ENTRY_ROWS, 128), BF16)), ("buf2", vmem(s + (FEED_ROWS, 128), BF16))]
        for name, rows in (("pair0", PAIR_ROWS), ("pair1", PAIR_ROWS), ("feed", FEED_ROWS)):
            for step, g in enumerate((2, 1, 0)):
                scratch.append((f"{name}_got{step}", vmem((s[g] - 1,) + s[:g] + (rows, 128), BF16)))
                if g < 2:
                    scratch.append((f"{name}_part{step}", vmem(s[: g + 1] + (rows, 128), BF16)))
        for name, rows in (("feed_vec", FEED_VECS), ("lead_vec", LEAD_VECS)):
            scratch += [(name, vmem((len(s) + 1, rows, 128), F32)), (f"{name}_got", vmem((len(s), 3, rows, 128), F32))]
        scratch += [(f"sem{i}", pltpu.SemaphoreType.DMA((2, 3, 3))) for i in range(1, 8)] + [("load_sem", pltpu.SemaphoreType.DMA((3,)))]
        out_shape = [vmem(shape, dtype) for _, shape, dtype in outs]
        params = dict(vmem_limit_bytes=58 * 1024 * 1024, collective_id=0, has_side_effects=True)
    else:
        ins = ("state_in", "embed_in", "grad_h") + tuple(name for name, _ in weights) + VECTOR_INPUTS
        in_specs = [in_vmem] * len(ins)
        outs += [(name, shape, F32) for name, shape in grads] + [("g_reduce", (FF, D), F32)]
        out_shape = [jax.ShapeDtypeStruct(shape, dtype) for _, shape, dtype in outs]
        scratch += [("grad_in", vmem((T, D), BF16))]
        params = dict(vmem_limit_bytes=63 * 1024 * 1024)
    names = ins + tuple(out[0] for out in outs) + tuple(name for name, _ in scratch)
    return pl.pallas_call(
        functools.partial(mega_kernel, names=names, n=n, tokens=T, comm=comm),
        in_specs=in_specs,
        out_specs=[in_vmem] * len(outs),
        out_shape=out_shape,
        scratch_shapes=[shape for _, shape in scratch],
        compiler_params=pltpu.CompilerParams(**params),
        name="block",
    )


def drain_kernel(*refs):
    count = len(refs) // 2
    sems = refs[-1]
    copies = [pltpu.make_async_copy(refs[i], refs[count + i], sems.at[i]) for i in range(count)]
    for copy in copies:
        copy.start()
    for copy in copies:
        copy.wait()


def drain(*arrays):
    count = len(arrays)
    return pl.pallas_call(
        drain_kernel,
        in_specs=[pl.BlockSpec(memory_space=pltpu.VMEM)] * count,
        out_specs=[pl.BlockSpec(memory_space=pl.ANY)] * count,
        out_shape=[jax.ShapeDtypeStruct(a.shape, a.dtype) for a in arrays],
        scratch_shapes=[pltpu.SemaphoreType.DMA((count,))],
        compiler_params=pltpu.CompilerParams(vmem_limit_bytes=1024 * 1024),
        name="drain",
    )(*arrays)


def on_device(loop_state, embedding, output_grad, entry_weight, exit_weight, lead_gain, lead_shift, expand_weight, reduce_weight, middle_gain, middle_shift, expand_bias, reduce_bias):
    n = lax.axis_size("fsdp")
    tokens = loop_state.shape[0]
    vectors = (lead_gain, lead_shift, middle_gain, middle_shift, reduce_bias, expand_bias)
    weights = (entry_weight, exit_weight, expand_weight, reduce_weight)
    if entry_weight.shape[0] == 8 and len(digit_groups(n)) == 3:
        return tuple(drain(*mega(n, tokens, True)(loop_state, embedding, output_grad, *weights, *vectors)))
    shards = weights + vectors
    packed = jnp.concatenate([a.reshape(-1) for a in shards])
    whole = lax.all_gather(packed, "fsdp", axis=0)
    full, at = [], 0
    for a in shards:
        whole_a = whole[:, at : at + a.size].reshape((n * a.shape[0],) + a.shape[1:])
        full.append(whole_a if a.ndim == 2 else whole_a.reshape(1, -1))
        at += a.size
    final, grad, total, g_entry, g_exit, g_expand, small, g_reduce = mega(n, tokens, False)(loop_state, embedding, output_grad, *full)
    terms = (g_entry, g_exit, small[0], small[1], g_expand, g_reduce, small[2], small[3], small[8:12].reshape(-1), small[5])
    sums = lax.psum_scatter(jnp.concatenate([a.reshape(n, -1) for a in terms], axis=1), "fsdp", scatter_dimension=0, tiled=True)[0]
    outs, at = [], 0
    for a in terms:
        size = a.size // n
        outs.append(sums[at : at + size].reshape((a.shape[0] // n,) + a.shape[1:]))
        at += size
    return (final, grad, total, *outs)


def solution(mesh):
    two, one = P("fsdp", None), P("fsdp")
    in_specs = (two, two, two, two, two, one, one, two, two, one, one, one, one)
    out_specs = (two, two, two, two, two, one, one, two, two, one, one, one, one)
    return jax.shard_map(on_device, mesh=mesh, in_specs=in_specs, out_specs=out_specs, check_vma=False)
```

```python
import functools
import math
from types import SimpleNamespace

import jax
import jax.numpy as jnp
from jax import lax
from jax.experimental import pallas as pl
from jax.experimental.pallas import tpu as pltpu
from jax.sharding import PartitionSpec as P

F32, BF16 = jnp.float32, jnp.bfloat16
LEN = 1024
LOOPS = 2
EPS = 1e-05
D = 256
FF = 1024
HD = 64
BLK = 256
LOG2E = 1.4426950408889634
LN2 = 0.6931471805599453
INV_SQRT_2PI = 1.0 / math.sqrt(2.0 * math.pi)
NEG = -1e30


def dot_nn(a, b):
    return lax.dot_general(a, b, (((1,), (0,)), ((), ())), preferred_element_type=F32)


def dot_nt(a, b):
    return lax.dot_general(a, b, (((1,), (1,)), ((), ())), preferred_element_type=F32)


def dot_tn(a, b):
    return lax.dot_general(a, b, (((0,), (0,)), ((), ())), preferred_element_type=F32)


def norm_parts(x):
    mean = jnp.mean(x, axis=-1, keepdims=True)
    center = x - mean
    var = jnp.mean(center * center, axis=-1, keepdims=True)
    rstd = lax.rsqrt(var + EPS)
    return center * rstd, rstd


def norm_pull(xhat, rstd, gain, dy):
    dn = dy * gain
    m1 = jnp.mean(dn, axis=-1, keepdims=True)
    m2 = jnp.mean(dn * xhat, axis=-1, keepdims=True)
    return rstd * (dn - m1 - xhat * m2)


def gelu_parts(x):
    cdf = 0.5 + 0.5 * lax.erf(x * math.sqrt(0.5))
    return cdf, jnp.exp2((-0.5 * LOG2E) * (x * x))


def lane_iota(rows):
    return lax.broadcasted_iota(jnp.int32, (rows, 128), 1)


def three_parts(x):
    hi = x.astype(BF16).astype(F32)
    r = x - hi
    mid = r.astype(BF16).astype(F32)
    return hi, mid, r - mid


def spread_parts(x, lane, spare):
    hi, mid, lo = three_parts(x)
    return jnp.where(lane == spare, hi, jnp.where(lane == spare + 1, mid, jnp.where(lane == spare + 2, lo, 0.0)))


def head_pairs(seqs):
    return [(pair, s) for pair in range(2) for s in range(seqs)]


def pair_slices(pair, s):
    seq = slice(s * LEN, (s + 1) * LEN)
    return seq, [slice(part * D + pair * 128, part * D + pair * 128 + 128) for part in range(3)]


def attn_forward(qkv, p, att, lx, vt, seqs, hook=None):
    nblk = LEN // BLK
    for b in range(2):
        vt[b, 0, HD:] = jnp.ones((HD, LEN), BF16)
        vt[b, 1, :HD] = jnp.ones((HD, LEN), BF16)
    low = lane_iota(BLK) < HD
    keep = lax.broadcasted_iota(jnp.int32, (BLK, BLK), 0) <= lax.broadcasted_iota(jnp.int32, (BLK, BLK), 1)
    row = lax.broadcasted_iota(jnp.int32, (8, BLK), 0)
    works = head_pairs(seqs)

    def scores(w, j, h):
        seq, (cq, ck, _) = pair_slices(*works[w])
        r0 = seq.start
        q = qkv[p, r0 + j * BLK:r0 + (j + 1) * BLK, cq]
        zero = jnp.zeros_like(q)
        q = jnp.where(low, q, zero) if h == 0 else jnp.where(low, zero, q)
        return dot_nt(qkv[p, r0:r0 + (j + 1) * BLK, ck], q)

    units = [(w, j, h) for w in range(len(works)) for j in range(nblk) for h in range(2)]
    st = None
    outs, pieces = [], []
    for u, (w, j, h) in enumerate(units):
        seq, (cq, _, cv) = pair_slices(*works[w])
        if j == 0 and h == 0:
            if hook is not None:
                hook(w)
            v = qkv[p, seq, cv].T
            vt[w % 2, 0, :HD] = v[:HD]
            vt[w % 2, 1, HD:] = v[HD:]
        if st is None:
            st = scores(w, j, h)
        later = scores(*units[u + 1]) if u + 1 < len(units) else None
        diag = jnp.where(keep, st[j * BLK:], NEG)
        st = jnp.concatenate([st[: j * BLK], diag], axis=0) if j else diag
        top = jnp.max(st, axis=0, keepdims=True)
        pr = jnp.exp2(st - top).astype(BF16)
        ox = dot_nn(vt[w % 2, h, :, : (j + 1) * BLK], pr)
        mine, den = (ox[:HD], ox[HD:]) if h == 0 else (ox[HD:], ox[:HD])
        outs.append(mine * (1.0 / den))
        hi, mid, lo = three_parts(-(top + jnp.log(den[:8]) * LOG2E))
        pieces.append(jnp.where(row == 0, hi, jnp.where(row == 1, mid, jnp.where(row == 2, lo, 0.0))))
        if h == 1:
            rows = slice(seq.start + j * BLK, seq.start + (j + 1) * BLK)
            att[p, rows, cq] = jnp.concatenate(outs, axis=0).T.astype(BF16)
            blank = jnp.zeros((HD - 8, BLK), F32)
            lx[p, rows, cq] = jnp.concatenate([pieces[1], blank, pieces[0], blank], axis=0).T.astype(BF16)
            outs, pieces = [], []
        st = later


def attn_backward(qkv, p, att, lx, datt, vx, kx, qx, dox, dkt, dvt, dq, seqs, hook):
    nblk = LEN // BLK
    low = lane_iota(LEN) < HD
    lane = lane_iota(LEN)
    keep = lax.broadcasted_iota(jnp.int32, (BLK, BLK), 1) <= lax.broadcasted_iota(jnp.int32, (BLK, BLK), 0)
    one = jnp.ones((LEN, 128), BF16)

    def work(pair, s):
        hook(pair, s)
        seq = pl.ds(pl.multiple_of(s * LEN, LEN), LEN)
        cq, ck, cv = (pl.ds(pl.multiple_of(part * D + pair * 128, 128), 128) for part in range(3))
        v = qkv[p, seq, cv]
        vx[0] = jnp.where(low, v, one)
        vx[1] = jnp.where(low, one, v)
        k = qkv[p, seq, ck]
        kx[0] = jnp.where(low, k, one)
        kx[1] = jnp.where(low, one, k)
        q = qkv[p, seq, cq]
        ls = lx[p, seq, cq]
        qx[0] = jnp.where(low, q, ls)
        qx[1] = jnp.where(low, ls, q)
        do = datt[seq, cq]
        dof = do.astype(F32)
        prod = dof * att[p, seq, cq].astype(F32)
        in0 = jnp.sum(jnp.where(low, prod, 0.0), axis=-1, keepdims=True)
        in1 = jnp.sum(jnp.where(low, 0.0, prod), axis=-1, keepdims=True)
        dox[0] = jnp.where(low, dof, spread_parts(jnp.broadcast_to(-in0, (LEN, 128)), lane, HD)).astype(BF16)
        dox[1] = jnp.where(low, spread_parts(jnp.broadcast_to(-in1, (LEN, 128)), lane, 0), dof).astype(BF16)
        qt = q.T
        dot = do.T

        def products(h, i):
            a = i * BLK
            return dot_nt(qx[h, a:], kx[h, a:a + BLK]), dot_nt(dox[h, a:], vx[h, a:a + BLK])

        units = [(h, i) for h in range(2) for i in range(nblk)]
        ready = products(*units[0])
        for u, (h, i) in enumerate(units):
            later = products(*units[u + 1]) if u + 1 < len(units) else None
            sc, dp = ready
            a = i * BLK
            pr = jnp.exp2(sc)
            diag = jnp.where(keep, pr[:BLK], 0.0)
            pr = jnp.concatenate([diag, pr[BLK:]], axis=0) if i < nblk - 1 else diag
            ds = (pr * dp).astype(BF16)
            prb = pr.astype(BF16)
            mine = slice(h * HD, h * HD + HD)
            dvt[mine, a:a + BLK] = dot_nn(dot[:, a:], prb)[mine]
            dkt[mine, a:a + BLK] = dot_nn(qt[:, a:], ds)[mine]
            part = dot_nn(ds, kx[h, a:a + BLK])
            if i == 0:
                dq[h] = part
            else:
                dq[h, a:] += part
            ready = later
        qkv[p, seq, cq] = (jnp.where(low, dq[0], dq[1]) * 0.125).astype(BF16)
        qkv[p, seq, ck] = (dkt[...].T * LN2).astype(BF16)
        qkv[p, seq, cv] = dvt[...].T.astype(BF16)

    def step(w, carry):
        work(w // seqs, w % seqs)
        return carry

    lax.fori_loop(0, 2 * seqs, step, 0)


def digit_groups(n):
    groups = [(1, 2)]
    stride = 2
    while stride < n:
        size = min(4, n // stride)
        groups.append((stride, size))
        stride *= size
    return groups[::-1]


class Links:
    def __init__(self, n):
        self.groups = digit_groups(n)
        self.me = lax.axis_index("fsdp")
        self.digits = [(self.me // stride) % size for stride, size in self.groups]
        self.sizes = tuple(size for _, size in self.groups)

    def digit(self, g, t):
        return (self.digits[g] + t) % self.sizes[g]

    def peer(self, g, t):
        return self.me + (self.digit(g, t) - self.digits[g]) * self.groups[g][0]

    def barrier(self):
        sem = pltpu.get_barrier_semaphore()
        count = 0
        for g, size in enumerate(self.sizes):
            for t in range(1, size):
                pl.semaphore_signal(sem, inc=1, device_id=(self.peer(g, t),), device_id_type=pl.DeviceIdType.MESH)
                count += 1
        return lambda: pl.semaphore_wait(sem, count)

    def copy(self, src, dst, sems, g, t):
        return pltpu.make_async_remote_copy(
            src_ref=src,
            dst_ref=dst,
            send_sem=sems.at[0, g, t - 1],
            recv_sem=sems.at[1, g, t - 1],
            device_id=(self.peer(g, t),),
            device_id_type=pl.DeviceIdType.MESH,
        )

    def held(self, buf, g, t=0):
        tail = [self.digit(g, t)] + self.digits[g + 1:]
        return buf.at[(slice(None),) * g + tuple(tail)]

    def gather_start(self, buf, sems, g):
        for t in range(1, self.sizes[g]):
            self.copy(self.held(buf, g), self.held(buf, g), sems, g, t).start()

    def gather_wait(self, buf, sems, g):
        for t in range(1, self.sizes[g]):
            self.copy(self.held(buf, g), self.held(buf, g, -t), sems, g, t).wait_recv()
        for t in range(1, self.sizes[g]):
            self.copy(self.held(buf, g), self.held(buf, g), sems, g, t).wait_send()

    def reduce_start(self, part, got, sems, g):
        for t in range(1, self.sizes[g]):
            src = part.at[(slice(None),) * g + (self.digit(g, t),)]
            self.copy(src, got.at[t - 1], sems, g, t).start()

    def reduce_wait(self, part, got, sems, g):
        for t in range(1, self.sizes[g]):
            src = part.at[(slice(None),) * g + (self.digit(g, t),)]
            self.copy(src, got.at[t - 1], sems, g, t).wait()
        total = part[(slice(None),) * g + (self.digits[g],)].astype(F32)
        for t in range(1, self.sizes[g]):
            total = total + got[t - 1].astype(F32)
        return total

    def sum_start(self, part, got, sems, g):
        for t in range(1, self.sizes[g]):
            self.copy(part.at[g], got.at[g, t - 1], sems, g, t).start()

    def sum_wait(self, part, got, sems, g):
        for t in range(1, self.sizes[g]):
            self.copy(part.at[g], got.at[g, t - 1], sems, g, t).wait()
        total = part[g]
        for t in range(1, self.sizes[g]):
            total = total + got[g, t - 1]
        part[g + 1] = total


class Reduction:
    def __init__(self, links, first, rest, sems):
        self.links, self.parts, self.gots, self.sems = links, [first] + rest[1::2], rest[0::2], sems

    def start(self, step):
        self.links.reduce_start(self.parts[step], self.gots[step], self.sems, len(self.links.sizes) - 1 - step)

    def take(self, step):
        return self.links.reduce_wait(self.parts[step], self.gots[step], self.sems, len(self.links.sizes) - 1 - step)

    def turn(self, step):
        total = self.take(step)
        self.parts[step + 1][...] = total.astype(BF16)
        self.start(step + 1)


def pair_rows(x, t):
    return jnp.concatenate([x[:, 256 * t : 256 * t + 128], x[:, 256 * t + 128 : 256 * t + 256]], axis=0)


ENTRY_ROWS = 64
FEED_ROWS = 144
PAIR_ROWS = 32
FEED_VECS = 16
LEAD_VECS = 8
CHUNK = 256


ROWS = 1024


def mega_kernel(*refs, names, n, tokens, comm):
    o = SimpleNamespace(**dict(zip(names, refs)))
    seqs = tokens // LEN
    chunks = [slice(c, c + CHUNK) for c in range(0, FF, CHUNK)]

    def pack_parameters():
        d = tuple(links.digits)
        x = o.entry_s[...].astype(F32)
        for t in range(3):
            o.buf1[d + (pl.ds(16 * t, 16),)] = pair_rows(x, t).astype(BF16)
        o.vec[...] = jnp.zeros_like(o.vec)
        for i, r in enumerate((o.lead_g, o.lead_s, o.mid_g, o.mid_s, o.red_b)):
            o.vec[i:i + 1, 0:8] = r[...].astype(F32).reshape(1, 8)
        o.vec[8:9, 0:32] = o.exp_b[...].astype(F32).reshape(1, 32)
        low = pltpu.roll(o.vec[0:8, :], (links.me * 8) % 128, 1)
        high = pltpu.roll(jnp.broadcast_to(o.vec[8:9, :], (8, 128)), (links.me * 32) % 128, 1)
        row = lax.broadcasted_iota(jnp.int32, (8, 128), 0)
        high = jnp.where(row == links.me // 4, high, 0.0)
        o.buf1[d + (pl.ds(48, 16),)] = jnp.concatenate([low, high], axis=0).astype(BF16)

    def pack_more_parameters():
        d = tuple(links.digits)
        o.buf2[d + (pl.ds(0, 16),)] = pair_rows(o.exit_s[...].astype(F32), 0).astype(BF16)
        x = o.expand_s[...].astype(F32)
        for t in range(4):
            o.buf2[d + (pl.ds(16 + 16 * t, 16),)] = pair_rows(x, t).astype(BF16)
        for c in range(2):
            o.buf2[d + (pl.ds(80 + 32 * c, 32),)] = o.reduce_s[:, 128 * c:128 * c + 128]

    def unpack(buf, at, count, dst):
        for t in range(count // 2):
            x = buf[:, :, :, at + 16 * t:at + 16 * t + 16, :].astype(F32).reshape(n, 16, 128)
            dst[:, 256 * t:256 * t + 128] = x[:, :8].reshape(8 * n, 128).astype(BF16)
            dst[:, 256 * t + 128:256 * t + 256] = x[:, 8:].reshape(8 * n, 128).astype(BF16)

    def unpack_first():
        unpack(o.buf1, 0, 6, o.entry_w)
        v = o.buf1[:, :, :, 48:64, :].astype(F32).reshape(n, 16, 128)
        first = jnp.sum(v[: n // 2], axis=0)
        second = jnp.sum(v[n // 2:], axis=0)
        o.vecs[0:5, 0:128] = first[0:5]
        o.vecs[0:5, 128:256] = second[0:5]
        both = (first + second)[8:16]
        for c in range(8):
            o.eb[0:1, 128 * c:128 * c + 128] = both[c:c + 1]

    def unpack_second():
        unpack(o.buf2, 0, 2, o.exit_w)
        unpack(o.buf2, 16, 8, o.expand_w)
        for c in range(2):
            x = o.buf2[:, :, :, 80 + 32 * c:112 + 32 * c, :]
            o.reduce_w[:, 128 * c:128 * c + 128] = x.reshape(32 * n, 128)

    def turn_weights():
        o.entry_t[...] = o.entry_w[...].T
        o.exit_t[...] = o.exit_w[...].T
        o.expand_t[...] = o.expand_w[...].T
        o.reduce_t[...] = o.reduce_w[...].T

    def chunk_rows(grad, c):
        return grad[:, 128 * c:128 * c + 128].reshape(n, 8, 128)

    def store_rows(part, at, top, bottom):
        x = jnp.concatenate([top, bottom], axis=1).astype(BF16)
        part[:, :, :, at:at + 16, :] = x.reshape(links.sizes + (16, 128))

    def halves(row):
        return [row[:, :128], row[:, 128:]]

    def vector_rows(part, rows, count):
        for i, r in enumerate(rows):
            part[0, i:i + 1, :] = r
        if len(rows) < count:
            part[0, len(rows):count, :] = jnp.zeros((count - len(rows), 128), F32)

    def own_eight(total, at):
        both = jnp.where(links.me >= n // 2, total[at + 1:at + 2], total[at:at + 1])
        both = pltpu.roll(jnp.broadcast_to(both, (8, 128)), (128 - (links.me * 8) % 128) % 128, 1)
        return both[0:1, 0:8].reshape(8)

    def feed_pack():
        store_rows(o.buf2, 0, chunk_rows(o.g_exit, 0), chunk_rows(o.g_exit, 1))
        for t in range(4):
            store_rows(o.buf2, 16 + 16 * t, chunk_rows(o.g_expand, 2 * t), chunk_rows(o.g_expand, 2 * t + 1))
        for c in range(2):
            x = o.g_reduce_t[128 * c:128 * c + 128, :].T.astype(BF16)
            o.buf2[:, :, :, 80 + 32 * c:112 + 32 * c, :] = x.reshape(links.sizes + (32, 128))
        rows = halves(o.g_small[2:3, :]) + halves(o.g_small[3:4, :]) + halves(o.g_small[5:6, :])
        rows += [o.g_exp_b[:, 128 * c:128 * c + 128] for c in range(8)]
        vector_rows(o.feed_vec, rows, FEED_VECS)

    def feed_end(total):
        for c in range(2):
            o.exit_o[:, 128 * c:128 * c + 128] = total[8 * c:8 * c + 8]
            o.reduce_o[:, 128 * c:128 * c + 128] = total[80 + 32 * c:112 + 32 * c]
        for c in range(8):
            o.expand_o[:, 128 * c:128 * c + 128] = total[16 + 8 * c:24 + 8 * c]

    def feed_vec_end():
        total = o.feed_vec[len(links.sizes)]
        o.mid_g_o[...] = own_eight(total, 0)
        o.mid_s_o[...] = own_eight(total, 2)
        o.red_b_o[...] = own_eight(total, 4)
        row = lax.broadcasted_iota(jnp.int32, (8, 128), 0)
        x = jnp.sum(jnp.where(row == links.me // 4, total[6:14], 0.0), axis=0, keepdims=True)
        x = pltpu.roll(jnp.broadcast_to(x, (8, 128)), (128 - (links.me * 32) % 128) % 128, 1)
        o.exp_b_o[...] = x[0:1, 0:32].reshape(32)

    def pair_grad(pair, n1):
        cols = [slice(part * D + pair * 128, part * D + pair * 128 + 128) for part in range(3)]
        q, k, v = ((o.g_entry[:, c] + dot_tn(n1, o.qkv[0, :, c])).reshape(n, 8, 128) for c in cols)
        store_rows(o.buf1, PAIR_ROWS * pair, q, k)
        store_rows(o.buf1, PAIR_ROWS * pair + 16, v, jnp.zeros_like(v))

    def pair_end(pair, total):
        for part in range(3):
            at = part * D + pair * 128
            o.entry_o[:, at:at + 128] = total[8 * part:8 * part + 8]

    def lead_vec_end():
        total = o.lead_vec[len(links.sizes)]
        o.lead_g_o[...] = own_eight(total, 0)
        o.lead_s_o[...] = own_eight(total, 2)

    every = slice(0, tokens)

    def first_mixed(rows=every):
        return o.state_in[rows].astype(F32) + o.embed_in[rows].astype(F32)

    def lead_normed(xhat):
        return (xhat * o.vecs[0:1, :] + o.vecs[1:2, :]).astype(BF16)

    def middle_normed(xhat):
        return (xhat * o.vecs[2:3, :] + o.vecs[3:4, :]).astype(BF16)

    def enter(p):
        x = o.grad[...] + o.embed_in[...].astype(F32)
        o.total[...] = x
        n1 = lead_normed(norm_parts(x)[0])
        for i in range(3):
            y = dot_nn(n1, o.entry_w[:, i * D:(i + 1) * D])
            o.qkv[p, :, i * D:(i + 1) * D] = (y * (LOG2E * 0.125) if i == 0 else y).astype(BF16)

    def forward_chunk(n2, c):
        hid = dot_nn(n2, o.expand_w[:, c]) + o.eb[:, c]
        cdf, e = gelu_parts(hid)
        return (hid * cdf).astype(BF16), cdf + hid * (e * INV_SQRT_2PI)

    def backward_chunk(d_out, n2, act, gp, c):
        reduce_g = dot_tn(d_out, act)
        dh = dot_nn(d_out, o.reduce_t[:, c]) * gp
        bias_g = jnp.sum(dh, axis=0, keepdims=True)
        dh = dh.astype(BF16)
        expand_g = dot_tn(n2, dh)
        o.g_reduce_t[:, c] += reduce_g
        o.g_exp_b[:, c] += bias_g
        o.g_expand[:, c] += expand_g
        return dot_nn(dh, o.expand_t[c, :])

    def clear():
        for r in (o.g_entry, o.g_exit, o.g_expand, o.g_reduce_t, o.g_small, o.g_exp_b):
            r[...] = jnp.zeros_like(r)

    def add_small(at, row):
        o.g_small[at:at + 1, :] += row

    def feed_finish(p, rows, g, dn, xhat, rstd):
        add_small(5, jnp.sum(g, axis=0, keepdims=True))
        add_small(2, jnp.sum(dn * xhat, axis=0, keepdims=True))
        add_small(3, jnp.sum(dn, axis=0, keepdims=True))
        dm = g + norm_pull(xhat, rstd, o.vecs[2:3, :], dn)
        o.grad[rows] = dm
        db = dm.astype(BF16)
        o.g_exit[...] += dot_tn(o.att[p, rows], db)
        o.grad_in[rows] = dot_nn(db, o.exit_t[...]).astype(BF16)

    def feed_first(rows):
        mid = o.total[rows] + dot_nn(o.att[0, rows], o.exit_w[...])
        o.middle[rows] = mid
        n2 = middle_normed(norm_parts(mid)[0])
        res = mid + o.vecs[4:5, :]
        for c in chunks:
            act, gp = forward_chunk(n2, c)
            o.active[rows, c] = act
            o.gelup[rows, c] = gp.astype(BF16)
            res = res + dot_nn(act, o.reduce_w[c, :])
        o.grad[rows] = res

    def feed_last(rows):
        mid = o.total[rows] + dot_nn(o.att[1, rows], o.exit_w[...])
        o.grad[rows] = mid
        n2 = middle_normed(norm_parts(mid)[0])
        res = mid + o.vecs[4:5, :]
        d_out = o.grad_in[rows]
        dn = None
        for c in chunks:
            act, gp = forward_chunk(n2, c)
            res = res + dot_nn(act, o.reduce_w[c, :])
            part = backward_chunk(d_out, n2, act, gp, c)
            dn = part if dn is None else dn + part
        o.final[rows] = res.astype(BF16)
        xhat, rstd = norm_parts(o.grad[rows])
        feed_finish(1, rows, o.grad_in[rows].astype(F32), dn, xhat, rstd)

    def feed_back(rows):
        n2 = middle_normed(norm_parts(o.middle[rows])[0])
        d_out = o.grad[rows].astype(BF16)
        dn = None
        for c in chunks:
            part = backward_chunk(d_out, n2, o.active[rows, c], o.gelup[rows, c].astype(F32), c)
            dn = part if dn is None else dn + part
        xhat, rstd = norm_parts(o.middle[rows])
        feed_finish(0, rows, o.grad[rows], dn, xhat, rstd)

    def by_rows(phase):
        def part(i, carry):
            phase(pl.ds(pl.multiple_of(i * ROWS, ROWS), ROWS))
            return carry
        lax.fori_loop(0, tokens // ROWS, part, 0)

    def add_entry(p, x):
        o.g_entry[...] += dot_tn(lead_normed(norm_parts(x)[0]), o.qkv[p])

    def leave(p):
        dn = dot_nn(o.qkv[p], o.entry_t[...])
        last = p == LOOPS - 1
        xhat, rstd = norm_parts(jnp.where(last, o.total[...], first_mixed()))
        add_small(0, jnp.sum(dn * xhat, axis=0, keepdims=True))
        add_small(1, jnp.sum(dn, axis=0, keepdims=True))
        g = o.grad[...] + norm_pull(xhat, rstd, o.vecs[0:1, :], dn)
        o.grad[...] = g
        o.total[...] = g + jnp.where(last, 0.0, o.total[...])

    def forward(p, hook=None):
        pl.run_scoped(lambda vt: attn_forward(o.qkv, p, o.att, o.lx, vt, seqs, hook), pltpu.VMEM((2, 2, 128, LEN), BF16))

    def backward(p, hook):
        head = [pltpu.VMEM((2, LEN, 128), BF16)] * 4 + [pltpu.VMEM((128, LEN), F32)] * 2 + [pltpu.VMEM((2, LEN, 128), F32)]
        pl.run_scoped(lambda *bufs: attn_backward(o.qkv, p, o.att, o.lx, o.grad_in, *bufs, seqs, hook), *head)

    def forward_passes(hook, ready):
        def one(p, carry):
            enter(p)
            forward(p, lambda w: hook(p, w))

            @pl.when(p == 0)
            def _():
                ready()
                by_rows(feed_first)

            return carry

        lax.fori_loop(0, LOOPS, one, 0)
        by_rows(feed_last)

    def backward_passes(hook, pair_done, ready):
        def one(i, carry):
            p = LOOPS - 1 - i
            backward(p, lambda pair, s: hook(p, pair, s))

            @pl.when(p == LOOPS - 1)
            def _():
                add_entry(LOOPS - 1, o.total[...])

            @pl.when(p == 0)
            def _():
                pair_done()

            leave(p)

            @pl.when(p == LOOPS - 1)
            def _():
                by_rows(feed_back)
                ready()

            return carry

        lax.fori_loop(0, LOOPS, one, 0)

    if not comm:
        for i, r in enumerate((o.lead_g, o.lead_s, o.mid_g, o.mid_s, o.red_b)):
            o.vecs[i:i + 1, :] = r[...].astype(F32)
        o.eb[...] = o.exp_b[...].astype(F32)
        o.grad_in[...] = o.grad_h[...]
        o.grad[...] = o.state_in[...].astype(F32)
        turn_weights()
        clear()
        forward_passes(lambda p, w: None, lambda: None)
        backward_passes(lambda p, pair, s: None, lambda: add_entry(0, first_mixed()), lambda: None)
        o.g_reduce[...] = o.g_reduce_t[...].T
        for i in range(4):
            o.g_small[8 + i:9 + i, :] = o.g_exp_b[:, i * D:(i + 1) * D]
        return

    links = Links(n)
    last = len(links.sizes) - 1
    arrived = links.barrier()
    loads = [
        pltpu.make_async_copy(src, dst, o.load_sem.at[i])
        for i, (src, dst) in enumerate(((o.state_h, o.state_in), (o.embed_h, o.embed_in), (o.grad_h, o.grad_in)))
    ]
    for load in loads:
        load.start()
    pack_parameters()
    arrived()
    links.gather_start(o.buf1, o.sem1, 0)
    pack_more_parameters()
    clear()
    links.gather_wait(o.buf1, o.sem1, 0)
    links.gather_start(o.buf1, o.sem1, 1)
    links.gather_start(o.buf2, o.sem2, 0)
    for load in loads:
        load.wait()
    o.grad[...] = o.state_in[...].astype(F32)
    links.gather_wait(o.buf1, o.sem1, 1)
    links.gather_start(o.buf1, o.sem1, 2)
    links.gather_wait(o.buf2, o.sem2, 0)
    links.gather_start(o.buf2, o.sem2, 1)
    links.gather_wait(o.buf1, o.sem1, 2)
    unpack_first()

    def gather_more(p, w):
        if w == seqs:
            @pl.when(p == 0)
            def _():
                links.gather_wait(o.buf2, o.sem2, 1)
                links.gather_start(o.buf2, o.sem2, 2)

    def gather_end():
        links.gather_wait(o.buf2, o.sem2, 2)
        unpack_second()
        turn_weights()

    forward_passes(gather_more, gather_end)
    feed = Reduction(links, o.buf2, [o.feed_got0, o.feed_part1, o.feed_got1, o.feed_part2, o.feed_got2], o.sem3)
    first = Reduction(links, o.buf1.at[:, :, :, pl.ds(0, PAIR_ROWS), :], [o.pair0_got0, o.pair0_part1, o.pair0_got1, o.pair0_part2, o.pair0_got2], o.sem4)
    second = Reduction(links, o.buf1.at[:, :, :, pl.ds(PAIR_ROWS, PAIR_ROWS), :], [o.pair1_got0, o.pair1_part1, o.pair1_got1, o.pair1_part2, o.pair1_got2], o.sem5)
    feed_vec = (o.feed_vec, o.feed_vec_got, o.sem6)
    lead_vec = (o.lead_vec, o.lead_vec_got, o.sem7)

    def reduce_begin():
        feed_pack()
        feed.start(0)
        links.sum_start(*feed_vec, 0)

    def reduce_more(p, pair, s):
        @pl.when((p == 0) & (pair == 0) & (s == 1))
        def _():
            feed.turn(0)
            links.sum_wait(*feed_vec, 0)
            links.sum_start(*feed_vec, 1)

        @pl.when((p == 0) & (pair == 1) & (s == 0))
        def _():
            o.att[1] = lead_normed(norm_parts(first_mixed())[0])
            pair_grad(0, o.att[1])
            first.start(0)

        @pl.when((p == 0) & (pair == 1) & (s == seqs - 1))
        def _():
            feed.turn(1)
            first.turn(0)
            links.sum_wait(*feed_vec, 1)
            links.sum_start(*feed_vec, 2)

    def reduce_last():
        pair_grad(1, o.att[1])
        second.start(0)
        first.turn(1)

    backward_passes(reduce_more, reduce_last, reduce_begin)
    vector_rows(o.lead_vec, halves(o.g_small[0:1, :]) + halves(o.g_small[1:2, :]), LEAD_VECS)
    links.sum_start(*lead_vec, 0)
    second.turn(0)
    feed_end(feed.take(2))
    links.sum_wait(*feed_vec, 2)
    feed_vec_end()
    links.sum_wait(*lead_vec, 0)
    links.sum_start(*lead_vec, 1)
    second.turn(1)
    pair_end(0, first.take(2))
    links.sum_wait(*lead_vec, 1)
    links.sum_start(*lead_vec, 2)
    pair_end(1, second.take(2))
    links.sum_wait(*lead_vec, 2)
    lead_vec_end()


VECTOR_INPUTS = ("lead_g", "lead_s", "mid_g", "mid_s", "red_b", "exp_b")


def mega(n, tokens, comm):
    T = tokens
    vmem = pltpu.VMEM
    outs = [("final", (T, D), BF16), ("grad", (T, D), F32), ("total", (T, D), F32)]
    scratch = [
        ("qkv", vmem((2, T, 3 * D), BF16)), ("att", vmem((2, T, D), BF16)), ("lx", vmem((2, T, D), BF16)),
        ("middle", vmem((T, D), F32)), ("active", vmem((T, FF), BF16)), ("gelup", vmem((T, FF), BF16)),
        ("entry_t", vmem((3 * D, D), BF16)), ("exit_t", vmem((D, D), BF16)), ("expand_t", vmem((FF, D), BF16)), ("reduce_t", vmem((D, FF), BF16)),
        ("vecs", vmem((8, D), F32)), ("eb", vmem((1, FF), F32)),
        ("g_reduce_t", vmem((D, FF), F32)), ("g_exp_b", vmem((1, FF), F32)),
    ]
    grads = [("g_entry", (D, 3 * D)), ("g_exit", (D, D)), ("g_expand", (D, FF)), ("g_small", (16, D))]
    weights = [("entry_w", (D, 3 * D)), ("exit_w", (D, D)), ("expand_w", (D, FF)), ("reduce_w", (FF, D))]
    in_vmem, in_hbm = pl.BlockSpec(memory_space=pltpu.VMEM), pl.BlockSpec(memory_space=pl.ANY)
    if comm:
        ins = ("state_h", "embed_h", "grad_h", "entry_s", "exit_s", "expand_s", "reduce_s") + VECTOR_INPUTS
        in_specs = [in_hbm] * 3 + [in_vmem] * 10
        r, rr = D // n, FF // n
        outs += [
            ("entry_o", (r, 3 * D), F32), ("exit_o", (r, D), F32), ("lead_g_o", (r,), F32), ("lead_s_o", (r,), F32),
            ("expand_o", (r, FF), F32), ("reduce_o", (rr, D), F32), ("mid_g_o", (r,), F32), ("mid_s_o", (r,), F32),
            ("exp_b_o", (rr,), F32), ("red_b_o", (r,), F32),
        ]
        scratch += [(name, vmem((T, D), BF16)) for name in ("state_in", "embed_in", "grad_in")]
        scratch += [(name, vmem(shape, F32)) for name, shape in grads] + [(name, vmem(shape, BF16)) for name, shape in weights]
        s = tuple(size for _, size in digit_groups(n))
        scratch += [("vec", vmem((16, 128), F32))]
        scratch += [("buf1", vmem(s + (ENTRY_ROWS, 128), BF16)), ("buf2", vmem(s + (FEED_ROWS, 128), BF16))]
        for name, rows in (("pair0", PAIR_ROWS), ("pair1", PAIR_ROWS), ("feed", FEED_ROWS)):
            for step, g in enumerate((2, 1, 0)):
                scratch.append((f"{name}_got{step}", vmem((s[g] - 1,) + s[:g] + (rows, 128), BF16)))
                if g < 2:
                    scratch.append((f"{name}_part{step}", vmem(s[: g + 1] + (rows, 128), BF16)))
        for name, rows in (("feed_vec", FEED_VECS), ("lead_vec", LEAD_VECS)):
            scratch += [(name, vmem((len(s) + 1, rows, 128), F32)), (f"{name}_got", vmem((len(s), 3, rows, 128), F32))]
        scratch += [(f"sem{i}", pltpu.SemaphoreType.DMA((2, 3, 3))) for i in range(1, 8)] + [("load_sem", pltpu.SemaphoreType.DMA((3,)))]
        out_shape = [vmem(shape, dtype) for _, shape, dtype in outs]
        params = dict(vmem_limit_bytes=58 * 1024 * 1024, collective_id=0, has_side_effects=True)
    else:
        ins = ("state_in", "embed_in", "grad_h") + tuple(name for name, _ in weights) + VECTOR_INPUTS
        in_specs = [in_vmem] * len(ins)
        outs += [(name, shape, F32) for name, shape in grads] + [("g_reduce", (FF, D), F32)]
        out_shape = [jax.ShapeDtypeStruct(shape, dtype) for _, shape, dtype in outs]
        scratch += [("grad_in", vmem((T, D), BF16))]
        params = dict(vmem_limit_bytes=63 * 1024 * 1024)
    names = ins + tuple(out[0] for out in outs) + tuple(name for name, _ in scratch)
    return pl.pallas_call(
        functools.partial(mega_kernel, names=names, n=n, tokens=T, comm=comm),
        in_specs=in_specs,
        out_specs=[in_vmem] * len(outs),
        out_shape=out_shape,
        scratch_shapes=[shape for _, shape in scratch],
        compiler_params=pltpu.CompilerParams(**params),
        name="block",
    )


def drain_kernel(*refs):
    count = len(refs) // 2
    sems = refs[-1]
    copies = [pltpu.make_async_copy(refs[i], refs[count + i], sems.at[i]) for i in range(count)]
    for copy in copies:
        copy.start()
    for copy in copies:
        copy.wait()


def drain(*arrays):
    count = len(arrays)
    return pl.pallas_call(
        drain_kernel,
        in_specs=[pl.BlockSpec(memory_space=pltpu.VMEM)] * count,
        out_specs=[pl.BlockSpec(memory_space=pl.ANY)] * count,
        out_shape=[jax.ShapeDtypeStruct(a.shape, a.dtype) for a in arrays],
        scratch_shapes=[pltpu.SemaphoreType.DMA((count,))],
        compiler_params=pltpu.CompilerParams(vmem_limit_bytes=1024 * 1024),
        name="drain",
    )(*arrays)


def on_device(loop_state, embedding, output_grad, entry_weight, exit_weight, lead_gain, lead_shift, expand_weight, reduce_weight, middle_gain, middle_shift, expand_bias, reduce_bias):
    n = lax.axis_size("fsdp")
    tokens = loop_state.shape[0]
    vectors = (lead_gain, lead_shift, middle_gain, middle_shift, reduce_bias, expand_bias)
    weights = (entry_weight, exit_weight, expand_weight, reduce_weight)
    if entry_weight.shape[0] == 8 and len(digit_groups(n)) == 3:
        return tuple(drain(*mega(n, tokens, True)(loop_state, embedding, output_grad, *weights, *vectors)))
    shards = weights + vectors
    packed = jnp.concatenate([a.reshape(-1) for a in shards])
    whole = lax.all_gather(packed, "fsdp", axis=0)
    full, at = [], 0
    for a in shards:
        whole_a = whole[:, at : at + a.size].reshape((n * a.shape[0],) + a.shape[1:])
        full.append(whole_a if a.ndim == 2 else whole_a.reshape(1, -1))
        at += a.size
    final, grad, total, g_entry, g_exit, g_expand, small, g_reduce = mega(n, tokens, False)(loop_state, embedding, output_grad, *full)
    terms = (g_entry, g_exit, small[0], small[1], g_expand, g_reduce, small[2], small[3], small[8:12].reshape(-1), small[5])
    sums = lax.psum_scatter(jnp.concatenate([a.reshape(n, -1) for a in terms], axis=1), "fsdp", scatter_dimension=0, tiled=True)[0]
    outs, at = [], 0
    for a in terms:
        size = a.size // n
        outs.append(sums[at : at + size].reshape((a.shape[0] // n,) + a.shape[1:]))
        at += size
    return (final, grad, total, *outs)


def solution(mesh):
    two, one = P("fsdp", None), P("fsdp")
    in_specs = (two, two, two, two, two, one, one, two, two, one, one, one, one)
    out_specs = (two, two, two, two, two, one, one, two, two, one, one, one, one)
    return jax.shard_map(on_device, mesh=mesh, in_specs=in_specs, out_specs=out_specs, check_vma=False)
```

```python
import functools
import math
from types import SimpleNamespace

import jax
import jax.numpy as jnp
from jax import lax
from jax.experimental import pallas as pl
from jax.experimental.pallas import tpu as pltpu
from jax.sharding import PartitionSpec as P

F32, BF16 = jnp.float32, jnp.bfloat16
LEN = 1024
LOOPS = 2
EPS = 1e-05
D = 256
FF = 1024
HD = 64
BLK = 256
LOG2E = 1.4426950408889634
LN2 = 0.6931471805599453
INV_SQRT_2PI = 1.0 / math.sqrt(2.0 * math.pi)
NEG = -1e30


def dot_nn(a, b):
    return lax.dot_general(a, b, (((1,), (0,)), ((), ())), preferred_element_type=F32)


def dot_nt(a, b):
    return lax.dot_general(a, b, (((1,), (1,)), ((), ())), preferred_element_type=F32)


def dot_tn(a, b):
    return lax.dot_general(a, b, (((0,), (0,)), ((), ())), preferred_element_type=F32)


def norm_parts(x):
    mean = jnp.mean(x, axis=-1, keepdims=True)
    center = x - mean
    var = jnp.mean(center * center, axis=-1, keepdims=True)
    rstd = lax.rsqrt(var + EPS)
    return center * rstd, rstd


def norm_pull(xhat, rstd, gain, dy):
    dn = dy * gain
    m1 = jnp.mean(dn, axis=-1, keepdims=True)
    m2 = jnp.mean(dn * xhat, axis=-1, keepdims=True)
    return rstd * (dn - m1 - xhat * m2)


def gelu_parts(x):
    cdf = 0.5 + 0.5 * lax.erf(x * math.sqrt(0.5))
    return cdf, jnp.exp2((-0.5 * LOG2E) * (x * x))


def lane_iota(rows):
    return lax.broadcasted_iota(jnp.int32, (rows, 128), 1)


def three_parts(x):
    hi = x.astype(BF16).astype(F32)
    r = x - hi
    mid = r.astype(BF16).astype(F32)
    return hi, mid, r - mid


def spread_parts(x, lane, spare):
    hi, mid, lo = three_parts(x)
    return jnp.where(lane == spare, hi, jnp.where(lane == spare + 1, mid, jnp.where(lane == spare + 2, lo, 0.0)))


def head_pairs(seqs):
    return [(pair, s) for pair in range(2) for s in range(seqs)]


def pair_slices(pair, s):
    seq = slice(s * LEN, (s + 1) * LEN)
    return seq, [slice(part * D + pair * 128, part * D + pair * 128 + 128) for part in range(3)]


def attn_forward(qkv, p, att, lx, vt, seqs, hook=None):
    nblk = LEN // BLK
    for b in range(2):
        vt[b, 0, HD:] = jnp.ones((HD, LEN), BF16)
        vt[b, 1, :HD] = jnp.ones((HD, LEN), BF16)
    low = lane_iota(BLK) < HD
    keep = lax.broadcasted_iota(jnp.int32, (BLK, BLK), 0) <= lax.broadcasted_iota(jnp.int32, (BLK, BLK), 1)
    row = lax.broadcasted_iota(jnp.int32, (8, BLK), 0)
    works = head_pairs(seqs)

    def scores(w, j, h):
        seq, (cq, ck, _) = pair_slices(*works[w])
        r0 = seq.start
        q = qkv[p, r0 + j * BLK:r0 + (j + 1) * BLK, cq]
        zero = jnp.zeros_like(q)
        q = jnp.where(low, q, zero) if h == 0 else jnp.where(low, zero, q)
        return dot_nt(qkv[p, r0:r0 + (j + 1) * BLK, ck], q)

    units = [(w, j, h) for w in range(len(works)) for j in range(nblk) for h in range(2)]
    st = None
    outs, pieces = [], []
    for u, (w, j, h) in enumerate(units):
        seq, (cq, _, cv) = pair_slices(*works[w])
        if j == 0 and h == 0:
            if hook is not None:
                hook(w)
            v = qkv[p, seq, cv].T
            vt[w % 2, 0, :HD] = v[:HD]
            vt[w % 2, 1, HD:] = v[HD:]
        if st is None:
            st = scores(w, j, h)
        later = scores(*units[u + 1]) if u + 1 < len(units) else None
        diag = jnp.where(keep, st[j * BLK:], NEG)
        st = jnp.concatenate([st[: j * BLK], diag], axis=0) if j else diag
        top = jnp.max(st, axis=0, keepdims=True)
        pr = jnp.exp2(st - top).astype(BF16)
        ox = dot_nn(vt[w % 2, h, :, : (j + 1) * BLK], pr)
        mine, den = (ox[:HD], ox[HD:]) if h == 0 else (ox[HD:], ox[:HD])
        outs.append(mine * (1.0 / den))
        hi, mid, lo = three_parts(-(top + jnp.log(den[:8]) * LOG2E))
        pieces.append(jnp.where(row == 0, hi, jnp.where(row == 1, mid, jnp.where(row == 2, lo, 0.0))))
        if h == 1:
            rows = slice(seq.start + j * BLK, seq.start + (j + 1) * BLK)
            att[p, rows, cq] = jnp.concatenate(outs, axis=0).T.astype(BF16)
            blank = jnp.zeros((HD - 8, BLK), F32)
            lx[p, rows, cq] = jnp.concatenate([pieces[1], blank, pieces[0], blank], axis=0).T.astype(BF16)
            outs, pieces = [], []
        st = later


def attn_backward(qkv, p, att, lx, datt, vx, kx, qx, dox, dkt, dvt, dq, seqs, hook):
    nblk = LEN // BLK
    low = lane_iota(LEN) < HD
    lane = lane_iota(LEN)
    keep = lax.broadcasted_iota(jnp.int32, (BLK, BLK), 1) <= lax.broadcasted_iota(jnp.int32, (BLK, BLK), 0)
    one = jnp.ones((LEN, 128), BF16)

    def work(pair, s):
        hook(pair, s)
        seq = pl.ds(pl.multiple_of(s * LEN, LEN), LEN)
        cq, ck, cv = (pl.ds(pl.multiple_of(part * D + pair * 128, 128), 128) for part in range(3))
        v = qkv[p, seq, cv]
        vx[0] = jnp.where(low, v, one)
        vx[1] = jnp.where(low, one, v)
        k = qkv[p, seq, ck]
        kx[0] = jnp.where(low, k, one)
        kx[1] = jnp.where(low, one, k)
        q = qkv[p, seq, cq]
        ls = lx[p, seq, cq]
        qx[0] = jnp.where(low, q, ls)
        qx[1] = jnp.where(low, ls, q)
        do = datt[seq, cq]
        dof = do.astype(F32)
        prod = dof * att[p, seq, cq].astype(F32)
        in0 = jnp.sum(jnp.where(low, prod, 0.0), axis=-1, keepdims=True)
        in1 = jnp.sum(jnp.where(low, 0.0, prod), axis=-1, keepdims=True)
        dox[0] = jnp.where(low, dof, spread_parts(jnp.broadcast_to(-in0, (LEN, 128)), lane, HD)).astype(BF16)
        dox[1] = jnp.where(low, spread_parts(jnp.broadcast_to(-in1, (LEN, 128)), lane, 0), dof).astype(BF16)
        qt = q.T
        dot = do.T

        def products(h, i):
            a = i * BLK
            return dot_nt(qx[h, a:], kx[h, a:a + BLK]), dot_nt(dox[h, a:], vx[h, a:a + BLK])

        units = [(h, i) for h in range(2) for i in range(nblk)]
        ready = products(*units[0])
        for u, (h, i) in enumerate(units):
            later = products(*units[u + 1]) if u + 1 < len(units) else None
            sc, dp = ready
            a = i * BLK
            pr = jnp.exp2(sc)
            diag = jnp.where(keep, pr[:BLK], 0.0)
            pr = jnp.concatenate([diag, pr[BLK:]], axis=0) if i < nblk - 1 else diag
            ds = (pr * dp).astype(BF16)
            prb = pr.astype(BF16)
            mine = slice(h * HD, h * HD + HD)
            dvt[mine, a:a + BLK] = dot_nn(dot[:, a:], prb)[mine]
            dkt[mine, a:a + BLK] = dot_nn(qt[:, a:], ds)[mine]
            part = dot_nn(ds, kx[h, a:a + BLK])
            if i == 0:
                dq[h] = part
            else:
                dq[h, a:] += part
            ready = later
        qkv[p, seq, cq] = (jnp.where(low, dq[0], dq[1]) * 0.125).astype(BF16)
        qkv[p, seq, ck] = (dkt[...].T * LN2).astype(BF16)
        qkv[p, seq, cv] = dvt[...].T.astype(BF16)

    def step(w, carry):
        work(w // seqs, w % seqs)
        return carry

    lax.fori_loop(0, 2 * seqs, step, 0)


def digit_groups(n):
    groups = [(1, 2)]
    stride = 2
    while stride < n:
        size = min(4, n // stride)
        groups.append((stride, size))
        stride *= size
    return groups[::-1]


class Links:
    def __init__(self, n):
        self.groups = digit_groups(n)
        self.me = lax.axis_index("fsdp")
        self.digits = [(self.me // stride) % size for stride, size in self.groups]
        self.sizes = tuple(size for _, size in self.groups)

    def digit(self, g, t):
        return (self.digits[g] + t) % self.sizes[g]

    def peer(self, g, t):
        return self.me + (self.digit(g, t) - self.digits[g]) * self.groups[g][0]

    def barrier(self):
        sem = pltpu.get_barrier_semaphore()
        count = 0
        for g, size in enumerate(self.sizes):
            for t in range(1, size):
                pl.semaphore_signal(sem, inc=1, device_id=(self.peer(g, t),), device_id_type=pl.DeviceIdType.MESH)
                count += 1
        return lambda: pl.semaphore_wait(sem, count)

    def copy(self, src, dst, sems, g, t):
        return pltpu.make_async_remote_copy(
            src_ref=src,
            dst_ref=dst,
            send_sem=sems.at[0, g, t - 1],
            recv_sem=sems.at[1, g, t - 1],
            device_id=(self.peer(g, t),),
            device_id_type=pl.DeviceIdType.MESH,
        )

    def held(self, buf, g, t=0):
        tail = [self.digit(g, t)] + self.digits[g + 1:]
        return buf.at[(slice(None),) * g + tuple(tail)]

    def gather_start(self, buf, sems, g):
        for t in range(1, self.sizes[g]):
            self.copy(self.held(buf, g), self.held(buf, g), sems, g, t).start()

    def gather_wait(self, buf, sems, g):
        for t in range(1, self.sizes[g]):
            self.copy(self.held(buf, g), self.held(buf, g, -t), sems, g, t).wait_recv()
        for t in range(1, self.sizes[g]):
            self.copy(self.held(buf, g), self.held(buf, g), sems, g, t).wait_send()

    def reduce_start(self, part, got, sems, g):
        for t in range(1, self.sizes[g]):
            src = part.at[(slice(None),) * g + (self.digit(g, t),)]
            self.copy(src, got.at[t - 1], sems, g, t).start()

    def reduce_wait(self, part, got, sems, g):
        for t in range(1, self.sizes[g]):
            src = part.at[(slice(None),) * g + (self.digit(g, t),)]
            self.copy(src, got.at[t - 1], sems, g, t).wait()
        total = part[(slice(None),) * g + (self.digits[g],)].astype(F32)
        for t in range(1, self.sizes[g]):
            total = total + got[t - 1].astype(F32)
        return total

    def sum_start(self, part, got, sems, g):
        for t in range(1, self.sizes[g]):
            self.copy(part.at[g], got.at[g, t - 1], sems, g, t).start()

    def sum_wait(self, part, got, sems, g):
        for t in range(1, self.sizes[g]):
            self.copy(part.at[g], got.at[g, t - 1], sems, g, t).wait()
        total = part[g]
        for t in range(1, self.sizes[g]):
            total = total + got[g, t - 1]
        part[g + 1] = total


class Reduction:
    def __init__(self, links, first, rest, sems):
        self.links, self.parts, self.gots, self.sems = links, [first] + rest[1::2], rest[0::2], sems

    def start(self, step):
        self.links.reduce_start(self.parts[step], self.gots[step], self.sems, len(self.links.sizes) - 1 - step)

    def take(self, step):
        return self.links.reduce_wait(self.parts[step], self.gots[step], self.sems, len(self.links.sizes) - 1 - step)

    def turn(self, step):
        total = self.take(step)
        self.parts[step + 1][...] = total.astype(BF16)
        self.start(step + 1)


def pair_rows(x, t):
    return jnp.concatenate([x[:, 256 * t : 256 * t + 128], x[:, 256 * t + 128 : 256 * t + 256]], axis=0)


ENTRY_ROWS = 64
FEED_ROWS = 144
PAIR_ROWS = 32
FEED_VECS = 16
LEAD_VECS = 8
CHUNK = 256


ROWS = 1024


def mega_kernel(*refs, names, n, tokens, comm):
    o = SimpleNamespace(**dict(zip(names, refs)))
    seqs = tokens // LEN
    chunks = [slice(c, c + CHUNK) for c in range(0, FF, CHUNK)]

    def pack_parameters():
        d = tuple(links.digits)
        x = o.entry_s[...].astype(F32)
        for t in range(3):
            o.buf1[d + (pl.ds(16 * t, 16),)] = pair_rows(x, t).astype(BF16)
        o.vec[...] = jnp.zeros_like(o.vec)
        for i, r in enumerate((o.lead_g, o.lead_s, o.mid_g, o.mid_s, o.red_b)):
            o.vec[i:i + 1, 0:8] = r[...].astype(F32).reshape(1, 8)
        o.vec[8:9, 0:32] = o.exp_b[...].astype(F32).reshape(1, 32)
        low = pltpu.roll(o.vec[0:8, :], (links.me * 8) % 128, 1)
        high = pltpu.roll(jnp.broadcast_to(o.vec[8:9, :], (8, 128)), (links.me * 32) % 128, 1)
        row = lax.broadcasted_iota(jnp.int32, (8, 128), 0)
        high = jnp.where(row == links.me // 4, high, 0.0)
        o.buf1[d + (pl.ds(48, 16),)] = jnp.concatenate([low, high], axis=0).astype(BF16)

    def pack_more_parameters():
        d = tuple(links.digits)
        o.buf2[d + (pl.ds(0, 16),)] = pair_rows(o.exit_s[...].astype(F32), 0).astype(BF16)
        x = o.expand_s[...].astype(F32)
        for t in range(4):
            o.buf2[d + (pl.ds(16 + 16 * t, 16),)] = pair_rows(x, t).astype(BF16)
        for c in range(2):
            o.buf2[d + (pl.ds(80 + 32 * c, 32),)] = o.reduce_s[:, 128 * c:128 * c + 128]

    def unpack(buf, at, count, dst):
        for t in range(count // 2):
            x = buf[:, :, :, at + 16 * t:at + 16 * t + 16, :].astype(F32).reshape(n, 16, 128)
            dst[:, 256 * t:256 * t + 128] = x[:, :8].reshape(8 * n, 128).astype(BF16)
            dst[:, 256 * t + 128:256 * t + 256] = x[:, 8:].reshape(8 * n, 128).astype(BF16)

    def unpack_first():
        unpack(o.buf1, 0, 6, o.entry_w)
        v = o.buf1[:, :, :, 48:64, :].astype(F32).reshape(n, 16, 128)
        first = jnp.sum(v[: n // 2], axis=0)
        second = jnp.sum(v[n // 2:], axis=0)
        o.vecs[0:5, 0:128] = first[0:5]
        o.vecs[0:5, 128:256] = second[0:5]
        both = (first + second)[8:16]
        for c in range(8):
            o.eb[0:1, 128 * c:128 * c + 128] = both[c:c + 1]

    def unpack_second():
        unpack(o.buf2, 0, 2, o.exit_w)
        unpack(o.buf2, 16, 8, o.expand_w)
        for c in range(2):
            x = o.buf2[:, :, :, 80 + 32 * c:112 + 32 * c, :]
            o.reduce_w[:, 128 * c:128 * c + 128] = x.reshape(32 * n, 128)

    def turn_weights():
        o.entry_t[...] = o.entry_w[...].T
        o.exit_t[...] = o.exit_w[...].T
        o.expand_t[...] = o.expand_w[...].T
        o.reduce_t[...] = o.reduce_w[...].T

    def chunk_rows(grad, c):
        return grad[:, 128 * c:128 * c + 128].reshape(n, 8, 128)

    def store_rows(part, at, top, bottom):
        x = jnp.concatenate([top, bottom], axis=1).astype(BF16)
        part[:, :, :, at:at + 16, :] = x.reshape(links.sizes + (16, 128))

    def halves(row):
        return [row[:, :128], row[:, 128:]]

    def vector_rows(part, rows, count):
        for i, r in enumerate(rows):
            part[0, i:i + 1, :] = r
        if len(rows) < count:
            part[0, len(rows):count, :] = jnp.zeros((count - len(rows), 128), F32)

    def own_eight(total, at):
        both = jnp.where(links.me >= n // 2, total[at + 1:at + 2], total[at:at + 1])
        both = pltpu.roll(jnp.broadcast_to(both, (8, 128)), (128 - (links.me * 8) % 128) % 128, 1)
        return both[0:1, 0:8].reshape(8)

    def feed_pack():
        store_rows(o.buf2, 0, chunk_rows(o.g_exit, 0), chunk_rows(o.g_exit, 1))
        for t in range(4):
            store_rows(o.buf2, 16 + 16 * t, chunk_rows(o.g_expand, 2 * t), chunk_rows(o.g_expand, 2 * t + 1))
        for c in range(2):
            x = o.g_reduce_t[128 * c:128 * c + 128, :].astype(BF16).T
            o.buf2[:, :, :, 80 + 32 * c:112 + 32 * c, :] = x.reshape(links.sizes + (32, 128))
        rows = halves(o.g_small[2:3, :]) + halves(o.g_small[3:4, :]) + halves(o.g_small[5:6, :])
        rows += [o.g_exp_b[:, 128 * c:128 * c + 128] for c in range(8)]
        vector_rows(o.feed_vec, rows, FEED_VECS)

    def feed_end(total):
        for c in range(2):
            o.exit_o[:, 128 * c:128 * c + 128] = total[8 * c:8 * c + 8]
            o.reduce_o[:, 128 * c:128 * c + 128] = total[80 + 32 * c:112 + 32 * c]
        for c in range(8):
            o.expand_o[:, 128 * c:128 * c + 128] = total[16 + 8 * c:24 + 8 * c]

    def feed_vec_end():
        total = o.feed_vec[len(links.sizes)]
        o.mid_g_o[...] = own_eight(total, 0)
        o.mid_s_o[...] = own_eight(total, 2)
        o.red_b_o[...] = own_eight(total, 4)
        row = lax.broadcasted_iota(jnp.int32, (8, 128), 0)
        x = jnp.sum(jnp.where(row == links.me // 4, total[6:14], 0.0), axis=0, keepdims=True)
        x = pltpu.roll(jnp.broadcast_to(x, (8, 128)), (128 - (links.me * 32) % 128) % 128, 1)
        o.exp_b_o[...] = x[0:1, 0:32].reshape(32)

    def pair_grad(pair, n1):
        cols = [slice(part * D + pair * 128, part * D + pair * 128 + 128) for part in range(3)]
        grad = dot_tn(n1, jnp.concatenate([o.qkv[0, :, c] for c in cols], axis=1))
        q, k, v = ((o.g_entry[:, c] + grad[:, 128 * i:128 * i + 128]).reshape(n, 8, 128) for i, c in enumerate(cols))
        store_rows(o.buf1, PAIR_ROWS * pair, q, k)
        store_rows(o.buf1, PAIR_ROWS * pair + 16, v, jnp.zeros_like(v))

    def pair_end(pair, total):
        for part in range(3):
            at = part * D + pair * 128
            o.entry_o[:, at:at + 128] = total[8 * part:8 * part + 8]

    def lead_vec_end():
        total = o.lead_vec[len(links.sizes)]
        o.lead_g_o[...] = own_eight(total, 0)
        o.lead_s_o[...] = own_eight(total, 2)

    every = slice(0, tokens)

    def first_mixed(rows=every):
        return o.state_in[rows].astype(F32) + o.embed_in[rows].astype(F32)

    def lead_normed(xhat):
        return (xhat * o.vecs[0:1, :] + o.vecs[1:2, :]).astype(BF16)

    def middle_normed(xhat):
        return (xhat * o.vecs[2:3, :] + o.vecs[3:4, :]).astype(BF16)

    def enter(p):
        x = o.grad[...] + o.embed_in[...].astype(F32)
        o.total[...] = x
        n1 = lead_normed(norm_parts(x)[0])
        for i in range(3):
            y = dot_nn(n1, o.entry_w[:, i * D:(i + 1) * D])
            o.qkv[p, :, i * D:(i + 1) * D] = (y * (LOG2E * 0.125) if i == 0 else y).astype(BF16)

    def forward_chunk(n2, c):
        hid = dot_nn(n2, o.expand_w[:, c]) + o.eb[:, c]
        cdf, e = gelu_parts(hid)
        return (hid * cdf).astype(BF16), cdf + hid * (e * INV_SQRT_2PI)

    def backward_chunk(d_out, n2, act, gp, c):
        reduce_g = dot_tn(d_out, act)
        dh = dot_nn(d_out, o.reduce_t[:, c]) * gp
        bias_g = jnp.sum(dh, axis=0, keepdims=True)
        dh = dh.astype(BF16)
        expand_g = dot_tn(n2, dh)
        o.g_reduce_t[:, c] += reduce_g
        o.g_exp_b[:, c] += bias_g
        o.g_expand[:, c] += expand_g
        return dot_nn(dh, o.expand_t[c, :])

    def clear():
        for r in (o.g_entry, o.g_exit, o.g_expand, o.g_reduce_t, o.g_small, o.g_exp_b):
            r[...] = jnp.zeros_like(r)

    def add_small(at, row):
        o.g_small[at:at + 1, :] += row

    def feed_finish(p, rows, g, dn, xhat, rstd):
        add_small(5, jnp.sum(g, axis=0, keepdims=True))
        add_small(2, jnp.sum(dn * xhat, axis=0, keepdims=True))
        add_small(3, jnp.sum(dn, axis=0, keepdims=True))
        dm = g + norm_pull(xhat, rstd, o.vecs[2:3, :], dn)
        o.grad[rows] = dm
        db = dm.astype(BF16)
        o.g_exit[...] += dot_tn(o.att[p, rows], db)
        o.grad_in[rows] = dot_nn(db, o.exit_t[...]).astype(BF16)

    def feed_first(rows):
        mid = o.total[rows] + dot_nn(o.att[0, rows], o.exit_w[...])
        o.middle[rows] = mid
        n2 = middle_normed(norm_parts(mid)[0])
        res = mid + o.vecs[4:5, :]
        for c in chunks:
            act, gp = forward_chunk(n2, c)
            o.active[rows, c] = act
            o.gelup[rows, c] = gp.astype(BF16)
            res = res + dot_nn(act, o.reduce_w[c, :])
        o.grad[rows] = res

    def feed_last(rows):
        mid = o.total[rows] + dot_nn(o.att[1, rows], o.exit_w[...])
        o.grad[rows] = mid
        n2 = middle_normed(norm_parts(mid)[0])
        res = mid + o.vecs[4:5, :]
        d_out = o.grad_in[rows]
        dn = None
        for c in chunks:
            act, gp = forward_chunk(n2, c)
            res = res + dot_nn(act, o.reduce_w[c, :])
            part = backward_chunk(d_out, n2, act, gp, c)
            dn = part if dn is None else dn + part
        o.final[rows] = res.astype(BF16)
        xhat, rstd = norm_parts(o.grad[rows])
        feed_finish(1, rows, o.grad_in[rows].astype(F32), dn, xhat, rstd)

    def feed_back(rows):
        n2 = middle_normed(norm_parts(o.middle[rows])[0])
        d_out = o.grad[rows].astype(BF16)
        dn = None
        for c in chunks:
            part = backward_chunk(d_out, n2, o.active[rows, c], o.gelup[rows, c].astype(F32), c)
            dn = part if dn is None else dn + part
        xhat, rstd = norm_parts(o.middle[rows])
        feed_finish(0, rows, o.grad[rows], dn, xhat, rstd)

    def by_rows(phase):
        def part(i, carry):
            phase(pl.ds(pl.multiple_of(i * ROWS, ROWS), ROWS))
            return carry
        lax.fori_loop(0, tokens // ROWS, part, 0)

    def add_entry(p, x):
        o.g_entry[...] += dot_tn(lead_normed(norm_parts(x)[0]), o.qkv[p])

    def lead_sums(p, x):
        dn = dot_nn(o.qkv[p], o.entry_t[...])
        add_small(0, jnp.sum(dn * norm_parts(x)[0], axis=0, keepdims=True))
        add_small(1, jnp.sum(dn, axis=0, keepdims=True))
        return dn

    def leave(dn, x, before):
        xhat, rstd = norm_parts(x)
        g = o.grad[...] + norm_pull(xhat, rstd, o.vecs[0:1, :], dn)
        o.grad[...] = g
        o.total[...] = g if before is None else before + g

    def forward(p, hook=None):
        pl.run_scoped(lambda vt: attn_forward(o.qkv, p, o.att, o.lx, vt, seqs, hook), pltpu.VMEM((2, 2, 128, LEN), BF16))

    def backward(p, hook):
        head = [pltpu.VMEM((2, LEN, 128), BF16)] * 4 + [pltpu.VMEM((128, LEN), F32)] * 2 + [pltpu.VMEM((2, LEN, 128), F32)]
        pl.run_scoped(lambda *bufs: attn_backward(o.qkv, p, o.att, o.lx, o.grad_in, *bufs, seqs, hook), *head)

    def forward_passes(hook, ready):
        def one(p, carry):
            enter(p)
            forward(p, lambda w: hook(p, w))

            @pl.when(p == 0)
            def _():
                ready()
                by_rows(feed_first)

            return carry

        lax.fori_loop(0, LOOPS, one, 0)
        by_rows(feed_last)

    def backward_passes(hook, ready):
        def one(i, carry):
            p = LOOPS - 1 - i
            backward(p, lambda pair, s: hook(p, pair, s))

            @pl.when(p == LOOPS - 1)
            def _():
                add_entry(LOOPS - 1, o.total[...])
                leave(lead_sums(LOOPS - 1, o.total[...]), o.total[...], None)
                by_rows(feed_back)
                ready()

            return carry

        lax.fori_loop(0, LOOPS, one, 0)

    if not comm:
        for i, r in enumerate((o.lead_g, o.lead_s, o.mid_g, o.mid_s, o.red_b)):
            o.vecs[i:i + 1, :] = r[...].astype(F32)
        o.eb[...] = o.exp_b[...].astype(F32)
        o.grad_in[...] = o.grad_h[...]
        o.grad[...] = o.state_in[...].astype(F32)
        turn_weights()
        clear()
        forward_passes(lambda p, w: None, lambda: None)
        backward_passes(lambda p, pair, s: None, lambda: None)
        add_entry(0, first_mixed())
        leave(lead_sums(0, first_mixed()), first_mixed(), o.total[...])
        o.g_reduce[...] = o.g_reduce_t[...].T
        for i in range(4):
            o.g_small[8 + i:9 + i, :] = o.g_exp_b[:, i * D:(i + 1) * D]
        return

    links = Links(n)
    last = len(links.sizes) - 1
    arrived = links.barrier()
    loads = [
        pltpu.make_async_copy(src, dst, o.load_sem.at[i])
        for i, (src, dst) in enumerate(((o.state_h, o.state_in), (o.embed_h, o.embed_in), (o.grad_h, o.grad_in)))
    ]
    for load in loads:
        load.start()
    pack_parameters()
    arrived()
    links.gather_start(o.buf1, o.sem1, 0)
    pack_more_parameters()
    clear()
    links.gather_wait(o.buf1, o.sem1, 0)
    links.gather_start(o.buf1, o.sem1, 1)
    links.gather_start(o.buf2, o.sem2, 0)
    for load in loads:
        load.wait()
    o.grad[...] = o.state_in[...].astype(F32)
    links.gather_wait(o.buf1, o.sem1, 1)
    links.gather_start(o.buf1, o.sem1, 2)
    links.gather_wait(o.buf2, o.sem2, 0)
    links.gather_start(o.buf2, o.sem2, 1)
    links.gather_wait(o.buf1, o.sem1, 2)
    unpack_first()

    def gather_more(p, w):
        if w == seqs:
            @pl.when(p == 0)
            def _():
                links.gather_wait(o.buf2, o.sem2, 1)
                links.gather_start(o.buf2, o.sem2, 2)

    def gather_end():
        links.gather_wait(o.buf2, o.sem2, 2)
        unpack_second()
        turn_weights()

    forward_passes(gather_more, gather_end)
    feed = Reduction(links, o.buf2, [o.feed_got0, o.feed_part1, o.feed_got1, o.feed_part2, o.feed_got2], o.sem3)
    first = Reduction(links, o.buf1.at[:, :, :, pl.ds(0, PAIR_ROWS), :], [o.pair0_got0, o.pair0_part1, o.pair0_got1, o.pair0_part2, o.pair0_got2], o.sem4)
    second = Reduction(links, o.buf1.at[:, :, :, pl.ds(PAIR_ROWS, PAIR_ROWS), :], [o.pair1_got0, o.pair1_part1, o.pair1_got1, o.pair1_part2, o.pair1_got2], o.sem5)
    feed_vec = (o.feed_vec, o.feed_vec_got, o.sem6)
    lead_vec = (o.lead_vec, o.lead_vec_got, o.sem7)

    def reduce_begin():
        feed_pack()
        feed.start(0)
        links.sum_start(*feed_vec, 0)

    def reduce_more(p, pair, s):
        @pl.when((p == 0) & (pair == 0) & (s == 1))
        def _():
            feed.turn(0)
            links.sum_wait(*feed_vec, 0)
            links.sum_start(*feed_vec, 1)

        @pl.when((p == 0) & (pair == 1) & (s == 0))
        def _():
            o.att[1] = lead_normed(norm_parts(first_mixed())[0])
            pair_grad(0, o.att[1])
            first.start(0)

        @pl.when((p == 0) & (pair == 1) & (s == seqs - 1))
        def _():
            feed.turn(1)
            first.turn(0)
            links.sum_wait(*feed_vec, 1)
            links.sum_start(*feed_vec, 2)

    backward_passes(reduce_more, reduce_begin)
    pair_grad(1, o.att[1])
    second.start(0)
    dn = lead_sums(0, first_mixed())
    vector_rows(o.lead_vec, halves(o.g_small[0:1, :]) + halves(o.g_small[1:2, :]), LEAD_VECS)
    links.sum_start(*lead_vec, 0)
    second.turn(0)
    first.turn(1)
    leave(dn, first_mixed(), o.total[...])
    feed_end(feed.take(2))
    links.sum_wait(*feed_vec, 2)
    feed_vec_end()
    links.sum_wait(*lead_vec, 0)
    links.sum_start(*lead_vec, 1)
    second.turn(1)
    pair_end(0, first.take(2))
    links.sum_wait(*lead_vec, 1)
    links.sum_start(*lead_vec, 2)
    pair_end(1, second.take(2))
    links.sum_wait(*lead_vec, 2)
    lead_vec_end()


VECTOR_INPUTS = ("lead_g", "lead_s", "mid_g", "mid_s", "red_b", "exp_b")


def mega(n, tokens, comm):
    T = tokens
    vmem = pltpu.VMEM
    outs = [("final", (T, D), BF16), ("grad", (T, D), F32), ("total", (T, D), F32)]
    scratch = [
        ("qkv", vmem((2, T, 3 * D), BF16)), ("att", vmem((2, T, D), BF16)), ("lx", vmem((2, T, D), BF16)),
        ("middle", vmem((T, D), F32)), ("active", vmem((T, FF), BF16)), ("gelup", vmem((T, FF), BF16)),
        ("entry_t", vmem((3 * D, D), BF16)), ("exit_t", vmem((D, D), BF16)), ("expand_t", vmem((FF, D), BF16)), ("reduce_t", vmem((D, FF), BF16)),
        ("vecs", vmem((8, D), F32)), ("eb", vmem((1, FF), F32)),
        ("g_reduce_t", vmem((D, FF), F32)), ("g_exp_b", vmem((1, FF), F32)),
    ]
    grads = [("g_entry", (D, 3 * D)), ("g_exit", (D, D)), ("g_expand", (D, FF)), ("g_small", (16, D))]
    weights = [("entry_w", (D, 3 * D)), ("exit_w", (D, D)), ("expand_w", (D, FF)), ("reduce_w", (FF, D))]
    in_vmem, in_hbm = pl.BlockSpec(memory_space=pltpu.VMEM), pl.BlockSpec(memory_space=pl.ANY)
    if comm:
        ins = ("state_h", "embed_h", "grad_h", "entry_s", "exit_s", "expand_s", "reduce_s") + VECTOR_INPUTS
        in_specs = [in_hbm] * 3 + [in_vmem] * 10
        r, rr = D // n, FF // n
        outs += [
            ("entry_o", (r, 3 * D), F32), ("exit_o", (r, D), F32), ("lead_g_o", (r,), F32), ("lead_s_o", (r,), F32),
            ("expand_o", (r, FF), F32), ("reduce_o", (rr, D), F32), ("mid_g_o", (r,), F32), ("mid_s_o", (r,), F32),
            ("exp_b_o", (rr,), F32), ("red_b_o", (r,), F32),
        ]
        scratch += [(name, vmem((T, D), BF16)) for name in ("state_in", "embed_in", "grad_in")]
        scratch += [(name, vmem(shape, F32)) for name, shape in grads] + [(name, vmem(shape, BF16)) for name, shape in weights]
        s = tuple(size for _, size in digit_groups(n))
        scratch += [("vec", vmem((16, 128), F32))]
        scratch += [("buf1", vmem(s + (ENTRY_ROWS, 128), BF16)), ("buf2", vmem(s + (FEED_ROWS, 128), BF16))]
        for name, rows in (("pair0", PAIR_ROWS), ("pair1", PAIR_ROWS), ("feed", FEED_ROWS)):
            for step, g in enumerate((2, 1, 0)):
                scratch.append((f"{name}_got{step}", vmem((s[g] - 1,) + s[:g] + (rows, 128), BF16)))
                if g < 2:
                    scratch.append((f"{name}_part{step}", vmem(s[: g + 1] + (rows, 128), BF16)))
        for name, rows in (("feed_vec", FEED_VECS), ("lead_vec", LEAD_VECS)):
            scratch += [(name, vmem((len(s) + 1, rows, 128), F32)), (f"{name}_got", vmem((len(s), 3, rows, 128), F32))]
        scratch += [(f"sem{i}", pltpu.SemaphoreType.DMA((2, 3, 3))) for i in range(1, 8)] + [("load_sem", pltpu.SemaphoreType.DMA((3,)))]
        out_shape = [vmem(shape, dtype) for _, shape, dtype in outs]
        params = dict(vmem_limit_bytes=58 * 1024 * 1024, collective_id=0, has_side_effects=True)
    else:
        ins = ("state_in", "embed_in", "grad_h") + tuple(name for name, _ in weights) + VECTOR_INPUTS
        in_specs = [in_vmem] * len(ins)
        outs += [(name, shape, F32) for name, shape in grads] + [("g_reduce", (FF, D), F32)]
        out_shape = [jax.ShapeDtypeStruct(shape, dtype) for _, shape, dtype in outs]
        scratch += [("grad_in", vmem((T, D), BF16))]
        params = dict(vmem_limit_bytes=63 * 1024 * 1024)
    names = ins + tuple(out[0] for out in outs) + tuple(name for name, _ in scratch)
    return pl.pallas_call(
        functools.partial(mega_kernel, names=names, n=n, tokens=T, comm=comm),
        in_specs=in_specs,
        out_specs=[in_vmem] * len(outs),
        out_shape=out_shape,
        scratch_shapes=[shape for _, shape in scratch],
        compiler_params=pltpu.CompilerParams(**params),
        name="block",
    )


def drain_kernel(*refs):
    count = len(refs) // 2
    sems = refs[-1]
    copies = [pltpu.make_async_copy(refs[i], refs[count + i], sems.at[i]) for i in range(count)]
    for copy in copies:
        copy.start()
    for copy in copies:
        copy.wait()


def drain(*arrays):
    count = len(arrays)
    return pl.pallas_call(
        drain_kernel,
        in_specs=[pl.BlockSpec(memory_space=pltpu.VMEM)] * count,
        out_specs=[pl.BlockSpec(memory_space=pl.ANY)] * count,
        out_shape=[jax.ShapeDtypeStruct(a.shape, a.dtype) for a in arrays],
        scratch_shapes=[pltpu.SemaphoreType.DMA((count,))],
        compiler_params=pltpu.CompilerParams(vmem_limit_bytes=1024 * 1024),
        name="drain",
    )(*arrays)


def on_device(loop_state, embedding, output_grad, entry_weight, exit_weight, lead_gain, lead_shift, expand_weight, reduce_weight, middle_gain, middle_shift, expand_bias, reduce_bias):
    n = lax.axis_size("fsdp")
    tokens = loop_state.shape[0]
    vectors = (lead_gain, lead_shift, middle_gain, middle_shift, reduce_bias, expand_bias)
    weights = (entry_weight, exit_weight, expand_weight, reduce_weight)
    if entry_weight.shape[0] == 8 and len(digit_groups(n)) == 3:
        return tuple(drain(*mega(n, tokens, True)(loop_state, embedding, output_grad, *weights, *vectors)))
    shards = weights + vectors
    packed = jnp.concatenate([a.reshape(-1) for a in shards])
    whole = lax.all_gather(packed, "fsdp", axis=0)
    full, at = [], 0
    for a in shards:
        whole_a = whole[:, at : at + a.size].reshape((n * a.shape[0],) + a.shape[1:])
        full.append(whole_a if a.ndim == 2 else whole_a.reshape(1, -1))
        at += a.size
    final, grad, total, g_entry, g_exit, g_expand, small, g_reduce = mega(n, tokens, False)(loop_state, embedding, output_grad, *full)
    terms = (g_entry, g_exit, small[0], small[1], g_expand, g_reduce, small[2], small[3], small[8:12].reshape(-1), small[5])
    sums = lax.psum_scatter(jnp.concatenate([a.reshape(n, -1) for a in terms], axis=1), "fsdp", scatter_dimension=0, tiled=True)[0]
    outs, at = [], 0
    for a in terms:
        size = a.size // n
        outs.append(sums[at : at + size].reshape((a.shape[0] // n,) + a.shape[1:]))
        at += size
    return (final, grad, total, *outs)


def solution(mesh):
    two, one = P("fsdp", None), P("fsdp")
    in_specs = (two, two, two, two, two, one, one, two, two, one, one, one, one)
    out_specs = (two, two, two, two, two, one, one, two, two, one, one, one, one)
    return jax.shard_map(on_device, mesh=mesh, in_specs=in_specs, out_specs=out_specs, check_vma=False)
```

```python
import functools
import math
from types import SimpleNamespace

import jax
import jax.numpy as jnp
from jax import lax
from jax.experimental import pallas as pl
from jax.experimental.pallas import tpu as pltpu
from jax.sharding import PartitionSpec as P

F32, BF16 = jnp.float32, jnp.bfloat16
LEN = 1024
LOOPS = 2
EPS = 1e-05
D = 256
FF = 1024
HD = 64
BLK = 256
LOG2E = 1.4426950408889634
LN2 = 0.6931471805599453
INV_SQRT_2PI = 1.0 / math.sqrt(2.0 * math.pi)
NEG = -1e30


def dot_nn(a, b):
    return lax.dot_general(a, b, (((1,), (0,)), ((), ())), preferred_element_type=F32)


def dot_nt(a, b):
    return lax.dot_general(a, b, (((1,), (1,)), ((), ())), preferred_element_type=F32)


def dot_tn(a, b):
    return lax.dot_general(a, b, (((0,), (0,)), ((), ())), preferred_element_type=F32)


def norm_parts(x):
    mean = jnp.mean(x, axis=-1, keepdims=True)
    center = x - mean
    var = jnp.mean(center * center, axis=-1, keepdims=True)
    rstd = lax.rsqrt(var + EPS)
    return center * rstd, rstd


def norm_pull(xhat, rstd, gain, dy):
    dn = dy * gain
    m1 = jnp.mean(dn, axis=-1, keepdims=True)
    m2 = jnp.mean(dn * xhat, axis=-1, keepdims=True)
    return rstd * (dn - m1 - xhat * m2)


def gelu_parts(x):
    cdf = 0.5 + 0.5 * lax.erf(x * math.sqrt(0.5))
    return cdf, jnp.exp2((-0.5 * LOG2E) * (x * x))


def lane_iota(rows):
    return lax.broadcasted_iota(jnp.int32, (rows, 128), 1)


def three_parts(x):
    hi = x.astype(BF16).astype(F32)
    r = x - hi
    mid = r.astype(BF16).astype(F32)
    return hi, mid, r - mid


def spread_parts(x, lane, spare):
    hi, mid, lo = three_parts(x)
    return jnp.where(lane == spare, hi, jnp.where(lane == spare + 1, mid, jnp.where(lane == spare + 2, lo, 0.0)))


def head_pairs(seqs):
    return [(pair, s) for pair in range(2) for s in range(seqs)]


def pair_slices(pair, s):
    seq = slice(s * LEN, (s + 1) * LEN)
    return seq, [slice(part * D + pair * 128, part * D + pair * 128 + 128) for part in range(3)]


def attn_forward(qkv, p, att, lx, vt, seqs, hook=None):
    nblk = LEN // BLK
    for b in range(2):
        vt[b, 0, HD:] = jnp.ones((HD, LEN), BF16)
        vt[b, 1, :HD] = jnp.ones((HD, LEN), BF16)
    low = lane_iota(BLK) < HD
    keep = lax.broadcasted_iota(jnp.int32, (BLK, BLK), 0) <= lax.broadcasted_iota(jnp.int32, (BLK, BLK), 1)
    row = lax.broadcasted_iota(jnp.int32, (8, BLK), 0)
    works = head_pairs(seqs)

    def scores(w, j, h):
        seq, (cq, ck, _) = pair_slices(*works[w])
        r0 = seq.start
        q = qkv[p, r0 + j * BLK:r0 + (j + 1) * BLK, cq]
        zero = jnp.zeros_like(q)
        q = jnp.where(low, q, zero) if h == 0 else jnp.where(low, zero, q)
        return dot_nt(qkv[p, r0:r0 + (j + 1) * BLK, ck], q)

    units = [(w, j, h) for w in range(len(works)) for j in range(nblk) for h in range(2)]
    ready = []
    outs, pieces = [], []
    for u, (w, j, h) in enumerate(units):
        seq, (cq, _, cv) = pair_slices(*works[w])
        if j == 0 and h == 0:
            if hook is not None:
                hook(w)
            v = qkv[p, seq, cv].T
            vt[w % 2, 0, :HD] = v[:HD]
            vt[w % 2, 1, HD:] = v[HD:]
        while len(ready) < 3 and u + len(ready) < len(units):
            ready.append(scores(*units[u + len(ready)]))
        st = ready.pop(0)
        diag = jnp.where(keep, st[j * BLK:], NEG)
        st = jnp.concatenate([st[: j * BLK], diag], axis=0) if j else diag
        top = jnp.max(st, axis=0, keepdims=True)
        pr = jnp.exp2(st - top).astype(BF16)
        ox = dot_nn(vt[w % 2, h, :, : (j + 1) * BLK], pr)
        mine, den = (ox[:HD], ox[HD:]) if h == 0 else (ox[HD:], ox[:HD])
        outs.append(mine * (1.0 / den))
        hi, mid, lo = three_parts(-(top + jnp.log(den[:8]) * LOG2E))
        pieces.append(jnp.where(row == 0, hi, jnp.where(row == 1, mid, jnp.where(row == 2, lo, 0.0))))
        if h == 1:
            rows = slice(seq.start + j * BLK, seq.start + (j + 1) * BLK)
            att[p, rows, cq] = jnp.concatenate(outs, axis=0).T.astype(BF16)
            blank = jnp.zeros((HD - 8, BLK), F32)
            lx[p, rows, cq] = jnp.concatenate([pieces[1], blank, pieces[0], blank], axis=0).T.astype(BF16)
            outs, pieces = [], []


def attn_backward(qkv, p, att, lx, datt, vx, kx, qx, dox, dkt, dvt, dq, seqs, hook):
    nblk = LEN // BLK
    low = lane_iota(LEN) < HD
    lane = lane_iota(LEN)
    keep = lax.broadcasted_iota(jnp.int32, (BLK, BLK), 1) <= lax.broadcasted_iota(jnp.int32, (BLK, BLK), 0)
    one = jnp.ones((LEN, 128), BF16)

    def work(pair, s):
        hook(pair, s)
        seq = pl.ds(pl.multiple_of(s * LEN, LEN), LEN)
        cq, ck, cv = (pl.ds(pl.multiple_of(part * D + pair * 128, 128), 128) for part in range(3))
        v = qkv[p, seq, cv]
        vx[0] = jnp.where(low, v, one)
        vx[1] = jnp.where(low, one, v)
        k = qkv[p, seq, ck]
        kx[0] = jnp.where(low, k, one)
        kx[1] = jnp.where(low, one, k)
        q = qkv[p, seq, cq]
        ls = lx[p, seq, cq]
        qx[0] = jnp.where(low, q, ls)
        qx[1] = jnp.where(low, ls, q)
        do = datt[seq, cq]
        dof = do.astype(F32)
        prod = dof * att[p, seq, cq].astype(F32)
        in0 = jnp.sum(jnp.where(low, prod, 0.0), axis=-1, keepdims=True)
        in1 = jnp.sum(jnp.where(low, 0.0, prod), axis=-1, keepdims=True)
        dox[0] = jnp.where(low, dof, spread_parts(jnp.broadcast_to(-in0, (LEN, 128)), lane, HD)).astype(BF16)
        dox[1] = jnp.where(low, spread_parts(jnp.broadcast_to(-in1, (LEN, 128)), lane, 0), dof).astype(BF16)
        qt = q.T
        dot = do.T

        def products(h, i):
            a = i * BLK
            return dot_nt(qx[h, a:], kx[h, a:a + BLK]), dot_nt(dox[h, a:], vx[h, a:a + BLK])

        units = [(h, i) for h in range(2) for i in range(nblk)]
        ready = products(*units[0])
        for u, (h, i) in enumerate(units):
            later = products(*units[u + 1]) if u + 1 < len(units) else None
            sc, dp = ready
            a = i * BLK
            pr = jnp.exp2(sc)
            diag = jnp.where(keep, pr[:BLK], 0.0)
            pr = jnp.concatenate([diag, pr[BLK:]], axis=0) if i < nblk - 1 else diag
            ds = (pr * dp).astype(BF16)
            prb = pr.astype(BF16)
            mine = slice(h * HD, h * HD + HD)
            dvt[mine, a:a + BLK] = dot_nn(dot[:, a:], prb)[mine]
            dkt[mine, a:a + BLK] = dot_nn(qt[:, a:], ds)[mine]
            part = dot_nn(ds, kx[h, a:a + BLK])
            if i == 0:
                dq[h] = part
            else:
                dq[h, a:] += part
            ready = later
        qkv[p, seq, cq] = (jnp.where(low, dq[0], dq[1]) * 0.125).astype(BF16)
        qkv[p, seq, ck] = (dkt[...].T * LN2).astype(BF16)
        qkv[p, seq, cv] = dvt[...].T.astype(BF16)

    def step(w, carry):
        work(w // seqs, w % seqs)
        return carry

    lax.fori_loop(0, 2 * seqs, step, 0)


def digit_groups(n):
    groups = [(1, 2)]
    stride = 2
    while stride < n:
        size = min(4, n // stride)
        groups.append((stride, size))
        stride *= size
    return groups[::-1]


class Links:
    def __init__(self, n):
        self.groups = digit_groups(n)
        self.me = lax.axis_index("fsdp")
        self.digits = [(self.me // stride) % size for stride, size in self.groups]
        self.sizes = tuple(size for _, size in self.groups)

    def digit(self, g, t):
        return (self.digits[g] + t) % self.sizes[g]

    def peer(self, g, t):
        return self.me + (self.digit(g, t) - self.digits[g]) * self.groups[g][0]

    def barrier(self):
        sem = pltpu.get_barrier_semaphore()
        count = 0
        for g, size in enumerate(self.sizes):
            for t in range(1, size):
                pl.semaphore_signal(sem, inc=1, device_id=(self.peer(g, t),), device_id_type=pl.DeviceIdType.MESH)
                count += 1
        return lambda: pl.semaphore_wait(sem, count)

    def copy(self, src, dst, sems, g, t):
        return pltpu.make_async_remote_copy(
            src_ref=src,
            dst_ref=dst,
            send_sem=sems.at[0, g, t - 1],
            recv_sem=sems.at[1, g, t - 1],
            device_id=(self.peer(g, t),),
            device_id_type=pl.DeviceIdType.MESH,
        )

    def held(self, buf, g, t=0):
        tail = [self.digit(g, t)] + self.digits[g + 1:]
        return buf.at[(slice(None),) * g + tuple(tail)]

    def gather_start(self, buf, sems, g):
        for t in range(1, self.sizes[g]):
            self.copy(self.held(buf, g), self.held(buf, g), sems, g, t).start()

    def gather_wait(self, buf, sems, g):
        for t in range(1, self.sizes[g]):
            self.copy(self.held(buf, g), self.held(buf, g, -t), sems, g, t).wait_recv()
        for t in range(1, self.sizes[g]):
            self.copy(self.held(buf, g), self.held(buf, g), sems, g, t).wait_send()

    def reduce_start(self, part, got, sems, g):
        for t in range(1, self.sizes[g]):
            src = part.at[(slice(None),) * g + (self.digit(g, t),)]
            self.copy(src, got.at[t - 1], sems, g, t).start()

    def reduce_wait(self, part, got, sems, g):
        for t in range(1, self.sizes[g]):
            src = part.at[(slice(None),) * g + (self.digit(g, t),)]
            self.copy(src, got.at[t - 1], sems, g, t).wait()
        total = part[(slice(None),) * g + (self.digits[g],)].astype(F32)
        for t in range(1, self.sizes[g]):
            total = total + got[t - 1].astype(F32)
        return total

    def sum_start(self, part, got, sems, g):
        for t in range(1, self.sizes[g]):
            self.copy(part.at[g], got.at[g, t - 1], sems, g, t).start()

    def sum_wait(self, part, got, sems, g):
        for t in range(1, self.sizes[g]):
            self.copy(part.at[g], got.at[g, t - 1], sems, g, t).wait()
        total = part[g]
        for t in range(1, self.sizes[g]):
            total = total + got[g, t - 1]
        part[g + 1] = total


class Reduction:
    def __init__(self, links, first, rest, sems):
        self.links, self.parts, self.gots, self.sems = links, [first] + rest[1::2], rest[0::2], sems

    def start(self, step):
        self.links.reduce_start(self.parts[step], self.gots[step], self.sems, len(self.links.sizes) - 1 - step)

    def take(self, step):
        return self.links.reduce_wait(self.parts[step], self.gots[step], self.sems, len(self.links.sizes) - 1 - step)

    def turn(self, step):
        total = self.take(step)
        self.parts[step + 1][...] = total.astype(BF16)
        self.start(step + 1)


def pair_rows(x, t):
    return jnp.concatenate([x[:, 256 * t : 256 * t + 128], x[:, 256 * t + 128 : 256 * t + 256]], axis=0)


ENTRY_ROWS = 64
FEED_ROWS = 144
PAIR_ROWS = 32
FEED_VECS = 16
LEAD_VECS = 8
CHUNK = 256


ROWS = 1024


def mega_kernel(*refs, names, n, tokens, comm):
    o = SimpleNamespace(**dict(zip(names, refs)))
    seqs = tokens // LEN
    chunks = [slice(c, c + CHUNK) for c in range(0, FF, CHUNK)]

    def pack_parameters():
        d = tuple(links.digits)
        x = o.entry_s[...].astype(F32)
        for t in range(3):
            o.buf1[d + (pl.ds(16 * t, 16),)] = pair_rows(x, t).astype(BF16)
        o.vec[...] = jnp.zeros_like(o.vec)
        for i, r in enumerate((o.lead_g, o.lead_s, o.mid_g, o.mid_s, o.red_b)):
            o.vec[i:i + 1, 0:8] = r[...].astype(F32).reshape(1, 8)
        o.vec[8:9, 0:32] = o.exp_b[...].astype(F32).reshape(1, 32)
        low = pltpu.roll(o.vec[0:8, :], (links.me * 8) % 128, 1)
        high = pltpu.roll(jnp.broadcast_to(o.vec[8:9, :], (8, 128)), (links.me * 32) % 128, 1)
        row = lax.broadcasted_iota(jnp.int32, (8, 128), 0)
        high = jnp.where(row == links.me // 4, high, 0.0)
        o.buf1[d + (pl.ds(48, 16),)] = jnp.concatenate([low, high], axis=0).astype(BF16)

    def pack_more_parameters():
        d = tuple(links.digits)
        o.buf2[d + (pl.ds(0, 16),)] = pair_rows(o.exit_s[...].astype(F32), 0).astype(BF16)
        x = o.expand_s[...].astype(F32)
        for t in range(4):
            o.buf2[d + (pl.ds(16 + 16 * t, 16),)] = pair_rows(x, t).astype(BF16)
        for c in range(2):
            o.buf2[d + (pl.ds(80 + 32 * c, 32),)] = o.reduce_s[:, 128 * c:128 * c + 128]

    def unpack(buf, at, count, dst):
        for t in range(count // 2):
            x = buf[:, :, :, at + 16 * t:at + 16 * t + 16, :].astype(F32).reshape(n, 16, 128)
            dst[:, 256 * t:256 * t + 128] = x[:, :8].reshape(8 * n, 128).astype(BF16)
            dst[:, 256 * t + 128:256 * t + 256] = x[:, 8:].reshape(8 * n, 128).astype(BF16)

    def unpack_first():
        unpack(o.buf1, 0, 6, o.entry_w)
        v = o.buf1[:, :, :, 48:64, :].astype(F32).reshape(n, 16, 128)
        first = jnp.sum(v[: n // 2], axis=0)
        second = jnp.sum(v[n // 2:], axis=0)
        o.vecs[0:5, 0:128] = first[0:5]
        o.vecs[0:5, 128:256] = second[0:5]
        both = (first + second)[8:16]
        for c in range(8):
            o.eb[0:1, 128 * c:128 * c + 128] = both[c:c + 1]

    def unpack_second():
        unpack(o.buf2, 0, 2, o.exit_w)
        unpack(o.buf2, 16, 8, o.expand_w)
        for c in range(2):
            x = o.buf2[:, :, :, 80 + 32 * c:112 + 32 * c, :]
            o.reduce_w[:, 128 * c:128 * c + 128] = x.reshape(32 * n, 128)

    def turn_weights():
        o.entry_t[...] = o.entry_w[...].T
        o.exit_t[...] = o.exit_w[...].T
        o.expand_t[...] = o.expand_w[...].T
        o.reduce_t[...] = o.reduce_w[...].T

    def chunk_rows(grad, c):
        return grad[:, 128 * c:128 * c + 128].reshape(n, 8, 128)

    def store_rows(part, at, top, bottom):
        x = jnp.concatenate([top, bottom], axis=1).astype(BF16)
        part[:, :, :, at:at + 16, :] = x.reshape(links.sizes + (16, 128))

    def halves(row):
        return [row[:, :128], row[:, 128:]]

    def vector_rows(part, rows, count):
        for i, r in enumerate(rows):
            part[0, i:i + 1, :] = r
        if len(rows) < count:
            part[0, len(rows):count, :] = jnp.zeros((count - len(rows), 128), F32)

    def own_eight(total, at):
        both = jnp.where(links.me >= n // 2, total[at + 1:at + 2], total[at:at + 1])
        both = pltpu.roll(jnp.broadcast_to(both, (8, 128)), (128 - (links.me * 8) % 128) % 128, 1)
        return both[0:1, 0:8].reshape(8)

    def feed_pack():
        store_rows(o.buf2, 0, chunk_rows(o.g_exit, 0), chunk_rows(o.g_exit, 1))
        for t in range(4):
            store_rows(o.buf2, 16 + 16 * t, chunk_rows(o.g_expand, 2 * t), chunk_rows(o.g_expand, 2 * t + 1))
        for c in range(2):
            x = o.g_reduce_t[128 * c:128 * c + 128, :].astype(BF16).T
            o.buf2[:, :, :, 80 + 32 * c:112 + 32 * c, :] = x.reshape(links.sizes + (32, 128))
        rows = halves(o.g_small[2:3, :]) + halves(o.g_small[3:4, :]) + halves(o.g_small[5:6, :])
        rows += [o.g_exp_b[:, 128 * c:128 * c + 128] for c in range(8)]
        vector_rows(o.feed_vec, rows, FEED_VECS)

    def feed_end(total):
        for c in range(2):
            o.exit_o[:, 128 * c:128 * c + 128] = total[8 * c:8 * c + 8]
            o.reduce_o[:, 128 * c:128 * c + 128] = total[80 + 32 * c:112 + 32 * c]
        for c in range(8):
            o.expand_o[:, 128 * c:128 * c + 128] = total[16 + 8 * c:24 + 8 * c]

    def feed_vec_end():
        total = o.feed_vec[len(links.sizes)]
        o.mid_g_o[...] = own_eight(total, 0)
        o.mid_s_o[...] = own_eight(total, 2)
        o.red_b_o[...] = own_eight(total, 4)
        row = lax.broadcasted_iota(jnp.int32, (8, 128), 0)
        x = jnp.sum(jnp.where(row == links.me // 4, total[6:14], 0.0), axis=0, keepdims=True)
        x = pltpu.roll(jnp.broadcast_to(x, (8, 128)), (128 - (links.me * 32) % 128) % 128, 1)
        o.exp_b_o[...] = x[0:1, 0:32].reshape(32)

    def pair_grad(pair, n1):
        cols = [slice(part * D + pair * 128, part * D + pair * 128 + 128) for part in range(3)]
        grad = dot_tn(n1, jnp.concatenate([o.qkv[0, :, c] for c in cols], axis=1))
        q, k, v = ((o.g_entry[:, c] + grad[:, 128 * i:128 * i + 128]).reshape(n, 8, 128) for i, c in enumerate(cols))
        store_rows(o.buf1, PAIR_ROWS * pair, q, k)
        store_rows(o.buf1, PAIR_ROWS * pair + 16, v, jnp.zeros_like(v))

    def pair_end(pair, total):
        for part in range(3):
            at = part * D + pair * 128
            o.entry_o[:, at:at + 128] = total[8 * part:8 * part + 8]

    def lead_vec_end():
        total = o.lead_vec[len(links.sizes)]
        o.lead_g_o[...] = own_eight(total, 0)
        o.lead_s_o[...] = own_eight(total, 2)

    every = slice(0, tokens)

    def first_mixed(rows=every):
        return o.state_in[rows].astype(F32) + o.embed_in[rows].astype(F32)

    def lead_normed(xhat):
        return (xhat * o.vecs[0:1, :] + o.vecs[1:2, :]).astype(BF16)

    def middle_normed(xhat):
        return (xhat * o.vecs[2:3, :] + o.vecs[3:4, :]).astype(BF16)

    def enter(p):
        x = o.grad[...] + o.embed_in[...].astype(F32)
        o.total[...] = x
        n1 = lead_normed(norm_parts(x)[0])
        for i in range(3):
            y = dot_nn(n1, o.entry_w[:, i * D:(i + 1) * D])
            o.qkv[p, :, i * D:(i + 1) * D] = (y * (LOG2E * 0.125) if i == 0 else y).astype(BF16)

    def forward_chunk(n2, c):
        hid = dot_nn(n2, o.expand_w[:, c]) + o.eb[:, c]
        cdf, e = gelu_parts(hid)
        return (hid * cdf).astype(BF16), cdf + hid * (e * INV_SQRT_2PI)

    def backward_chunk(d_out, n2, act, gp, c):
        reduce_g = dot_tn(d_out, act)
        dh = dot_nn(d_out, o.reduce_t[:, c]) * gp
        bias_g = jnp.sum(dh, axis=0, keepdims=True)
        dh = dh.astype(BF16)
        expand_g = dot_tn(n2, dh)
        o.g_reduce_t[:, c] += reduce_g
        o.g_exp_b[:, c] += bias_g
        o.g_expand[:, c] += expand_g
        return dot_nn(dh, o.expand_t[c, :])

    def clear():
        for r in (o.g_entry, o.g_exit, o.g_expand, o.g_reduce_t, o.g_small, o.g_exp_b):
            r[...] = jnp.zeros_like(r)

    def add_small(at, row):
        o.g_small[at:at + 1, :] += row

    def feed_finish(p, rows, g, dn, xhat, rstd):
        add_small(5, jnp.sum(g, axis=0, keepdims=True))
        add_small(2, jnp.sum(dn * xhat, axis=0, keepdims=True))
        add_small(3, jnp.sum(dn, axis=0, keepdims=True))
        dm = g + norm_pull(xhat, rstd, o.vecs[2:3, :], dn)
        o.grad[rows] = dm
        db = dm.astype(BF16)
        o.g_exit[...] += dot_tn(o.att[p, rows], db)
        o.grad_in[rows] = dot_nn(db, o.exit_t[...]).astype(BF16)

    def feed_first(rows):
        mid = o.total[rows] + dot_nn(o.att[0, rows], o.exit_w[...])
        o.middle[rows] = mid
        n2 = middle_normed(norm_parts(mid)[0])
        res = mid + o.vecs[4:5, :]
        for c in chunks:
            act, gp = forward_chunk(n2, c)
            o.active[rows, c] = act
            o.gelup[rows, c] = gp.astype(BF16)
            res = res + dot_nn(act, o.reduce_w[c, :])
        o.grad[rows] = res

    def feed_last(rows):
        mid = o.total[rows] + dot_nn(o.att[1, rows], o.exit_w[...])
        o.grad[rows] = mid
        n2 = middle_normed(norm_parts(mid)[0])
        res = mid + o.vecs[4:5, :]
        d_out = o.grad_in[rows]
        dn = None
        for c in chunks:
            act, gp = forward_chunk(n2, c)
            res = res + dot_nn(act, o.reduce_w[c, :])
            part = backward_chunk(d_out, n2, act, gp, c)
            dn = part if dn is None else dn + part
        o.final[rows] = res.astype(BF16)
        xhat, rstd = norm_parts(o.grad[rows])
        feed_finish(1, rows, o.grad_in[rows].astype(F32), dn, xhat, rstd)

    def feed_back(rows):
        n2 = middle_normed(norm_parts(o.middle[rows])[0])
        d_out = o.grad[rows].astype(BF16)
        dn = None
        for c in chunks:
            part = backward_chunk(d_out, n2, o.active[rows, c], o.gelup[rows, c].astype(F32), c)
            dn = part if dn is None else dn + part
        xhat, rstd = norm_parts(o.middle[rows])
        feed_finish(0, rows, o.grad[rows], dn, xhat, rstd)

    def by_rows(phase):
        def part(i, carry):
            phase(pl.ds(pl.multiple_of(i * ROWS, ROWS), ROWS))
            return carry
        lax.fori_loop(0, tokens // ROWS, part, 0)

    def add_entry(p, x):
        o.g_entry[...] += dot_tn(lead_normed(norm_parts(x)[0]), o.qkv[p])

    def leave_last(rows):
        x = o.total[rows]
        xhat, rstd = norm_parts(x)
        dqkv = o.qkv[LOOPS - 1, rows]
        o.g_entry[...] += dot_tn(lead_normed(xhat), dqkv)
        dn = dot_nn(dqkv, o.entry_t[...])
        add_small(0, jnp.sum(dn * xhat, axis=0, keepdims=True))
        add_small(1, jnp.sum(dn, axis=0, keepdims=True))
        g = o.grad[rows] + norm_pull(xhat, rstd, o.vecs[0:1, :], dn)
        o.grad[rows] = g
        o.total[rows] = g

    def lead_sums(p, x):
        dn = dot_nn(o.qkv[p], o.entry_t[...])
        add_small(0, jnp.sum(dn * norm_parts(x)[0], axis=0, keepdims=True))
        add_small(1, jnp.sum(dn, axis=0, keepdims=True))
        return dn

    def leave(dn, x, before):
        xhat, rstd = norm_parts(x)
        g = o.grad[...] + norm_pull(xhat, rstd, o.vecs[0:1, :], dn)
        o.grad[...] = g
        o.total[...] = g if before is None else before + g

    def forward(p, hook=None):
        pl.run_scoped(lambda vt: attn_forward(o.qkv, p, o.att, o.lx, vt, seqs, hook), pltpu.VMEM((2, 2, 128, LEN), BF16))

    def backward(p, hook):
        head = [pltpu.VMEM((2, LEN, 128), BF16)] * 4 + [pltpu.VMEM((128, LEN), F32)] * 2 + [pltpu.VMEM((2, LEN, 128), F32)]
        pl.run_scoped(lambda *bufs: attn_backward(o.qkv, p, o.att, o.lx, o.grad_in, *bufs, seqs, hook), *head)

    def forward_passes(hook, ready):
        def one(p, carry):
            enter(p)
            forward(p, lambda w: hook(p, w))

            @pl.when(p == 0)
            def _():
                ready()
                by_rows(feed_first)

            return carry

        lax.fori_loop(0, LOOPS, one, 0)
        by_rows(feed_last)

    def backward_passes(hook, ready):
        def one(i, carry):
            p = LOOPS - 1 - i
            backward(p, lambda pair, s: hook(p, pair, s))

            @pl.when(p == LOOPS - 1)
            def _():
                by_rows(leave_last)
                by_rows(feed_back)
                ready()

            return carry

        lax.fori_loop(0, LOOPS, one, 0)

    if not comm:
        for i, r in enumerate((o.lead_g, o.lead_s, o.mid_g, o.mid_s, o.red_b)):
            o.vecs[i:i + 1, :] = r[...].astype(F32)
        o.eb[...] = o.exp_b[...].astype(F32)
        o.grad_in[...] = o.grad_h[...]
        o.grad[...] = o.state_in[...].astype(F32)
        turn_weights()
        clear()
        forward_passes(lambda p, w: None, lambda: None)
        backward_passes(lambda p, pair, s: None, lambda: None)
        add_entry(0, first_mixed())
        leave(lead_sums(0, first_mixed()), first_mixed(), o.total[...])
        o.g_reduce[...] = o.g_reduce_t[...].T
        for i in range(4):
            o.g_small[8 + i:9 + i, :] = o.g_exp_b[:, i * D:(i + 1) * D]
        return

    links = Links(n)
    last = len(links.sizes) - 1
    arrived = links.barrier()
    loads = [
        pltpu.make_async_copy(src, dst, o.load_sem.at[i])
        for i, (src, dst) in enumerate(((o.state_h, o.state_in), (o.embed_h, o.embed_in), (o.grad_h, o.grad_in)))
    ]
    for load in loads:
        load.start()
    pack_parameters()
    arrived()
    links.gather_start(o.buf1, o.sem1, 0)
    pack_more_parameters()
    clear()
    links.gather_wait(o.buf1, o.sem1, 0)
    links.gather_start(o.buf1, o.sem1, 1)
    links.gather_start(o.buf2, o.sem2, 0)
    for load in loads:
        load.wait()
    o.grad[...] = o.state_in[...].astype(F32)
    links.gather_wait(o.buf1, o.sem1, 1)
    links.gather_start(o.buf1, o.sem1, 2)
    links.gather_wait(o.buf2, o.sem2, 0)
    links.gather_start(o.buf2, o.sem2, 1)
    links.gather_wait(o.buf1, o.sem1, 2)
    unpack_first()

    def gather_more(p, w):
        if w == seqs:
            @pl.when(p == 0)
            def _():
                links.gather_wait(o.buf2, o.sem2, 1)
                links.gather_start(o.buf2, o.sem2, 2)

    def gather_end():
        links.gather_wait(o.buf2, o.sem2, 2)
        unpack_second()
        turn_weights()

    forward_passes(gather_more, gather_end)
    feed = Reduction(links, o.buf2, [o.feed_got0, o.feed_part1, o.feed_got1, o.feed_part2, o.feed_got2], o.sem3)
    first = Reduction(links, o.buf1.at[:, :, :, pl.ds(0, PAIR_ROWS), :], [o.pair0_got0, o.pair0_part1, o.pair0_got1, o.pair0_part2, o.pair0_got2], o.sem4)
    second = Reduction(links, o.buf1.at[:, :, :, pl.ds(PAIR_ROWS, PAIR_ROWS), :], [o.pair1_got0, o.pair1_part1, o.pair1_got1, o.pair1_part2, o.pair1_got2], o.sem5)
    feed_vec = (o.feed_vec, o.feed_vec_got, o.sem6)
    lead_vec = (o.lead_vec, o.lead_vec_got, o.sem7)

    def reduce_begin():
        feed_pack()
        feed.start(0)
        links.sum_start(*feed_vec, 0)

    def reduce_more(p, pair, s):
        @pl.when((p == 0) & (pair == 0) & (s == 1))
        def _():
            feed.turn(0)
            links.sum_wait(*feed_vec, 0)
            links.sum_start(*feed_vec, 1)

        @pl.when((p == 0) & (pair == 1) & (s == 0))
        def _():
            o.att[1] = lead_normed(norm_parts(first_mixed())[0])
            pair_grad(0, o.att[1])
            first.start(0)

        @pl.when((p == 0) & (pair == 1) & (s == seqs - 1))
        def _():
            feed.turn(1)
            first.turn(0)
            links.sum_wait(*feed_vec, 1)
            links.sum_start(*feed_vec, 2)

    backward_passes(reduce_more, reduce_begin)
    pair_grad(1, o.att[1])
    second.start(0)
    dn = lead_sums(0, first_mixed())
    vector_rows(o.lead_vec, halves(o.g_small[0:1, :]) + halves(o.g_small[1:2, :]), LEAD_VECS)
    links.sum_start(*lead_vec, 0)
    second.turn(0)
    first.turn(1)
    leave(dn, first_mixed(), o.total[...])
    feed_end(feed.take(2))
    links.sum_wait(*feed_vec, 2)
    feed_vec_end()
    links.sum_wait(*lead_vec, 0)
    links.sum_start(*lead_vec, 1)
    second.turn(1)
    pair_end(0, first.take(2))
    links.sum_wait(*lead_vec, 1)
    links.sum_start(*lead_vec, 2)
    pair_end(1, second.take(2))
    links.sum_wait(*lead_vec, 2)
    lead_vec_end()


VECTOR_INPUTS = ("lead_g", "lead_s", "mid_g", "mid_s", "red_b", "exp_b")


def mega(n, tokens, comm):
    T = tokens
    vmem = pltpu.VMEM
    outs = [("final", (T, D), BF16), ("grad", (T, D), F32), ("total", (T, D), F32)]
    scratch = [
        ("qkv", vmem((2, T, 3 * D), BF16)), ("att", vmem((2, T, D), BF16)), ("lx", vmem((2, T, D), BF16)),
        ("middle", vmem((T, D), F32)), ("active", vmem((T, FF), BF16)), ("gelup", vmem((T, FF), BF16)),
        ("entry_t", vmem((3 * D, D), BF16)), ("exit_t", vmem((D, D), BF16)), ("expand_t", vmem((FF, D), BF16)), ("reduce_t", vmem((D, FF), BF16)),
        ("vecs", vmem((8, D), F32)), ("eb", vmem((1, FF), F32)),
        ("g_reduce_t", vmem((D, FF), F32)), ("g_exp_b", vmem((1, FF), F32)),
    ]
    grads = [("g_entry", (D, 3 * D)), ("g_exit", (D, D)), ("g_expand", (D, FF)), ("g_small", (16, D))]
    weights = [("entry_w", (D, 3 * D)), ("exit_w", (D, D)), ("expand_w", (D, FF)), ("reduce_w", (FF, D))]
    in_vmem, in_hbm = pl.BlockSpec(memory_space=pltpu.VMEM), pl.BlockSpec(memory_space=pl.ANY)
    if comm:
        ins = ("state_h", "embed_h", "grad_h", "entry_s", "exit_s", "expand_s", "reduce_s") + VECTOR_INPUTS
        in_specs = [in_hbm] * 3 + [in_vmem] * 10
        r, rr = D // n, FF // n
        outs += [
            ("entry_o", (r, 3 * D), F32), ("exit_o", (r, D), F32), ("lead_g_o", (r,), F32), ("lead_s_o", (r,), F32),
            ("expand_o", (r, FF), F32), ("reduce_o", (rr, D), F32), ("mid_g_o", (r,), F32), ("mid_s_o", (r,), F32),
            ("exp_b_o", (rr,), F32), ("red_b_o", (r,), F32),
        ]
        scratch += [(name, vmem((T, D), BF16)) for name in ("state_in", "embed_in", "grad_in")]
        scratch += [(name, vmem(shape, F32)) for name, shape in grads] + [(name, vmem(shape, BF16)) for name, shape in weights]
        s = tuple(size for _, size in digit_groups(n))
        scratch += [("vec", vmem((16, 128), F32))]
        scratch += [("buf1", vmem(s + (ENTRY_ROWS, 128), BF16)), ("buf2", vmem(s + (FEED_ROWS, 128), BF16))]
        for name, rows in (("pair0", PAIR_ROWS), ("pair1", PAIR_ROWS), ("feed", FEED_ROWS)):
            for step, g in enumerate((2, 1, 0)):
                scratch.append((f"{name}_got{step}", vmem((s[g] - 1,) + s[:g] + (rows, 128), BF16)))
                if g < 2:
                    scratch.append((f"{name}_part{step}", vmem(s[: g + 1] + (rows, 128), BF16)))
        for name, rows in (("feed_vec", FEED_VECS), ("lead_vec", LEAD_VECS)):
            scratch += [(name, vmem((len(s) + 1, rows, 128), F32)), (f"{name}_got", vmem((len(s), 3, rows, 128), F32))]
        scratch += [(f"sem{i}", pltpu.SemaphoreType.DMA((2, 3, 3))) for i in range(1, 8)] + [("load_sem", pltpu.SemaphoreType.DMA((3,)))]
        out_shape = [vmem(shape, dtype) for _, shape, dtype in outs]
        params = dict(vmem_limit_bytes=58 * 1024 * 1024, collective_id=0, has_side_effects=True)
    else:
        ins = ("state_in", "embed_in", "grad_h") + tuple(name for name, _ in weights) + VECTOR_INPUTS
        in_specs = [in_vmem] * len(ins)
        outs += [(name, shape, F32) for name, shape in grads] + [("g_reduce", (FF, D), F32)]
        out_shape = [jax.ShapeDtypeStruct(shape, dtype) for _, shape, dtype in outs]
        scratch += [("grad_in", vmem((T, D), BF16))]
        params = dict(vmem_limit_bytes=63 * 1024 * 1024)
    names = ins + tuple(out[0] for out in outs) + tuple(name for name, _ in scratch)
    return pl.pallas_call(
        functools.partial(mega_kernel, names=names, n=n, tokens=T, comm=comm),
        in_specs=in_specs,
        out_specs=[in_vmem] * len(outs),
        out_shape=out_shape,
        scratch_shapes=[shape for _, shape in scratch],
        compiler_params=pltpu.CompilerParams(**params),
        name="block",
    )


def drain_kernel(*refs):
    count = len(refs) // 2
    sems = refs[-1]
    copies = [pltpu.make_async_copy(refs[i], refs[count + i], sems.at[i]) for i in range(count)]
    for copy in copies:
        copy.start()
    for copy in copies:
        copy.wait()


def drain(*arrays):
    count = len(arrays)
    return pl.pallas_call(
        drain_kernel,
        in_specs=[pl.BlockSpec(memory_space=pltpu.VMEM)] * count,
        out_specs=[pl.BlockSpec(memory_space=pl.ANY)] * count,
        out_shape=[jax.ShapeDtypeStruct(a.shape, a.dtype) for a in arrays],
        scratch_shapes=[pltpu.SemaphoreType.DMA((count,))],
        compiler_params=pltpu.CompilerParams(vmem_limit_bytes=1024 * 1024),
        name="drain",
    )(*arrays)


def on_device(loop_state, embedding, output_grad, entry_weight, exit_weight, lead_gain, lead_shift, expand_weight, reduce_weight, middle_gain, middle_shift, expand_bias, reduce_bias):
    n = lax.axis_size("fsdp")
    tokens = loop_state.shape[0]
    vectors = (lead_gain, lead_shift, middle_gain, middle_shift, reduce_bias, expand_bias)
    weights = (entry_weight, exit_weight, expand_weight, reduce_weight)
    if entry_weight.shape[0] == 8 and len(digit_groups(n)) == 3:
        return tuple(drain(*mega(n, tokens, True)(loop_state, embedding, output_grad, *weights, *vectors)))
    shards = weights + vectors
    packed = jnp.concatenate([a.reshape(-1) for a in shards])
    whole = lax.all_gather(packed, "fsdp", axis=0)
    full, at = [], 0
    for a in shards:
        whole_a = whole[:, at : at + a.size].reshape((n * a.shape[0],) + a.shape[1:])
        full.append(whole_a if a.ndim == 2 else whole_a.reshape(1, -1))
        at += a.size
    final, grad, total, g_entry, g_exit, g_expand, small, g_reduce = mega(n, tokens, False)(loop_state, embedding, output_grad, *full)
    terms = (g_entry, g_exit, small[0], small[1], g_expand, g_reduce, small[2], small[3], small[8:12].reshape(-1), small[5])
    sums = lax.psum_scatter(jnp.concatenate([a.reshape(n, -1) for a in terms], axis=1), "fsdp", scatter_dimension=0, tiled=True)[0]
    outs, at = [], 0
    for a in terms:
        size = a.size // n
        outs.append(sums[at : at + size].reshape((a.shape[0] // n,) + a.shape[1:]))
        at += size
    return (final, grad, total, *outs)


def solution(mesh):
    two, one = P("fsdp", None), P("fsdp")
    in_specs = (two, two, two, two, two, one, one, two, two, one, one, one, one)
    out_specs = (two, two, two, two, two, one, one, two, two, one, one, one, one)
    return jax.shard_map(on_device, mesh=mesh, in_specs=in_specs, out_specs=out_specs, check_vma=False)
```
